32 devices in a mesh: groups: 2 (over x), tensor: 8 (over z, y), store: 2 (over core).
Axes of the slice: x: 2, y: 2, z: 4, core: 2. Of those that a mesh axis runs over, the one named last changes fastest.
Arguments:
- tokens: bfloat16 [4, 1024, 8192], P(('groups', 'store'), 'tensor'), parts along dimension 0, may hold values from -6 to 6
- query_weight: bfloat16 [8192, 8192], P(None, 'tensor'), may hold values from -0.0625 to 0.0625
- adapter_down_maps: bfloat16 [64, 64, 8192], P(('tensor', 'store')), may hold values from -0.0625 to 0.0625
- adapter_up_maps: bfloat16 [64, 64, 8192], P(('tensor', 'store')), may hold values from -0.75 to 0.75
- adapter_home_slot: int32 [64], replicated, may hold values from 0 to 63, as said below
- adapter_per_block: int32 [2, 8], replicated, may hold values from 0 to 63, as said below
Outputs:
- query: bfloat16 [4, 1024, 8192], P(('groups', 'store'), None, 'tensor'), parts along dimension 0
The draws below stay inside these ranges and needn't reach their ends.
There are 2 independent parts, one for each index of `groups`. The reference program is written for one: setup_inputs(seed, part) draws one part's arguments, and reference() takes and returns one part's arrays. A program takes and returns all parts, laid end to end along the dimension named above; an argument that names none is the same for every part. Nothing has to cross between parts.
Inputs may be any that keep to these rules, and one draw needn't show every extreme that they name: `adapter_home_slot`: A permutation: each adapter has its own slot; slot j lies on the device of index j // 4 along tensor+store. `adapter_per_block`: each request batch names exactly min(8, 16) different adapters, and the different adapters of one batch always lie in slots on different devices.
All inputs are finite; a program needn't handle non-finite values.
Results may differ from the reference program's by a relative error of at most 0.0031.
Values may be sent and summed in bfloat16 or wider, within the bound.
No kernel may reach another device: no remote copies, remote signals or barrier semaphores. Data moves between devices by JAX's collectives and lax.ppermute only.
A program may use at most 128 MiB of HBM per device.

```python
import jax
import jax.numpy as jnp

MODEL_WIDTH = 8192
ADAPTER_RANK = 64
BLOCK = 128
ADAPT_DEV = 4
ADAPTER_COUNT = 64
GROUP_ROWS = 1024
BLOCKS = 8
N_STORE = 2


def shared_layout(key):
    return jax.random.permutation(jax.random.fold_in(key, 11), ADAPTER_COUNT).astype(jnp.int32)


def draw_adapter_home_slot(key, part):
    return shared_layout(key)


def draw_adapter_per_block(key, part):
    adapter_home_slot = shared_layout(key)
    key = jax.random.fold_in(key, 5)
    devices_all = ADAPTER_COUNT // ADAPT_DEV
    first = min(BLOCKS, devices_all)
    holder = jnp.argsort(adapter_home_slot, stable=True).astype(jnp.int32)
    batches = []
    for index in range(N_STORE):
        sub = jax.random.fold_in(key, index)
        homes = jax.random.permutation(jax.random.fold_in(sub, 1), devices_all)[:first].astype(jnp.int32)
        places = jax.random.randint(jax.random.fold_in(sub, 2), (first,), 0, ADAPT_DEV).astype(jnp.int32)
        chosen = holder[homes * ADAPT_DEV + places]
        extra = jax.random.randint(jax.random.fold_in(sub, 3), (BLOCKS - first,), 0, first).astype(jnp.int32)
        picks = jnp.concatenate([jnp.arange(first, dtype=jnp.int32), extra])
        order = jax.random.permutation(jax.random.fold_in(sub, 4), BLOCKS).astype(jnp.int32)
        batches.append(chosen[picks[order]])
    return jnp.stack(batches).astype(jnp.int32)


def level_of(own_key, shape, pieces, low, high):
    def one(axis_at, parts):
        steps = jax.random.uniform(jax.random.fold_in(jax.random.fold_in(own_key, 6), axis_at), (parts,), jnp.float32, low / len(pieces), high / len(pieces))
        return jnp.repeat(jnp.exp(steps), shape[axis_at] // parts).reshape((-1,) + (1,) * (len(shape) - axis_at - 1))

    level = one(*pieces[0])
    for cut in pieces[1:]:
        level = level * one(*cut)
    return level


def normal_values(rng, dims, deviation, most, shards=(), held_as=jnp.bfloat16):
    values = deviation * jax.random.normal(rng, dims, jnp.float32)
    if shards:
        values = values * level_of(rng, dims, shards, -0.22, 0.18)
    return jnp.clip(values, -most, most).astype(held_as)


def setup_inputs(seed: int = 0, part: int = 0) -> dict:
    splits = jax.random.split(jax.random.key(seed), 7)
    own_keys = jax.random.split(jax.random.fold_in(splits[6], part), 7)
    return {
        "tokens": normal_values(own_keys[0], (N_STORE, GROUP_ROWS, MODEL_WIDTH), 1.0, 6.0, ((0, 2), (1, 8))),
        "query_weight": normal_values(splits[1], (MODEL_WIDTH, MODEL_WIDTH), MODEL_WIDTH ** -0.5, 0.0625, ((1, 8),)),
        "adapter_down_maps": normal_values(splits[2], (ADAPTER_COUNT, ADAPTER_RANK, MODEL_WIDTH), MODEL_WIDTH ** -0.5, 0.0625, ((0, 16),)),
        "adapter_up_maps": normal_values(splits[3], (ADAPTER_COUNT, ADAPTER_RANK, MODEL_WIDTH), ADAPTER_RANK ** -0.5, 0.75, ((0, 16),)),
        "adapter_home_slot": draw_adapter_home_slot(jax.random.fold_in(splits[6], 71), part),
        "adapter_per_block": draw_adapter_per_block(jax.random.fold_in(splits[6], 71), part),
    }


def reference(tokens, query_weight, adapter_down_maps, adapter_up_maps, adapter_home_slot, adapter_per_block):
    rows = tokens.reshape(N_STORE * GROUP_ROWS, MODEL_WIDTH)
    base = jnp.dot(rows, query_weight, preferred_element_type=jnp.float32)
    store_slots = adapter_home_slot[adapter_per_block].reshape(N_STORE * BLOCKS)
    down_map_blocks = adapter_down_maps[store_slots].astype(jnp.float32)
    up_map_blocks = adapter_up_maps[store_slots].astype(jnp.float32)
    row_blocks = rows.reshape(N_STORE * BLOCKS, BLOCK, MODEL_WIDTH).astype(jnp.float32)
    shrunk = jnp.einsum("bnd,brd->bnr", row_blocks, down_map_blocks).astype(jnp.bfloat16)
    grown = jnp.einsum("bnr,brf->bnf", shrunk.astype(jnp.float32), up_map_blocks)
    query = base + 0.5 * grown.reshape(N_STORE * GROUP_ROWS, MODEL_WIDTH)
    return query.astype(jnp.bfloat16).reshape(N_STORE, GROUP_ROWS, MODEL_WIDTH)
```

```python
import jax
import jax.numpy as jnp
from jax import lax
from jax.sharding import PartitionSpec as P

BLOCK = 128
EARLY = 16
HALF = 72


def find_slots(adapter_home_slot, adapter_per_block):
    catalog = jnp.arange(adapter_home_slot.shape[0], dtype=jnp.int32)
    return jnp.sum(
        jnp.where(
            adapter_per_block[:, :, None] == catalog[None, None, :],
            adapter_home_slot[None, None, :],
            0,
        ),
        axis=2,
    )


def general_body(
    tokens, query_weight, adapter_down_maps, adapter_up_maps, adapter_home_slot, adapter_per_block
):
    shard_count = lax.axis_size("tensor")
    store_count = lax.axis_size("store")
    devices_all = shard_count * store_count
    my_tensor = lax.axis_index("tensor")
    my_store = lax.axis_index("store")
    myself = lax.axis_index(("tensor", "store"))
    held_adapters, rank_index, feature_width = adapter_down_maps.shape
    feature_index = query_weight.shape[1]
    own_rows = tokens[0]
    group_rows = own_rows.shape[0] * shard_count
    blocks = group_rows // BLOCK
    store_slots = find_slots(adapter_home_slot, adapter_per_block)
    owner = store_slots // held_adapters
    inside = store_slots % held_adapters
    picked = jnp.max(jnp.where(owner == myself, inside, -1), axis=1)
    select = (picked[:, None] == jnp.arange(held_adapters, dtype=jnp.int32)[None, :]).astype(
        jnp.bfloat16
    )
    down_map_parts = adapter_down_maps.reshape(
        held_adapters, rank_index, shard_count, feature_index
    )
    up_map_parts = adapter_up_maps.reshape(held_adapters, rank_index, shard_count, feature_index)
    send_down = jnp.einsum(
        "sl,lrtf->tsrf", select, down_map_parts, preferred_element_type=jnp.float32
    ).astype(jnp.bfloat16)
    send_up = jnp.einsum(
        "sl,lrtf->tsrf", select, up_map_parts, preferred_element_type=jnp.float32
    ).astype(jnp.bfloat16)
    recv_down, recv_up = (
        lax.all_to_all(
            sent.reshape(devices_all, rank_index, feature_index),
            ("tensor", "store"),
            split_axis=0,
            concat_axis=0,
            tiled=True,
        )
        for sent in (send_down, send_up)
    )
    owner_row = lax.dynamic_index_in_dim(owner, my_store, 0, keepdims=False)
    source_pick = (owner_row[:, None] == jnp.arange(devices_all, dtype=jnp.int32)[None, :]).astype(
        jnp.bfloat16
    )
    block_down = jnp.einsum(
        "bj,jrf->brf", source_pick, recv_down, preferred_element_type=jnp.float32
    ).astype(jnp.bfloat16)
    block_up = jnp.einsum(
        "bj,jrf->brf", source_pick, recv_up, preferred_element_type=jnp.float32
    ).astype(jnp.bfloat16)
    piece = lax.all_gather(own_rows, "tensor", axis=0, tiled=True)
    product = jnp.dot(piece, query_weight, preferred_element_type=jnp.float32)
    features = lax.dynamic_slice_in_dim(piece, my_tensor * feature_index, feature_index, 1)
    partial_value = jnp.einsum(
        "bnf,brf->bnr",
        features.reshape(blocks, BLOCK, feature_index),
        block_down,
        preferred_element_type=jnp.float32,
    )
    shrunk = lax.psum(partial_value, "tensor").astype(jnp.bfloat16)
    grown = jnp.einsum(
        "bnr,brf->bnf", shrunk, block_up, preferred_element_type=jnp.float32
    ).reshape(group_rows, feature_index)
    query = (product + 0.5 * grown).astype(jnp.bfloat16)
    return query[None]


def both_ways(pairs):
    return pairs + [(b, a) for a, b in pairs]


NEAR = both_ways([(0, 2), (1, 3), (4, 6), (5, 7)])
MIDDLE = both_ways([(2, 4), (3, 5)])
OUTWARD = [(2, 0), (3, 1), (4, 6), (5, 7)]
INWARD = [(b, a) for a, b in OUTWARD]
ACROSS = both_ways([(0, 1), (2, 3), (4, 5), (6, 7)])
ACROSS_INNER = both_ways([(2, 3), (4, 5)])
ACROSS_ENDS = both_ways([(0, 1), (6, 7)])


def send(value, pairs):
    return lax.ppermute(value, "tensor", pairs)


def swap(value, axis):
    return lax.ppermute(value, axis, [(0, 1), (1, 0)])


def chain_body(
    tokens, query_weight, adapter_down_maps, adapter_up_maps, adapter_home_slot, adapter_per_block
):
    me = lax.axis_index("tensor")
    z, y = me // 2, me % 2
    store = lax.axis_index("store")
    group = lax.axis_index("groups")
    myself = me * 2 + store
    inner = (z == 1) | (z == 2)
    held, rank, width = adapter_down_maps.shape
    columns = query_weight.shape[1]
    part = columns // 2
    rows = tokens[0]

    store_slots = find_slots(adapter_home_slot, adapter_per_block)
    owner = store_slots // held
    inside = store_slots % held
    picked = jnp.max(jnp.where(owner == myself, inside, 0), axis=1)
    owner_row = lax.dynamic_index_in_dim(owner, store, 0, keepdims=False)

    early = rows[:EARLY]
    early_other = send(early, ACROSS)
    pieces = [rows[EARLY:HALF], rows[HALF:], jnp.concatenate([early, early_other])]
    near = [send(p, NEAR) for p in pieces]
    far = [send(p, MIDDLE) for p in pieces]
    far_out = [send(p, OUTWARD) for p in far]
    last = [send(p, MIDDLE) for p in near]
    last_out = [send(p, OUTWARD) for p in last]
    own_y = [send(p, ACROSS) for p in pieces[:2]]
    near_y = [send(p, ACROSS) for p in near[:2]]
    far_y = [send(p, ACROSS_INNER) for p in far[:2]]
    far_out_y = [send(p, ACROSS_ENDS) for p in far_out[:2]]
    last_y = [send(p, ACROSS_INNER) for p in last[:2]]
    last_out_y = [send(p, ACROSS_ENDS) for p in last_out[:2]]

    def mine(p):
        return jnp.concatenate([p[2][:EARLY], p[0], p[1]])

    def other(p, p_y):
        return jnp.concatenate([p[2][EARLY:], p_y[0], p_y[1]])

    def either(p, q):
        return [jnp.where(inner, a, b) for a, b in zip(p, q)]

    z_near = z + 1 - 2 * (z % 2)
    z_far = jnp.where(z < 2, 2, 1)
    z_last = jnp.where(z < 2, 3, 0)

    def pick(maps, index):
        return lax.dynamic_index_in_dim(maps, picked[index], 0, keepdims=False)

    down_own = lax.dynamic_index_in_dim(
        adapter_down_maps, lax.dynamic_index_in_dim(picked, store, 0, False), 0, keepdims=False
    )
    down_lent = lax.dynamic_index_in_dim(
        adapter_down_maps, lax.dynamic_index_in_dim(picked, 1 - store, 0, False), 0, keepdims=False
    )
    down_swapped = swap(down_lent, "store")
    chip_down = jnp.stack([down_own, down_swapped])
    end_down = send(chip_down, INWARD)
    candidates = jnp.concatenate([chip_down, end_down])
    z_end = jnp.where(z < 2, 0, 3)

    def shrink(block, index):
        home = lax.dynamic_index_in_dim(owner_row, index, 0, False)
        core = jnp.where(home % 2 == store, 0, 1)
        is_own = home // 2 == me
        is_end = home // 2 == z_end * 2 + y
        down = lax.dynamic_index_in_dim(
            candidates, jnp.where(is_own, core, 2 + core), 0, keepdims=False
        )
        value = lax.dot_general(
            down, block, (((1,), (1,)), ((), ())), preferred_element_type=jnp.float32
        )
        return jnp.where(inner & (is_own | is_end), value, 0).astype(jnp.bfloat16)

    inner_blocks = [
        (mine(pieces), z * 2 + y),
        (other(pieces, own_y), z * 2 + 1 - y),
        (mine(near), z_near * 2 + y),
        (other(near, near_y), z_near * 2 + 1 - y),
        (mine(far), z_far * 2 + y),
        (other(far, far_y), z_far * 2 + 1 - y),
        (mine(last), z_last * 2 + y),
        (other(last, last_y), z_last * 2 + 1 - y),
    ]
    shrunk = jnp.zeros((8, rank, BLOCK), jnp.bfloat16)
    for block, index in inner_blocks:
        shrunk = lax.dynamic_update_slice(shrunk, shrink(block, index)[None], (index, 0, 0))
    shrunk = shrunk + send(shrunk, ACROSS_INNER)
    shrunk = shrunk + send(shrunk, MIDDLE)
    shrunk = jnp.where(inner, shrunk, send(shrunk, OUTWARD))

    def columns_of(up):
        halves = up.reshape(rank, 8, 2, part)
        half = lax.dynamic_index_in_dim(halves, group, 2, keepdims=False)
        return half.transpose(1, 0, 2)

    up_sent = jnp.stack(
        [columns_of(pick(adapter_up_maps, 0)), columns_of(pick(adapter_up_maps, 1))], axis=1
    )
    up_got = lax.all_to_all(
        up_sent.reshape(16, rank, part), ("tensor", "store"), split_axis=0, concat_axis=0, tiled=True
    )
    up_half = jnp.stack(
        [lax.dynamic_index_in_dim(up_got, owner_row[b], 0, keepdims=False) for b in range(8)]
    )
    up_other = swap(up_half, "groups")
    up = jnp.concatenate(
        [jnp.where(group == 0, up_half, up_other), jnp.where(group == 0, up_other, up_half)], axis=2
    )

    far_any, far_any_y = either(far, far_out), either(far_y, far_out_y)
    last_any, last_any_y = either(last, last_out), either(last_y, last_out_y)
    blocks = inner_blocks[:4] + [
        (mine(far_any), z_far * 2 + y),
        (other(far_any, far_any_y), z_far * 2 + 1 - y),
        (mine(last_any), z_last * 2 + y),
        (other(last_any, last_any_y), z_last * 2 + 1 - y),
    ]
    query = jnp.zeros((8 * BLOCK, columns), jnp.bfloat16)
    for block, index in blocks:
        base = jnp.dot(block, query_weight, preferred_element_type=jnp.float32)
        grown = lax.dot_general(
            lax.dynamic_index_in_dim(shrunk, index, 0, keepdims=False),
            lax.dynamic_index_in_dim(up, index, 0, keepdims=False),
            (((0,), (0,)), ((), ())),
            preferred_element_type=jnp.float32,
        )
        value = (base + 0.5 * grown).astype(jnp.bfloat16)
        query = lax.dynamic_update_slice(query, value, (index * BLOCK, 0))
    return query[None]


def body(tokens, *rest):
    sizes = tuple(lax.axis_size(name) for name in ("groups", "tensor", "store"))
    fits = sizes == (2, 8, 2) and tokens.shape[1] == BLOCK
    return (chain_body if fits else general_body)(tokens, *rest)


def solution(mesh):
    placed = (
        P(("groups", "store"), "tensor", None),
        P(None, "tensor"),
        P(("tensor", "store"), None, None),
        P(("tensor", "store"), None, None),
        P(),
        P(),
    )
    return jax.shard_map(
        body,
        mesh=mesh,
        in_specs=placed,
        out_specs=P(("groups", "store"), None, "tensor"),
        check_vma=False,
    )
```

```python
import jax
import jax.numpy as jnp
from jax import lax
from jax.sharding import PartitionSpec as P

BLOCK = 128


def find_slots(adapter_home_slot, adapter_per_block):
    catalog = jnp.arange(adapter_home_slot.shape[0], dtype=jnp.int32)
    return jnp.sum(
        jnp.where(
            adapter_per_block[:, :, None] == catalog[None, None, :],
            adapter_home_slot[None, None, :],
            0,
        ),
        axis=2,
    )


def general_body(
    tokens, query_weight, adapter_down_maps, adapter_up_maps, adapter_home_slot, adapter_per_block
):
    shard_count = lax.axis_size("tensor")
    store_count = lax.axis_size("store")
    devices_all = shard_count * store_count
    my_tensor = lax.axis_index("tensor")
    my_store = lax.axis_index("store")
    myself = lax.axis_index(("tensor", "store"))
    held_adapters, rank_index, feature_width = adapter_down_maps.shape
    feature_index = query_weight.shape[1]
    own_rows = tokens[0]
    group_rows = own_rows.shape[0] * shard_count
    blocks = group_rows // BLOCK
    store_slots = find_slots(adapter_home_slot, adapter_per_block)
    owner = store_slots // held_adapters
    inside = store_slots % held_adapters
    picked = jnp.max(jnp.where(owner == myself, inside, -1), axis=1)
    select = (picked[:, None] == jnp.arange(held_adapters, dtype=jnp.int32)[None, :]).astype(
        jnp.bfloat16
    )
    down_map_parts = adapter_down_maps.reshape(
        held_adapters, rank_index, shard_count, feature_index
    )
    up_map_parts = adapter_up_maps.reshape(held_adapters, rank_index, shard_count, feature_index)
    send_down = jnp.einsum(
        "sl,lrtf->tsrf", select, down_map_parts, preferred_element_type=jnp.float32
    ).astype(jnp.bfloat16)
    send_up = jnp.einsum(
        "sl,lrtf->tsrf", select, up_map_parts, preferred_element_type=jnp.float32
    ).astype(jnp.bfloat16)
    recv_down, recv_up = (
        lax.all_to_all(
            sent.reshape(devices_all, rank_index, feature_index),
            ("tensor", "store"),
            split_axis=0,
            concat_axis=0,
            tiled=True,
        )
        for sent in (send_down, send_up)
    )
    owner_row = lax.dynamic_index_in_dim(owner, my_store, 0, keepdims=False)
    source_pick = (owner_row[:, None] == jnp.arange(devices_all, dtype=jnp.int32)[None, :]).astype(
        jnp.bfloat16
    )
    block_down = jnp.einsum(
        "bj,jrf->brf", source_pick, recv_down, preferred_element_type=jnp.float32
    ).astype(jnp.bfloat16)
    block_up = jnp.einsum(
        "bj,jrf->brf", source_pick, recv_up, preferred_element_type=jnp.float32
    ).astype(jnp.bfloat16)
    piece = lax.all_gather(own_rows, "tensor", axis=0, tiled=True)
    product = jnp.dot(piece, query_weight, preferred_element_type=jnp.float32)
    features = lax.dynamic_slice_in_dim(piece, my_tensor * feature_index, feature_index, 1)
    partial_value = jnp.einsum(
        "bnf,brf->bnr",
        features.reshape(blocks, BLOCK, feature_index),
        block_down,
        preferred_element_type=jnp.float32,
    )
    shrunk = lax.psum(partial_value, "tensor").astype(jnp.bfloat16)
    grown = jnp.einsum(
        "bnr,brf->bnf", shrunk, block_up, preferred_element_type=jnp.float32
    ).reshape(group_rows, feature_index)
    query = (product + 0.5 * grown).astype(jnp.bfloat16)
    return query[None]


def both_ways(pairs):
    return pairs + [(b, a) for a, b in pairs]


ACROSS = both_ways([(0, 1), (2, 3), (4, 5), (6, 7)])
NEAR = both_ways([(0, 2), (1, 3), (4, 6), (5, 7)])
FAR = both_ways([(0, 4), (1, 5), (2, 6), (3, 7)])
CHUNKS = 4


def swap(value, axis):
    return lax.ppermute(value, axis, [(0, 1), (1, 0)])


def chain_body(
    tokens, query_weight, adapter_down_maps, adapter_up_maps, adapter_home_slot, adapter_per_block
):
    me = lax.axis_index("tensor")
    store = lax.axis_index("store")
    group = lax.axis_index("groups")
    myself = me * 2 + store
    held, rank, width = adapter_down_maps.shape
    columns = query_weight.shape[1]
    part = columns // 2
    rows = tokens[0]
    step = BLOCK // CHUNKS

    store_slots = find_slots(adapter_home_slot, adapter_per_block)
    owner = store_slots // held
    inside = store_slots % held
    picked = jnp.max(jnp.where(owner == myself, inside, 0), axis=1)
    owner_row = lax.dynamic_index_in_dim(owner, store, 0, keepdims=False)

    gathered = [
        lax.all_gather(rows[c * step : (c + 1) * step], "tensor", axis=0) for c in range(CHUNKS)
    ]

    def pick(maps, index):
        local = lax.dynamic_index_in_dim(picked, index, 0, keepdims=False)
        return lax.dynamic_index_in_dim(maps, local, 0, keepdims=False)

    down_own = pick(adapter_down_maps, store)
    down_swapped = swap(pick(adapter_down_maps, 1 - store), "store")
    candidates = jnp.concatenate([down_own, down_swapped])
    use_own = (owner_row == myself)[:, None, None]
    use_swapped = (owner_row == me * 2 + 1 - store)[:, None, None]

    def shrink(chunk):
        value = lax.dot_general(
            candidates,
            chunk.reshape(8 * step, width),
            (((1,), (1,)), ((), ())),
            preferred_element_type=jnp.float32,
        )
        value = value.reshape(2, rank, 8, step).transpose(0, 2, 1, 3)
        value = jnp.where(use_own, value[0], jnp.where(use_swapped, value[1], 0))
        value = value.astype(jnp.bfloat16)
        for pairs in (ACROSS, NEAR, FAR):
            value = value + lax.ppermute(value, "tensor", pairs)
        return value

    def columns_of(up):
        halves = up.reshape(rank, 8, 2, part)
        half = lax.dynamic_index_in_dim(halves, group, 2, keepdims=False)
        return half.transpose(1, 0, 2)

    up_sent = jnp.stack(
        [columns_of(pick(adapter_up_maps, 0)), columns_of(pick(adapter_up_maps, 1))], axis=1
    )
    up_got = lax.all_to_all(
        up_sent.reshape(16, rank, part), ("tensor", "store"), split_axis=0, concat_axis=0, tiled=True
    )
    up_half = jnp.stack(
        [lax.dynamic_index_in_dim(up_got, owner_row[b], 0, keepdims=False) for b in range(8)]
    )
    up_other = swap(up_half, "groups")
    up = jnp.concatenate(
        [jnp.where(group == 0, up_half, up_other), jnp.where(group == 0, up_other, up_half)], axis=2
    )

    outputs = []
    for chunk in gathered:
        base = jnp.dot(
            chunk.reshape(8 * step, width), query_weight, preferred_element_type=jnp.float32
        )
        grown = jnp.einsum("brn,brf->bnf", shrink(chunk), up, preferred_element_type=jnp.float32)
        value = base.reshape(8, step, columns) + 0.5 * grown
        outputs.append(value.astype(jnp.bfloat16))
    query = jnp.concatenate(outputs, axis=1)
    return query.reshape(1, 8 * BLOCK, columns)


def body(tokens, *rest):
    sizes = tuple(lax.axis_size(name) for name in ("groups", "tensor", "store"))
    fits = sizes == (2, 8, 2) and tokens.shape[1] == BLOCK
    return (chain_body if fits else general_body)(tokens, *rest)


def solution(mesh):
    placed = (
        P(("groups", "store"), "tensor", None),
        P(None, "tensor"),
        P(("tensor", "store"), None, None),
        P(("tensor", "store"), None, None),
        P(),
        P(),
    )
    return jax.shard_map(
        body,
        mesh=mesh,
        in_specs=placed,
        out_specs=P(("groups", "store"), None, "tensor"),
        check_vma=False,
    )
```

```python
import jax
import jax.numpy as jnp
from jax import lax
from jax.sharding import PartitionSpec as P

BLOCK = 128


def find_slots(adapter_home_slot, adapter_per_block):
    catalog = jnp.arange(adapter_home_slot.shape[0], dtype=jnp.int32)
    return jnp.sum(
        jnp.where(
            adapter_per_block[:, :, None] == catalog[None, None, :],
            adapter_home_slot[None, None, :],
            0,
        ),
        axis=2,
    )


def general_body(
    tokens, query_weight, adapter_down_maps, adapter_up_maps, adapter_home_slot, adapter_per_block
):
    shard_count = lax.axis_size("tensor")
    store_count = lax.axis_size("store")
    devices_all = shard_count * store_count
    my_tensor = lax.axis_index("tensor")
    my_store = lax.axis_index("store")
    myself = lax.axis_index(("tensor", "store"))
    held_adapters, rank_index, feature_width = adapter_down_maps.shape
    feature_index = query_weight.shape[1]
    own_rows = tokens[0]
    group_rows = own_rows.shape[0] * shard_count
    blocks = group_rows // BLOCK
    store_slots = find_slots(adapter_home_slot, adapter_per_block)
    owner = store_slots // held_adapters
    inside = store_slots % held_adapters
    picked = jnp.max(jnp.where(owner == myself, inside, -1), axis=1)
    select = (picked[:, None] == jnp.arange(held_adapters, dtype=jnp.int32)[None, :]).astype(
        jnp.bfloat16
    )
    down_map_parts = adapter_down_maps.reshape(
        held_adapters, rank_index, shard_count, feature_index
    )
    up_map_parts = adapter_up_maps.reshape(held_adapters, rank_index, shard_count, feature_index)
    send_down = jnp.einsum(
        "sl,lrtf->tsrf", select, down_map_parts, preferred_element_type=jnp.float32
    ).astype(jnp.bfloat16)
    send_up = jnp.einsum(
        "sl,lrtf->tsrf", select, up_map_parts, preferred_element_type=jnp.float32
    ).astype(jnp.bfloat16)
    recv_down, recv_up = (
        lax.all_to_all(
            sent.reshape(devices_all, rank_index, feature_index),
            ("tensor", "store"),
            split_axis=0,
            concat_axis=0,
            tiled=True,
        )
        for sent in (send_down, send_up)
    )
    owner_row = lax.dynamic_index_in_dim(owner, my_store, 0, keepdims=False)
    source_pick = (owner_row[:, None] == jnp.arange(devices_all, dtype=jnp.int32)[None, :]).astype(
        jnp.bfloat16
    )
    block_down = jnp.einsum(
        "bj,jrf->brf", source_pick, recv_down, preferred_element_type=jnp.float32
    ).astype(jnp.bfloat16)
    block_up = jnp.einsum(
        "bj,jrf->brf", source_pick, recv_up, preferred_element_type=jnp.float32
    ).astype(jnp.bfloat16)
    piece = lax.all_gather(own_rows, "tensor", axis=0, tiled=True)
    product = jnp.dot(piece, query_weight, preferred_element_type=jnp.float32)
    features = lax.dynamic_slice_in_dim(piece, my_tensor * feature_index, feature_index, 1)
    partial_value = jnp.einsum(
        "bnf,brf->bnr",
        features.reshape(blocks, BLOCK, feature_index),
        block_down,
        preferred_element_type=jnp.float32,
    )
    shrunk = lax.psum(partial_value, "tensor").astype(jnp.bfloat16)
    grown = jnp.einsum(
        "bnr,brf->bnf", shrunk, block_up, preferred_element_type=jnp.float32
    ).reshape(group_rows, feature_index)
    query = (product + 0.5 * grown).astype(jnp.bfloat16)
    return query[None]


def both_ways(pairs):
    return pairs + [(b, a) for a, b in pairs]


ACROSS = both_ways([(0, 1), (2, 3), (4, 5), (6, 7)])
NEAR = both_ways([(0, 2), (1, 3), (4, 6), (5, 7)])
MIDDLE = both_ways([(2, 4), (3, 5)])
OUTWARD = [(2, 0), (3, 1), (4, 6), (5, 7)]
FAR = both_ways([(0, 4), (1, 5), (2, 6), (3, 7)])
HALF = BLOCK // 2


def send(value, pairs):
    return lax.ppermute(value, "tensor", pairs)


def swap(value, axis):
    return lax.ppermute(value, axis, [(0, 1), (1, 0)])


def chain_body(
    tokens, query_weight, adapter_down_maps, adapter_up_maps, adapter_home_slot, adapter_per_block
):
    me = lax.axis_index("tensor")
    z, y = me // 2, me % 2
    store = lax.axis_index("store")
    group = lax.axis_index("groups")
    myself = me * 2 + store
    inner = (z == 1) | (z == 2)
    held, rank, width = adapter_down_maps.shape
    columns = query_weight.shape[1]
    part = columns // 2
    rows = tokens[0]

    store_slots = find_slots(adapter_home_slot, adapter_per_block)
    owner = store_slots // held
    inside = store_slots % held
    picked = jnp.max(jnp.where(owner == myself, inside, 0), axis=1)
    owner_row = lax.dynamic_index_in_dim(owner, store, 0, keepdims=False)

    def pick(maps, index):
        local = lax.dynamic_index_in_dim(picked, index, 0, keepdims=False)
        return lax.dynamic_index_in_dim(maps, local, 0, keepdims=False)

    def columns_of(up):
        halves = up.reshape(rank, 8, 2, part)
        half = lax.dynamic_index_in_dim(halves, group, 2, keepdims=False)
        return half.transpose(1, 0, 2)

    up_sent = jnp.stack(
        [columns_of(pick(adapter_up_maps, 0)), columns_of(pick(adapter_up_maps, 1))], axis=1
    )
    up_got = lax.all_to_all(
        up_sent.reshape(16, rank, part), ("tensor", "store"), split_axis=0, concat_axis=0, tiled=True
    )
    up_half = jnp.stack(
        [lax.dynamic_index_in_dim(up_got, owner_row[b], 0, keepdims=False) for b in range(8)]
    )
    up_other = swap(up_half, "groups")
    up = jnp.concatenate(
        [jnp.where(group == 0, up_half, up_other), jnp.where(group == 0, up_other, up_half)], axis=2
    )

    candidates = jnp.concatenate(
        [pick(adapter_down_maps, store), swap(pick(adapter_down_maps, 1 - store), "store")]
    )

    z_of = {
        "own": z,
        "near": z + 1 - 2 * (z % 2),
        "far": jnp.where(z < 2, 2, 1),
        "last": jnp.where(z < 2, 3, 0),
    }

    def place(name, half):
        column = 1 - y if name.endswith("_y") else y
        return z_of[name.removesuffix("_y")] * 2 + column, half

    def work(state, arrivals):
        base, shrunk = state
        block = jnp.concatenate([value for _, value in arrivals])
        product = jnp.dot(block, query_weight, preferred_element_type=jnp.float32)
        small = lax.dot_general(
            candidates, block, (((1,), (1,)), ((), ())), preferred_element_type=jnp.float32
        )
        for at, (name_half, _) in enumerate(arrivals):
            index, half = place(*name_half)
            home = lax.dynamic_index_in_dim(owner_row, index, 0, keepdims=False)
            cut = slice(at * HALF, (at + 1) * HALF)
            value = jnp.where(
                home == myself,
                small[:rank, cut],
                jnp.where(home == me * 2 + 1 - store, small[rank:, cut], 0),
            ).astype(jnp.bfloat16)
            shrunk = lax.dynamic_update_slice(shrunk, value[None, None], (index, half, 0, 0))
            base = lax.dynamic_update_slice(base, product[cut], (index * BLOCK + half * HALF, 0))
        return base, shrunk

    have = {("own", 0): rows[:HALF], ("own", 1): rows[HALF:]}
    state = (
        jnp.zeros((8 * BLOCK, columns), jnp.float32),
        jnp.zeros((8, 2, rank, HALF), jnp.bfloat16),
    )
    steps = [
        (("own", 0), ("own", 0, NEAR), ("own", 0)),
        (("own", 1), ("own", 1, NEAR), ("own", 1)),
        (("near", 0), ("far", 0, OUTWARD), ("near", 0)),
        (("far", 0), ("far", 1, OUTWARD), ("near", 1)),
        (("far", 1), ("last", 0, OUTWARD), None),
        (("last", 0), ("last", 1, OUTWARD), None),
        (("last", 1), ("own_y", 1, NEAR), None),
    ]
    inner_has = {}
    fresh = [(("own", 0), have["own", 0]), (("own", 1), have["own", 1])]
    for across, along, middle in steps:
        got_y = send(have[across], ACROSS)
        name, half, pairs = along
        sent = inner_has[name, half] if pairs is OUTWARD else have[name, half]
        got_z = send(sent, pairs)
        got_m = None if middle is None else send(have[middle], MIDDLE)
        state = work(state, fresh)
        got_y, got_z, got_m, state, have, inner_has = lax.optimization_barrier(
            (got_y, got_z, got_m, state, have, inner_has)
        )
        if middle is not None:
            inner_has[{"own": "far", "near": "last"}[middle[0]], middle[1]] = got_m
        if pairs is OUTWARD:
            arrived = (name, half)
            got_z = jnp.where(inner, inner_has[arrived], got_z)
        else:
            arrived = ({"own": "near", "own_y": "near_y"}[name], half)
        have[arrived] = got_z
        seen_y = ("own_y" if across[0] == "own" else across[0] + "_y", across[1])
        have[seen_y] = got_y
        fresh = [(arrived, got_z), (seen_y, got_y)]
    base, shrunk = work(state, fresh)

    for pairs in (ACROSS, NEAR, FAR):
        shrunk = shrunk + send(shrunk, pairs)
    grown = jnp.einsum("bhrn,brf->bhnf", shrunk, up, preferred_element_type=jnp.float32)
    query = base + 0.5 * grown.reshape(8 * BLOCK, columns)
    return query.astype(jnp.bfloat16)[None]


def body(tokens, *rest):
    sizes = tuple(lax.axis_size(name) for name in ("groups", "tensor", "store"))
    fits = sizes == (2, 8, 2) and tokens.shape[1] == BLOCK
    return (chain_body if fits else general_body)(tokens, *rest)


def solution(mesh):
    placed = (
        P(("groups", "store"), "tensor", None),
        P(None, "tensor"),
        P(("tensor", "store"), None, None),
        P(("tensor", "store"), None, None),
        P(),
        P(),
    )
    return jax.shard_map(
        body,
        mesh=mesh,
        in_specs=placed,
        out_specs=P(("groups", "store"), None, "tensor"),
        check_vma=False,
    )
```

```python
import functools

import jax
import jax.numpy as jnp
from jax import lax
from jax.experimental import pallas as pl
from jax.experimental.pallas import tpu as pltpu
from jax.sharding import PartitionSpec as P

BLOCK = 128


def find_slots(adapter_home_slot, adapter_per_block):
    catalog = jnp.arange(adapter_home_slot.shape[0], dtype=jnp.int32)
    return jnp.sum(
        jnp.where(
            adapter_per_block[:, :, None] == catalog[None, None, :],
            adapter_home_slot[None, None, :],
            0,
        ),
        axis=2,
    )


def general_body(
    tokens, query_weight, adapter_down_maps, adapter_up_maps, adapter_home_slot, adapter_per_block
):
    shard_count = lax.axis_size("tensor")
    store_count = lax.axis_size("store")
    devices_all = shard_count * store_count
    my_tensor = lax.axis_index("tensor")
    my_store = lax.axis_index("store")
    myself = lax.axis_index(("tensor", "store"))
    held_adapters, rank_index, feature_width = adapter_down_maps.shape
    feature_index = query_weight.shape[1]
    own_rows = tokens[0]
    group_rows = own_rows.shape[0] * shard_count
    blocks = group_rows // BLOCK
    store_slots = find_slots(adapter_home_slot, adapter_per_block)
    owner = store_slots // held_adapters
    inside = store_slots % held_adapters
    picked = jnp.max(jnp.where(owner == myself, inside, -1), axis=1)
    select = (picked[:, None] == jnp.arange(held_adapters, dtype=jnp.int32)[None, :]).astype(
        jnp.bfloat16
    )
    down_map_parts = adapter_down_maps.reshape(
        held_adapters, rank_index, shard_count, feature_index
    )
    up_map_parts = adapter_up_maps.reshape(held_adapters, rank_index, shard_count, feature_index)
    send_down = jnp.einsum(
        "sl,lrtf->tsrf", select, down_map_parts, preferred_element_type=jnp.float32
    ).astype(jnp.bfloat16)
    send_up = jnp.einsum(
        "sl,lrtf->tsrf", select, up_map_parts, preferred_element_type=jnp.float32
    ).astype(jnp.bfloat16)
    recv_down, recv_up = (
        lax.all_to_all(
            sent.reshape(devices_all, rank_index, feature_index),
            ("tensor", "store"),
            split_axis=0,
            concat_axis=0,
            tiled=True,
        )
        for sent in (send_down, send_up)
    )
    owner_row = lax.dynamic_index_in_dim(owner, my_store, 0, keepdims=False)
    source_pick = (owner_row[:, None] == jnp.arange(devices_all, dtype=jnp.int32)[None, :]).astype(
        jnp.bfloat16
    )
    block_down = jnp.einsum(
        "bj,jrf->brf", source_pick, recv_down, preferred_element_type=jnp.float32
    ).astype(jnp.bfloat16)
    block_up = jnp.einsum(
        "bj,jrf->brf", source_pick, recv_up, preferred_element_type=jnp.float32
    ).astype(jnp.bfloat16)
    piece = lax.all_gather(own_rows, "tensor", axis=0, tiled=True)
    product = jnp.dot(piece, query_weight, preferred_element_type=jnp.float32)
    features = lax.dynamic_slice_in_dim(piece, my_tensor * feature_index, feature_index, 1)
    partial_value = jnp.einsum(
        "bnf,brf->bnr",
        features.reshape(blocks, BLOCK, feature_index),
        block_down,
        preferred_element_type=jnp.float32,
    )
    shrunk = lax.psum(partial_value, "tensor").astype(jnp.bfloat16)
    grown = jnp.einsum(
        "bnr,brf->bnf", shrunk, block_up, preferred_element_type=jnp.float32
    ).reshape(group_rows, feature_index)
    query = (product + 0.5 * grown).astype(jnp.bfloat16)
    return query[None]


def both_ways(pairs):
    return pairs + [(b, a) for a, b in pairs]


ACROSS = both_ways([(0, 1), (2, 3), (4, 5), (6, 7)])
NEAR = both_ways([(0, 2), (1, 3), (4, 6), (5, 7)])
MIDDLE = both_ways([(2, 4), (3, 5)])
OUTWARD = [(2, 0), (3, 1), (4, 6), (5, 7)]
ALONG = [[(i, (i + 2 * d) % 8) for i in range(8)] for d in (1, 2, 3)]
PIECE = BLOCK // 4
DEPTH = 2048
VMEM_LIMIT = 40 * 1024 * 1024


def send(value, pairs):
    return lax.ppermute(value, "tensor", pairs)


def swap(value, axis):
    return lax.ppermute(value, axis, [(0, 1), (1, 0)])


def params():
    return pltpu.CompilerParams(vmem_limit_bytes=VMEM_LIMIT)


def rows_kernel(n, with_base, with_small, aliased, table, *refs):
    refs = list(refs)
    pieces = [refs.pop(0) for _ in range(n)]
    weight = refs.pop(0) if with_base else None
    downs = [refs.pop(0) for _ in range(2)] if with_small else None
    if aliased:
        for _ in range(with_base + with_small):
            refs.pop(0)
    base_out = refs.pop(0) if with_base else None
    small_out = refs.pop(0) if with_small else None
    acc = refs.pop(0) if with_base else None
    small, rounded = (refs.pop(0), refs.pop(0)) if with_small else (None, None)
    sems = refs.pop(0)
    k = pl.program_id(0)
    x = jnp.concatenate([p[...] for p in pieces], axis=0)

    def add(total, value):
        @pl.when(k == 0)
        def _():
            total[...] = value

        @pl.when(k > 0)
        def _():
            total[...] += value

    if with_base:
        add(acc, jnp.dot(x, weight[...], preferred_element_type=jnp.float32))
    if with_small:
        down = jnp.concatenate([downs[0][0], downs[1][...]], axis=0)
        add(
            small,
            lax.dot_general(
                x, down, (((1,), (1,)), ((), ())), preferred_element_type=jnp.float32
            ),
        )

    @pl.when(k == pl.num_programs(0) - 1)
    def _():
        copies = []
        for i in range(n):
            cut = pl.ds(i * PIECE, PIECE)
            if with_base:
                to = pl.ds(pl.multiple_of(table[1 + i] * PIECE, PIECE), PIECE)
                copies.append(
                    pltpu.make_async_copy(acc.at[cut], base_out.at[to], sems.at[len(copies)])
                )
            if with_small:
                lane = lax.broadcasted_iota(jnp.int32, (PIECE, 2 * 64), 1)
                use = jnp.where(lane < 64, table[1 + 2 * n + i], table[1 + 3 * n + i])
                rounded[cut] = jnp.where(use > 0, small[cut], 0.0).astype(jnp.bfloat16)
                to = pl.ds(pl.multiple_of(table[1 + n + i] * PIECE, PIECE), PIECE)
                copies.append(
                    pltpu.make_async_copy(rounded.at[cut], small_out.at[to], sems.at[len(copies)])
                )
        for copy in copies:
            copy.start()
        for copy in copies:
            copy.wait()


def rows_call(pieces, table, weight, down_maps, down_swapped, base, small, wants):
    n = len(pieces)
    with_base, with_small = wants
    width, columns = weight.shape
    rank = down_swapped.shape[0]
    aliased = base is not None
    operands, specs = list(pieces), []
    specs += [pl.BlockSpec((PIECE, DEPTH), lambda k, t: (0, k))] * n
    if with_base:
        operands.append(weight)
        specs.append(pl.BlockSpec((DEPTH, columns), lambda k, t: (k, 0)))
    if with_small:
        operands += [down_maps, down_swapped]
        specs.append(pl.BlockSpec((1, rank, DEPTH), lambda k, t: (t[0], 0, k)))
        specs.append(pl.BlockSpec((rank, DEPTH), lambda k, t: (0, k)))
    outs, scratch, aliases = [], [], {}
    rows = 8 * BLOCK
    if with_base:
        outs.append(jax.ShapeDtypeStruct((rows, columns), jnp.float32))
        scratch.append(pltpu.VMEM((n * PIECE, columns), jnp.float32))
    if with_small:
        outs.append(jax.ShapeDtypeStruct((rows, 2 * rank), jnp.bfloat16))
        scratch.append(pltpu.VMEM((n * PIECE, 2 * rank), jnp.float32))
        scratch.append(pltpu.VMEM((n * PIECE, 2 * rank), jnp.bfloat16))
    scratch.append(pltpu.SemaphoreType.DMA((2 * n,)))
    if aliased:
        for at, value in enumerate([base] * with_base + [small] * with_small):
            aliases[1 + len(operands)] = at
            operands.append(value)
            specs.append(pl.BlockSpec(memory_space=pl.ANY))
    wide = columns * with_base + 2 * rank * with_small
    return pl.pallas_call(
        functools.partial(rows_kernel, n, with_base, with_small, aliased),
        grid_spec=pltpu.PrefetchScalarGridSpec(
            num_scalar_prefetch=1,
            grid=(width // DEPTH,),
            in_specs=specs,
            out_specs=[pl.BlockSpec(memory_space=pl.ANY)] * len(outs),
            scratch_shapes=scratch,
        ),
        out_shape=outs,
        input_output_aliases=aliases,
        compiler_params=params(),
        cost_estimate=pl.CostEstimate(
            flops=2 * n * PIECE * width * wide,
            bytes_accessed=2 * width * (wide + n * PIECE),
            transcendentals=0,
        ),
        name="rows",
    )(table, *operands)


def pack_kernel(table, up, out):
    part = out.shape[3]
    for t in range(8):
        at = pl.multiple_of((2 * t + table[2]) * part, part)
        out[t, 0] = up[0, :, pl.ds(at, part)]


def pack_call(table, up_maps):
    _, rank, width = up_maps.shape
    part = width // 16
    return pl.pallas_call(
        pack_kernel,
        grid_spec=pltpu.PrefetchScalarGridSpec(
            num_scalar_prefetch=1,
            grid=(2,),
            in_specs=[pl.BlockSpec((1, rank, width), lambda s, t: (t[s], 0, 0))],
            out_specs=pl.BlockSpec((8, 1, rank, part), lambda s, t: (0, s, 0, 0)),
        ),
        out_shape=jax.ShapeDtypeStruct((8, 2, rank, part), jnp.bfloat16),
        compiler_params=params(),
        name="pack",
    )(table, up_maps)


def take_kernel(table, got, out):
    out[...] = got[...]


def take_call(table, got):
    _, rank, part = got.shape
    return pl.pallas_call(
        take_kernel,
        grid_spec=pltpu.PrefetchScalarGridSpec(
            num_scalar_prefetch=1,
            grid=(8,),
            in_specs=[pl.BlockSpec((1, rank, part), lambda b, t: (t[b], 0, 0))],
            out_specs=pl.BlockSpec((1, rank, part), lambda b, t: (b, 0, 0)),
        ),
        out_shape=jax.ShapeDtypeStruct((8, rank, part), jnp.bfloat16),
        compiler_params=params(),
        name="take",
    )(table, got)


def finish_kernel(table, base, first, second, up_mine, up_other, out):
    both = jnp.concatenate([first[...], second[...]], axis=0).astype(jnp.float32)
    shrunk = (both[:, :64] + both[:, 64:]).astype(jnp.bfloat16)
    part = up_mine.shape[2]
    for up, side in ((up_mine, table[0]), (up_other, 1 - table[0])):
        cut = pl.ds(pl.multiple_of(side * part, part), part)
        grown = jnp.dot(shrunk, up[0], preferred_element_type=jnp.float32)
        out[:, cut] = (base[:, cut] + 0.5 * grown).astype(out.dtype)


def finish_call(table, base, first, second, up_mine, up_other):
    rows, columns = base.shape
    _, rank, part = up_mine.shape
    half = pl.BlockSpec((BLOCK // 2, 2 * rank), lambda b, t: (b, 0))
    up = pl.BlockSpec((1, rank, part), lambda b, t: (b, 0, 0))
    whole = pl.BlockSpec((BLOCK, columns), lambda b, t: (b, 0))
    return pl.pallas_call(
        finish_kernel,
        grid_spec=pltpu.PrefetchScalarGridSpec(
            num_scalar_prefetch=1,
            grid=(8,),
            in_specs=[whole, half, half, up, up],
            out_specs=whole,
        ),
        out_shape=jax.ShapeDtypeStruct((rows, columns), jnp.bfloat16),
        compiler_params=params(),
        name="finish",
    )(table, base, first, second, up_mine, up_other)


STEPS = [
    (("own", 0), ("own", 0, NEAR), ("own", 0)),
    (("own", 1), ("own", 1, NEAR), ("near", 0)),
    (("near", 0), ("far", 0, OUTWARD), ("own", 1)),
    (("far", 0), ("last", 0, OUTWARD), ("near", 1)),
    (("last", 0), ("far", 1, OUTWARD), None),
    (("far", 1), ("last", 1, OUTWARD), None),
    (("last", 1), ("own_y", 1, NEAR), None),
]


def chain_body(
    tokens, query_weight, adapter_down_maps, adapter_up_maps, adapter_home_slot, adapter_per_block
):
    me = lax.axis_index("tensor")
    z, y = me // 2, me % 2
    store = lax.axis_index("store")
    group = lax.axis_index("groups")
    myself = me * 2 + store
    inner = (z == 1) | (z == 2)
    held, rank, width = adapter_down_maps.shape
    rows = tokens[0]

    store_slots = find_slots(adapter_home_slot, adapter_per_block)
    owner = store_slots // held
    inside = store_slots % held
    picked = jnp.max(jnp.where(owner == myself, inside, 0), axis=1)
    owner_row = lax.dynamic_index_in_dim(owner, store, 0, keepdims=False)
    pick_own = lax.dynamic_index_in_dim(picked, store, 0, keepdims=False)
    pick_lent = lax.dynamic_index_in_dim(picked, 1 - store, 0, keepdims=False)
    is_own = (owner_row == myself).astype(jnp.int32)
    is_swapped = (owner_row == me * 2 + 1 - store).astype(jnp.int32)

    z_of = {
        "own": z,
        "near": z + 1 - 2 * (z % 2),
        "far": jnp.where(z < 2, 2, 1),
        "last": jnp.where(z < 2, 3, 0),
    }

    def make_table(keys):
        blocks, base_at, small_at = [], [], []
        for name, half, sub in keys:
            column = 1 - y if name.endswith("_y") else y
            block = z_of[name.removesuffix("_y")] * 2 + column
            blocks.append(block)
            base_at.append(block * 4 + half * 2 + sub)
            small_at.append(half * 16 + block * 2 + sub)
        blocks = jnp.stack(blocks)
        return jnp.concatenate(
            [pick_own[None], jnp.stack(base_at), jnp.stack(small_at), is_own[blocks], is_swapped[blocks]]
        ).astype(jnp.int32)

    def work(state, keys, have, wants=(True, True)):
        base, small = state
        outs = rows_call(
            [have[key] for key in keys],
            make_table(keys),
            query_weight,
            adapter_down_maps,
            down_swapped,
            base,
            small,
            wants,
        )
        if wants == (True, True):
            return tuple(outs)
        return (outs[0], small) if wants[0] else (base, outs[0])

    have = {
        ("own", half, sub): rows[(2 * half + sub) * PIECE : (2 * half + sub + 1) * PIECE]
        for half in range(2)
        for sub in range(2)
    }
    inner_has = {}

    def issue(n):
        across, along, middle = STEPS[n // 2]
        sub = n % 2
        name, half, pairs = along
        sent = (inner_has if pairs is OUTWARD else have)[name, half, sub]
        got = {"y": send(have[across + (sub,)], ACROSS), "z": send(sent, pairs)}
        if middle is not None:
            got["m"] = send(have[middle + (sub,)], MIDDLE)
        return got

    def arrive(n, got):
        across, along, middle = STEPS[n // 2]
        sub = n % 2
        name, half, pairs = along
        if middle is not None:
            inner_has[{"own": "far", "near": "last"}[middle[0]], middle[1], sub] = got["m"]
        if pairs is OUTWARD:
            key = (name, half, sub)
            have[key] = jnp.where(inner, inner_has[key], got["z"])
        else:
            key = ({"own": "near", "own_y": "near_y"}[name], half, sub)
            have[key] = got["z"]
        seen = (across[0] + "_y", across[1], sub)
        have[seen] = got["y"]
        return [key, seen]

    flight = {0: issue(0), 1: issue(1)}
    down_swapped = swap(
        lax.dynamic_index_in_dim(adapter_down_maps, pick_lent, 0, keepdims=False), "store"
    )
    up_sent = pack_call(jnp.concatenate([picked, group[None]]).astype(jnp.int32), adapter_up_maps)

    state = (None, None)
    waiting = [key for key in have]
    extra = {"up": up_sent}
    up_got = None
    for n in range(14):
        got, state, have, inner_has, extra = lax.optimization_barrier(
            (flight.pop(n), state, have, inner_has, extra)
        )
        waiting += arrive(n, got)
        if n + 2 < 14:
            flight[n + 2] = issue(n + 2)
        if n == 9:
            up_got = lax.all_to_all(
                extra.pop("up").reshape(16, rank, -1),
                ("tensor", "store"),
                split_axis=0,
                concat_axis=0,
                tiled=True,
            )
        if n == 10:
            first = state[1][: 4 * BLOCK]
            flight[12]["first"] = send(first, ACROSS)
            extra["first"] = first
        if n == 12:
            first = extra.pop("first") + got["first"]
            firsts = [first] + [send(first, pairs) for pairs in ALONG]
        if n in (1, 5, 9, 11):
            state = work(state, waiting, have)
            waiting = []

    state = work(state, waiting, have, (False, True))
    second = state[1][4 * BLOCK :]
    second = second + send(second, ACROSS)
    seconds = [second] + [send(second, pairs) for pairs in ALONG]
    state = work(state, waiting, have, (True, False))

    up_mine = take_call(owner_row.astype(jnp.int32), up_got)
    up_other = swap(up_mine, "groups")
    query = finish_call(
        group[None].astype(jnp.int32), state[0], sum(firsts), sum(seconds), up_mine, up_other
    )
    return query[None]


def body(tokens, *rest):
    sizes = tuple(lax.axis_size(name) for name in ("groups", "tensor", "store"))
    fits = sizes == (2, 8, 2) and tokens.shape[1] == BLOCK
    return (chain_body if fits else general_body)(tokens, *rest)


def solution(mesh):
    placed = (
        P(("groups", "store"), "tensor", None),
        P(None, "tensor"),
        P(("tensor", "store"), None, None),
        P(("tensor", "store"), None, None),
        P(),
        P(),
    )
    return jax.shard_map(
        body,
        mesh=mesh,
        in_specs=placed,
        out_specs=P(("groups", "store"), None, "tensor"),
        check_vma=False,
    )
```

```python
import functools

import jax
import jax.numpy as jnp
import numpy as np
from jax import lax
from jax.experimental import pallas as pl
from jax.experimental.pallas import tpu as pltpu
from jax.sharding import PartitionSpec as P

BLOCK = 128


def find_slots(adapter_home_slot, adapter_per_block):
    catalog = jnp.arange(adapter_home_slot.shape[0], dtype=jnp.int32)
    return jnp.sum(
        jnp.where(
            adapter_per_block[:, :, None] == catalog[None, None, :],
            adapter_home_slot[None, None, :],
            0,
        ),
        axis=2,
    )


def general_body(
    tokens, query_weight, adapter_down_maps, adapter_up_maps, adapter_home_slot, adapter_per_block
):
    shard_count = lax.axis_size("tensor")
    store_count = lax.axis_size("store")
    devices_all = shard_count * store_count
    my_tensor = lax.axis_index("tensor")
    my_store = lax.axis_index("store")
    myself = lax.axis_index(("tensor", "store"))
    held_adapters, rank_index, feature_width = adapter_down_maps.shape
    feature_index = query_weight.shape[1]
    own_rows = tokens[0]
    group_rows = own_rows.shape[0] * shard_count
    blocks = group_rows // BLOCK
    store_slots = find_slots(adapter_home_slot, adapter_per_block)
    owner = store_slots // held_adapters
    inside = store_slots % held_adapters
    picked = jnp.max(jnp.where(owner == myself, inside, -1), axis=1)
    select = (picked[:, None] == jnp.arange(held_adapters, dtype=jnp.int32)[None, :]).astype(
        jnp.bfloat16
    )
    down_map_parts = adapter_down_maps.reshape(
        held_adapters, rank_index, shard_count, feature_index
    )
    up_map_parts = adapter_up_maps.reshape(held_adapters, rank_index, shard_count, feature_index)
    send_down = jnp.einsum(
        "sl,lrtf->tsrf", select, down_map_parts, preferred_element_type=jnp.float32
    ).astype(jnp.bfloat16)
    send_up = jnp.einsum(
        "sl,lrtf->tsrf", select, up_map_parts, preferred_element_type=jnp.float32
    ).astype(jnp.bfloat16)
    recv_down, recv_up = (
        lax.all_to_all(
            sent.reshape(devices_all, rank_index, feature_index),
            ("tensor", "store"),
            split_axis=0,
            concat_axis=0,
            tiled=True,
        )
        for sent in (send_down, send_up)
    )
    owner_row = lax.dynamic_index_in_dim(owner, my_store, 0, keepdims=False)
    source_pick = (owner_row[:, None] == jnp.arange(devices_all, dtype=jnp.int32)[None, :]).astype(
        jnp.bfloat16
    )
    block_down = jnp.einsum(
        "bj,jrf->brf", source_pick, recv_down, preferred_element_type=jnp.float32
    ).astype(jnp.bfloat16)
    block_up = jnp.einsum(
        "bj,jrf->brf", source_pick, recv_up, preferred_element_type=jnp.float32
    ).astype(jnp.bfloat16)
    piece = lax.all_gather(own_rows, "tensor", axis=0, tiled=True)
    product = jnp.dot(piece, query_weight, preferred_element_type=jnp.float32)
    features = lax.dynamic_slice_in_dim(piece, my_tensor * feature_index, feature_index, 1)
    partial_value = jnp.einsum(
        "bnf,brf->bnr",
        features.reshape(blocks, BLOCK, feature_index),
        block_down,
        preferred_element_type=jnp.float32,
    )
    shrunk = lax.psum(partial_value, "tensor").astype(jnp.bfloat16)
    grown = jnp.einsum(
        "bnr,brf->bnf", shrunk, block_up, preferred_element_type=jnp.float32
    ).reshape(group_rows, feature_index)
    query = (product + 0.5 * grown).astype(jnp.bfloat16)
    return query[None]


def both_ways(pairs):
    return pairs + [(b, a) for a, b in pairs]


ACROSS = both_ways([(0, 1), (2, 3), (4, 5), (6, 7)])
NEAR = both_ways([(0, 2), (1, 3), (4, 6), (5, 7)])
MIDDLE = both_ways([(2, 4), (3, 5)])
OUTWARD = [(2, 0), (3, 1), (4, 6), (5, 7)]
ALONG = [[(i, (i + 2 * d) % 8) for i in range(8)] for d in (1, 2, 3)]
PIECE = BLOCK // 4
DEPTH = 1024
VMEM_LIMIT = 16 * 1024 * 1024


def send(value, pairs):
    return lax.ppermute(value, "tensor", pairs)


def swap(value, axis):
    return lax.ppermute(value, axis, [(0, 1), (1, 0)])


def params():
    return pltpu.CompilerParams(vmem_limit_bytes=VMEM_LIMIT)


def rows_kernel(n, first, with_base, with_small, aliased, table, *refs):
    refs = list(refs)
    pieces = [refs.pop(0) for _ in range(n)]
    weight = refs.pop(0) if with_base else None
    downs = [refs.pop(0) for _ in range(2)] if with_small else None
    if aliased:
        for _ in range(with_base + with_small):
            refs.pop(0)
    base_out = refs.pop(0) if with_base else None
    small_out = refs.pop(0) if with_small else None
    acc = refs.pop(0) if with_base else None
    small, rounded = (refs.pop(0), refs.pop(0)) if with_small else (None, None)
    sems = refs.pop(0)
    k = pl.program_id(0)
    x = jnp.concatenate([p[...] for p in pieces], axis=0)

    def add(total, value):
        @pl.when(k == 0)
        def _():
            total[...] = value

        @pl.when(k > 0)
        def _():
            total[...] += value

    if with_base:
        add(acc, jnp.dot(x, weight[...], preferred_element_type=jnp.float32))
    if with_small:
        down = jnp.concatenate([downs[0][...], downs[1][...]], axis=0)
        add(
            small,
            lax.dot_general(
                x, down, (((1,), (1,)), ((), ())), preferred_element_type=jnp.float32
            ),
        )

    @pl.when(k == pl.num_programs(0) - 1)
    def _():
        copies = []
        for i in range(n):
            cut = pl.ds(i * PIECE, PIECE)
            if with_base:
                to = pl.ds(pl.multiple_of(table[0, first + i] * PIECE, PIECE), PIECE)
                copies.append(
                    pltpu.make_async_copy(acc.at[cut], base_out.at[to], sems.at[len(copies)])
                )
            if with_small:
                lane = lax.broadcasted_iota(jnp.int32, (PIECE, 2 * 64), 1)
                use = jnp.where(lane < 64, table[2, first + i], table[3, first + i])
                rounded[cut] = jnp.where(use > 0, small[cut], 0.0).astype(jnp.bfloat16)
                to = pl.ds(pl.multiple_of(table[1, first + i] * PIECE, PIECE), PIECE)
                copies.append(
                    pltpu.make_async_copy(rounded.at[cut], small_out.at[to], sems.at[len(copies)])
                )
        for copy in copies:
            copy.start()
        for copy in copies:
            copy.wait()


def rows_call(first, pieces, table, weight, down_own, down_swapped, base, small, wants):
    n = len(pieces)
    with_base, with_small = wants
    width, columns = weight.shape
    rank = down_swapped.shape[0]
    aliased = base is not None
    operands, specs = list(pieces), []
    specs += [pl.BlockSpec((PIECE, DEPTH), lambda k, t: (0, k))] * n
    if with_base:
        operands.append(weight)
        specs.append(pl.BlockSpec((DEPTH, columns), lambda k, t: (k, 0)))
    if with_small:
        operands += [down_own, down_swapped]
        specs += [pl.BlockSpec((rank, DEPTH), lambda k, t: (0, k))] * 2
    outs, scratch, aliases = [], [], {}
    rows = 8 * BLOCK
    if with_base:
        outs.append(jax.ShapeDtypeStruct((rows, columns), jnp.float32))
        scratch.append(pltpu.VMEM((n * PIECE, columns), jnp.float32))
    if with_small:
        outs.append(jax.ShapeDtypeStruct((rows, 2 * rank), jnp.bfloat16))
        scratch.append(pltpu.VMEM((n * PIECE, 2 * rank), jnp.float32))
        scratch.append(pltpu.VMEM((n * PIECE, 2 * rank), jnp.bfloat16))
    scratch.append(pltpu.SemaphoreType.DMA((2 * n,)))
    if aliased:
        for at, value in enumerate([base] * with_base + [small] * with_small):
            aliases[1 + len(operands)] = at
            operands.append(value)
            specs.append(pl.BlockSpec(memory_space=pltpu.HBM))
    return pl.pallas_call(
        functools.partial(rows_kernel, n, first, with_base, with_small, aliased),
        grid_spec=pltpu.PrefetchScalarGridSpec(
            num_scalar_prefetch=1,
            grid=(width // DEPTH,),
            in_specs=specs,
            out_specs=[pl.BlockSpec(memory_space=pltpu.HBM)] * len(outs),
            scratch_shapes=scratch,
        ),
        out_shape=outs,
        input_output_aliases=aliases,
        compiler_params=params(),
        cost_estimate=pl.CostEstimate(flops=1, bytes_accessed=1, transcendentals=0),
        name="rows",
    )(table, *operands)


def pack_kernel(table, up, out):
    part = out.shape[3]
    for t in range(8):
        at = pl.multiple_of((2 * t + table[2]) * part, part)
        out[t, 0] = up[0, :, pl.ds(at, part)]


def pack_call(table, up_maps):
    _, rank, width = up_maps.shape
    part = width // 16
    return pl.pallas_call(
        pack_kernel,
        grid_spec=pltpu.PrefetchScalarGridSpec(
            num_scalar_prefetch=1,
            grid=(2,),
            in_specs=[pl.BlockSpec((1, rank, width), lambda s, t: (t[s], 0, 0))],
            out_specs=pl.BlockSpec((8, 1, rank, part), lambda s, t: (0, s, 0, 0)),
        ),
        out_shape=jax.ShapeDtypeStruct((8, 2, rank, part), jnp.bfloat16),
        compiler_params=params(),
        name="pack",
    )(table, up_maps)


def take_kernel(table, got, out):
    out[...] = got[...]


def take_call(table, got):
    _, rank, part = got.shape
    return pl.pallas_call(
        take_kernel,
        grid_spec=pltpu.PrefetchScalarGridSpec(
            num_scalar_prefetch=1,
            grid=(8,),
            in_specs=[pl.BlockSpec((1, rank, part), lambda b, t: (t[b], 0, 0))],
            out_specs=pl.BlockSpec((1, rank, part), lambda b, t: (b, 0, 0)),
        ),
        out_shape=jax.ShapeDtypeStruct((8, rank, part), jnp.bfloat16),
        compiler_params=params(),
        name="take",
    )(table, got)


def finish_kernel(table, base, first, second, up_mine, up_other, out):
    both = jnp.concatenate([first[...], second[...]], axis=0).astype(jnp.float32)
    shrunk = (both[:, :64] + both[:, 64:]).astype(jnp.bfloat16)
    part = up_mine.shape[2]
    for up, side in ((up_mine, table[0]), (up_other, 1 - table[0])):
        cut = pl.ds(pl.multiple_of(side * part, part), part)
        grown = jnp.dot(shrunk, up[0], preferred_element_type=jnp.float32)
        out[:, cut] = (base[:, cut] + 0.5 * grown).astype(out.dtype)


def finish_call(table, base, first, second, up_mine, up_other):
    rows, columns = base.shape
    _, rank, part = up_mine.shape
    half = pl.BlockSpec((BLOCK // 2, 2 * rank), lambda b, t: (b, 0))
    up = pl.BlockSpec((1, rank, part), lambda b, t: (b, 0, 0))
    whole = pl.BlockSpec((BLOCK, columns), lambda b, t: (b, 0))
    return pl.pallas_call(
        finish_kernel,
        grid_spec=pltpu.PrefetchScalarGridSpec(
            num_scalar_prefetch=1,
            grid=(8,),
            in_specs=[whole, half, half, up, up],
            out_specs=whole,
        ),
        out_shape=jax.ShapeDtypeStruct((rows, columns), jnp.bfloat16),
        compiler_params=params(),
        name="finish",
    )(table, base, first, second, up_mine, up_other)


STEPS = [
    (("own", 0), ("own", 0, NEAR), ("own", 0)),
    (("own", 1), ("own", 1, NEAR), ("near", 0)),
    (("near", 0), ("far", 0, OUTWARD), ("own", 1)),
    (("far", 0), ("last", 0, OUTWARD), ("near", 1)),
    (("last", 0), ("far", 1, OUTWARD), None),
    (("far", 1), ("last", 1, OUTWARD), None),
    (("last", 1), ("own_y", 1, NEAR), None),
]


def arrivals(n):
    across, (name, half, pairs), _ = STEPS[n // 2]
    along = name if pairs is OUTWARD else {"own": "near", "own_y": "near_y"}[name]
    return [(along, half, n % 2), (across[0] + "_y", across[1], n % 2)]


def chain_body(
    tokens, query_weight, adapter_down_maps, adapter_up_maps, adapter_home_slot, adapter_per_block
):
    me = lax.axis_index("tensor")
    z, y = me // 2, me % 2
    store = lax.axis_index("store")
    group = lax.axis_index("groups")
    myself = me * 2 + store
    inner = (z == 1) | (z == 2)
    held, rank, width = adapter_down_maps.shape
    rows = tokens[0]

    store_slots = find_slots(adapter_home_slot, adapter_per_block)
    owner = store_slots // held
    inside = store_slots % held
    picked = jnp.max(jnp.where(owner == myself, inside, 0), axis=1)
    owner_row = lax.dynamic_index_in_dim(owner, store, 0, keepdims=False)
    pick_own = lax.dynamic_index_in_dim(picked, store, 0, keepdims=False)
    pick_lent = lax.dynamic_index_in_dim(picked, 1 - store, 0, keepdims=False)
    is_own = (owner_row == myself).astype(jnp.int32)
    is_swapped = (owner_row == me * 2 + 1 - store).astype(jnp.int32)

    z_of = {
        "own": z,
        "near": z + 1 - 2 * (z % 2),
        "far": jnp.where(z < 2, 2, 1),
        "last": jnp.where(z < 2, 3, 0),
    }

    order = [("own", half, sub) for half in range(2) for sub in range(2)]
    for n in range(14):
        order += arrivals(n)
    order = {key: at for at, key in enumerate(order)}
    blocks, halves, subs = [], [], []
    for name, half, sub in order:
        column = 1 - y if name.endswith("_y") else y
        blocks.append(z_of[name.removesuffix("_y")] * 2 + column)
        halves.append(half)
        subs.append(sub)
    blocks = jnp.stack(blocks).astype(jnp.int32)
    halves, subs = np.array(halves, np.int32), np.array(subs, np.int32)
    hit = blocks[:, None] == jnp.arange(8, dtype=jnp.int32)[None, :]
    owners = jnp.sum(jnp.where(hit, owner_row[None, :], 0), axis=1)
    table = jnp.stack(
        [
            blocks * 4 + halves * 2 + subs,
            halves * 16 + blocks * 2 + subs,
            owners == myself,
            owners == me * 2 + 1 - store,
        ]
    ).astype(jnp.int32)

    def work(state, keys, have, wants=(True, True)):
        base, small = state
        outs = rows_call(
            order[keys[0]],
            [have[key] for key in keys],
            table,
            query_weight,
            down_own,
            down_swapped,
            base,
            small,
            wants,
        )
        if wants == (True, True):
            return tuple(outs)
        return (outs[0], small) if wants[0] else (base, outs[0])

    have = {
        ("own", half, sub): rows[(2 * half + sub) * PIECE : (2 * half + sub + 1) * PIECE]
        for half in range(2)
        for sub in range(2)
    }
    inner_has = {}

    def issue(n):
        across, along, middle = STEPS[n // 2]
        sub = n % 2
        name, half, pairs = along
        sent = (inner_has if pairs is OUTWARD else have)[name, half, sub]
        got = {"y": send(have[across + (sub,)], ACROSS), "z": send(sent, pairs)}
        if middle is not None:
            got["m"] = send(have[middle + (sub,)], MIDDLE)
        return got

    def arrive(n, got):
        across, along, middle = STEPS[n // 2]
        sub = n % 2
        name, half, pairs = along
        if middle is not None:
            inner_has[{"own": "far", "near": "last"}[middle[0]], middle[1], sub] = got["m"]
        key, seen = arrivals(n)
        have[key] = jnp.where(inner, inner_has[key], got["z"]) if pairs is OUTWARD else got["z"]
        have[seen] = got["y"]
        return [key, seen]

    flight = {0: issue(0), 1: issue(1)}
    down_own = lax.dynamic_index_in_dim(adapter_down_maps, pick_own, 0, keepdims=False)
    down_swapped = swap(
        lax.dynamic_index_in_dim(adapter_down_maps, pick_lent, 0, keepdims=False), "store"
    )
    up_sent = pack_call(jnp.concatenate([picked, group[None]]).astype(jnp.int32), adapter_up_maps)

    state = (None, None)
    waiting = [key for key in have]
    extra = {"up": up_sent}
    for n in range(14):
        got, state, have, inner_has, extra = lax.optimization_barrier(
            (flight.pop(n), state, have, inner_has, extra)
        )
        waiting += arrive(n, got)
        if n + 2 < 14:
            flight[n + 2] = issue(n + 2)
        if n == 9:
            up_got = lax.all_to_all(
                extra.pop("up").reshape(16, rank, -1),
                ("tensor", "store"),
                split_axis=0,
                concat_axis=0,
                tiled=True,
            )
        if n == 10:
            first = state[1][: 4 * BLOCK]
            flight[12]["first"] = send(first, ACROSS)
            extra["first"] = first
        if n == 12:
            extra["got"] = up_got
            first = extra.pop("first") + got["first"]
            firsts = [first] + [send(first, pairs) for pairs in ALONG]
        if n in (1, 5, 9, 11):
            state = work(state, waiting, have)
            waiting = []

    up_mine = take_call(owner_row.astype(jnp.int32), extra["got"])
    up_other = swap(up_mine, "groups")
    state = work(state, waiting, have, (False, True))
    second = state[1][4 * BLOCK :]
    second = second + send(second, ACROSS)
    seconds = [second] + [send(second, pairs) for pairs in ALONG]
    state = work(state, waiting, have, (True, False))

    query = finish_call(
        group[None].astype(jnp.int32), state[0], sum(firsts[1:], firsts[0]), sum(seconds[1:], seconds[0]), up_mine, up_other
    )
    return query[None]


def body(tokens, *rest):
    sizes = tuple(lax.axis_size(name) for name in ("groups", "tensor", "store"))
    fits = sizes == (2, 8, 2) and tokens.shape[1] == BLOCK
    return (chain_body if fits else general_body)(tokens, *rest)


def solution(mesh):
    placed = (
        P(("groups", "store"), "tensor", None),
        P(None, "tensor"),
        P(("tensor", "store"), None, None),
        P(("tensor", "store"), None, None),
        P(),
        P(),
    )
    return jax.shard_map(
        body,
        mesh=mesh,
        in_specs=placed,
        out_specs=P(("groups", "store"), None, "tensor"),
        check_vma=False,
    )
```

```python
import functools

import jax
import jax.numpy as jnp
import numpy as np
from jax import lax
from jax.experimental import pallas as pl
from jax.experimental.pallas import tpu as pltpu
from jax.sharding import PartitionSpec as P

BLOCK = 128


def find_slots(adapter_home_slot, adapter_per_block):
    catalog = jnp.arange(adapter_home_slot.shape[0], dtype=jnp.int32)
    return jnp.sum(
        jnp.where(
            adapter_per_block[:, :, None] == catalog[None, None, :],
            adapter_home_slot[None, None, :],
            0,
        ),
        axis=2,
    )


def general_body(
    tokens, query_weight, adapter_down_maps, adapter_up_maps, adapter_home_slot, adapter_per_block
):
    shard_count = lax.axis_size("tensor")
    store_count = lax.axis_size("store")
    devices_all = shard_count * store_count
    my_tensor = lax.axis_index("tensor")
    my_store = lax.axis_index("store")
    myself = lax.axis_index(("tensor", "store"))
    held_adapters, rank_index, feature_width = adapter_down_maps.shape
    feature_index = query_weight.shape[1]
    own_rows = tokens[0]
    group_rows = own_rows.shape[0] * shard_count
    blocks = group_rows // BLOCK
    store_slots = find_slots(adapter_home_slot, adapter_per_block)
    owner = store_slots // held_adapters
    inside = store_slots % held_adapters
    picked = jnp.max(jnp.where(owner == myself, inside, -1), axis=1)
    select = (picked[:, None] == jnp.arange(held_adapters, dtype=jnp.int32)[None, :]).astype(
        jnp.bfloat16
    )
    down_map_parts = adapter_down_maps.reshape(
        held_adapters, rank_index, shard_count, feature_index
    )
    up_map_parts = adapter_up_maps.reshape(held_adapters, rank_index, shard_count, feature_index)
    send_down = jnp.einsum(
        "sl,lrtf->tsrf", select, down_map_parts, preferred_element_type=jnp.float32
    ).astype(jnp.bfloat16)
    send_up = jnp.einsum(
        "sl,lrtf->tsrf", select, up_map_parts, preferred_element_type=jnp.float32
    ).astype(jnp.bfloat16)
    recv_down, recv_up = (
        lax.all_to_all(
            sent.reshape(devices_all, rank_index, feature_index),
            ("tensor", "store"),
            split_axis=0,
            concat_axis=0,
            tiled=True,
        )
        for sent in (send_down, send_up)
    )
    owner_row = lax.dynamic_index_in_dim(owner, my_store, 0, keepdims=False)
    source_pick = (owner_row[:, None] == jnp.arange(devices_all, dtype=jnp.int32)[None, :]).astype(
        jnp.bfloat16
    )
    block_down = jnp.einsum(
        "bj,jrf->brf", source_pick, recv_down, preferred_element_type=jnp.float32
    ).astype(jnp.bfloat16)
    block_up = jnp.einsum(
        "bj,jrf->brf", source_pick, recv_up, preferred_element_type=jnp.float32
    ).astype(jnp.bfloat16)
    piece = lax.all_gather(own_rows, "tensor", axis=0, tiled=True)
    product = jnp.dot(piece, query_weight, preferred_element_type=jnp.float32)
    features = lax.dynamic_slice_in_dim(piece, my_tensor * feature_index, feature_index, 1)
    partial_value = jnp.einsum(
        "bnf,brf->bnr",
        features.reshape(blocks, BLOCK, feature_index),
        block_down,
        preferred_element_type=jnp.float32,
    )
    shrunk = lax.psum(partial_value, "tensor").astype(jnp.bfloat16)
    grown = jnp.einsum(
        "bnr,brf->bnf", shrunk, block_up, preferred_element_type=jnp.float32
    ).reshape(group_rows, feature_index)
    query = (product + 0.5 * grown).astype(jnp.bfloat16)
    return query[None]


def both_ways(pairs):
    return pairs + [(b, a) for a, b in pairs]


ACROSS = both_ways([(0, 1), (2, 3), (4, 5), (6, 7)])
NEAR = both_ways([(0, 2), (1, 3), (4, 6), (5, 7)])
MIDDLE = both_ways([(2, 4), (3, 5)])
OUTWARD = [(2, 0), (3, 1), (4, 6), (5, 7)]
ALONG = [[(i, (i + 2 * d) % 8) for i in range(8)] for d in (1, 2, 3)]
HALF = BLOCK // 2
VMEM_LIMIT = 24 * 1024 * 1024


def send(value, pairs):
    return lax.ppermute(value, "tensor", pairs)


def swap(value, axis):
    return lax.ppermute(value, axis, [(0, 1), (1, 0)])


def params():
    return pltpu.CompilerParams(vmem_limit_bytes=VMEM_LIMIT)


def pack_kernel(table, up, out):
    part = out.shape[3]
    for t in range(8):
        at = pl.multiple_of((2 * t + table[2]) * part, part)
        out[t, 0] = up[0, :, pl.ds(at, part)]


def pack_call(table, up_maps):
    _, rank, width = up_maps.shape
    part = width // 16
    return pl.pallas_call(
        pack_kernel,
        grid_spec=pltpu.PrefetchScalarGridSpec(
            num_scalar_prefetch=1,
            grid=(2,),
            in_specs=[pl.BlockSpec((1, rank, width), lambda s, t: (t[s], 0, 0))],
            out_specs=pl.BlockSpec((8, 1, rank, part), lambda s, t: (0, s, 0, 0)),
        ),
        out_shape=jax.ShapeDtypeStruct((8, 2, rank, part), jnp.bfloat16),
        compiler_params=params(),
        name="pack",
    )(table, up_maps)


def take_kernel(table, got, out):
    out[...] = got[...]


def take_call(table, got):
    _, rank, part = got.shape
    return pl.pallas_call(
        take_kernel,
        grid_spec=pltpu.PrefetchScalarGridSpec(
            num_scalar_prefetch=1,
            grid=(8,),
            in_specs=[pl.BlockSpec((1, rank, part), lambda b, t: (t[b], 0, 0))],
            out_specs=pl.BlockSpec((1, rank, part), lambda b, t: (b, 0, 0)),
        ),
        out_shape=jax.ShapeDtypeStruct((8, rank, part), jnp.bfloat16),
        compiler_params=params(),
        name="take",
    )(table, got)


def finish_kernel(table, *refs):
    *bases, shrunk, up_mine, up_other, out = refs
    at = pl.program_id(0)
    second = table[1, at] > 0
    part = up_mine.shape[2]
    for g, base in enumerate(bases):

        @pl.when(at // 4 == g)
        def _():
            for up, side in ((up_mine, table[2, at]), (up_other, 1 - table[2, at])):
                cut = pl.ds(pl.multiple_of(side * part, part), part)
                grown = lax.dot_general(
                    shrunk[0], up[0], (((0,), (0,)), ((), ())), preferred_element_type=jnp.float32
                )
                grown = jnp.where(second, grown[HALF:], grown[:HALF])
                out[:, cut] = (base[:, cut] + 0.5 * grown).astype(out.dtype)


def finish_call(table, bases, shrunk, up_mine, up_other):
    columns = bases[0].shape[1]
    _, rank, part = up_mine.shape

    def base_spec(g):
        return pl.BlockSpec((HALF, columns), lambda i, t: (jnp.clip(i - 4 * g, 0, 3), 0))

    up = pl.BlockSpec((1, rank, part), lambda i, t: (t[0, i], 0, 0))
    return pl.pallas_call(
        finish_kernel,
        grid_spec=pltpu.PrefetchScalarGridSpec(
            num_scalar_prefetch=1,
            grid=(16,),
            in_specs=[base_spec(g) for g in range(4)]
            + [pl.BlockSpec((1, rank, BLOCK), lambda i, t: (t[0, i], 0, 0)), up, up],
            out_specs=pl.BlockSpec((HALF, columns), lambda i, t: (2 * t[0, i] + t[1, i], 0)),
        ),
        out_shape=jax.ShapeDtypeStruct((8 * BLOCK, columns), jnp.bfloat16),
        compiler_params=params(),
        name="finish",
    )(table, *bases, shrunk, up_mine, up_other)


ACROSS_SENDS = [
    ("own", 0), ("own", 1), ("near", 1), ("near", 0), ("far", 0), ("far", 1), ("last", 0)
]
ALONG_SENDS = [
    ("own", 0, NEAR), ("own", 1, NEAR), ("far", 0, OUTWARD), ("far", 1, OUTWARD),
    ("last", 0, OUTWARD), ("last", 1, OUTWARD), ("last_y", 1, OUTWARD),
]
MIDDLE_SENDS = [("own", 0), ("own", 1), ("near", 0), ("near", 1), ("near_y", 1)]
BEYOND = {"own": "far", "near": "last", "near_y": "last_y"}


def arrivals(n):
    name, half, pairs = ALONG_SENDS[n]
    across = ACROSS_SENDS[n]
    return [("near" if pairs is NEAR else name, half), (across[0] + "_y", across[1])]


def chain_body(
    tokens, query_weight, adapter_down_maps, adapter_up_maps, adapter_home_slot, adapter_per_block
):
    me = lax.axis_index("tensor")
    z, y = me // 2, me % 2
    store = lax.axis_index("store")
    group = lax.axis_index("groups")
    myself = me * 2 + store
    inner = (z == 1) | (z == 2)
    held, rank, width = adapter_down_maps.shape
    rows = tokens[0]

    have = {("own", 0): rows[:HALF], ("own", 1): rows[HALF:]}
    inner_has = {}

    def send_across(n):
        return send(have[ACROSS_SENDS[n]], ACROSS)

    def send_along(n):
        name, half, pairs = ALONG_SENDS[n]
        return send((inner_has if pairs is OUTWARD else have)[name, half], pairs)

    def send_middle(n):
        return send(have[MIDDLE_SENDS[n]], MIDDLE)

    flight = {n: {} for n in range(7)}
    flight[0]["z"], flight[0]["y"] = send_along(0), send_across(0)
    flight[0]["m"] = send_middle(0)
    flight[1]["z"], flight[1]["y"] = send_along(1), send_across(1)

    store_slots = find_slots(adapter_home_slot, adapter_per_block)
    owner = store_slots // held
    inside = store_slots % held
    picked = jnp.max(jnp.where(owner == myself, inside, 0), axis=1)
    owner_row = lax.dynamic_index_in_dim(owner, store, 0, keepdims=False).astype(jnp.int32)
    pick_own = lax.dynamic_index_in_dim(picked, store, 0, keepdims=False)
    pick_lent = lax.dynamic_index_in_dim(picked, 1 - store, 0, keepdims=False)

    down_own = lax.dynamic_index_in_dim(adapter_down_maps, pick_own, 0, keepdims=False)
    down_lent = lax.dynamic_index_in_dim(adapter_down_maps, pick_lent, 0, keepdims=False)
    candidates = jnp.concatenate([down_own, swap(down_lent, "store")])
    up_sent = pack_call(jnp.concatenate([picked, group[None]]).astype(jnp.int32), adapter_up_maps)

    z_of = {
        "own": z,
        "near": z + 1 - 2 * (z % 2),
        "far": jnp.where(z < 2, 2, 1),
        "last": jnp.where(z < 2, 3, 0),
    }
    order = [("own", 0), ("own", 1)]
    for n in range(7):
        order += arrivals(n)
    order = {key: at for at, key in enumerate(order)}
    blocks = jnp.stack(
        [
            z_of[name.removesuffix("_y")] * 2 + (1 - y if name.endswith("_y") else y)
            for name, _ in order
        ]
    ).astype(jnp.int32)
    halves = np.array([half for _, half in order], np.int32)
    hit = blocks[:, None] == jnp.arange(8, dtype=jnp.int32)[None, :]
    owners = jnp.sum(jnp.where(hit, owner_row[None, :], 0), axis=1)
    is_own = owners == myself
    is_swapped = owners == me * 2 + 1 - store

    def shrink(shrunk, keys):
        block = jnp.concatenate([have[key] for key in keys])
        small = lax.dot_general(
            candidates, block, (((1,), (1,)), ((), ())), preferred_element_type=jnp.float32
        )
        for i, key in enumerate(keys):
            at = order[key]
            cut = slice(i * HALF, (i + 1) * HALF)
            value = jnp.where(
                is_own[at], small[:rank, cut], jnp.where(is_swapped[at], small[rank:, cut], 0)
            )
            shrunk = lax.dynamic_update_slice(
                shrunk, value.astype(jnp.bfloat16)[None, None], (blocks[at], int(halves[at]), 0, 0)
            )
        return shrunk

    def times_weight(keys):
        block = jnp.concatenate([have[key] for key in keys])
        return jnp.dot(block, query_weight, preferred_element_type=jnp.float32)

    waiting = [("own", 0), ("own", 1)]
    shrunk = jnp.zeros((8, 2, rank, HALF), jnp.bfloat16)
    bases = []
    extra = {"up": up_sent}
    for n in range(7):
        got, have, inner_has, shrunk, bases, extra = lax.optimization_barrier(
            (flight[n], have, inner_has, shrunk, bases, extra)
        )
        if "m" in got:
            name, half = MIDDLE_SENDS[n]
            inner_has[BEYOND[name], half] = got["m"]
        along, across = arrivals(n)
        have[along] = (
            got["z"] if ALONG_SENDS[n][2] is NEAR else jnp.where(inner, inner_has[along], got["z"])
        )
        have[across] = got["y"]
        waiting += [along, across]
        if n == 1:
            flight[2]["y"] = send_across(2)
        if n + 2 < 7:
            flight[n + 2]["z"] = send_along(n + 2)
            if n > 0:
                flight[n + 2]["y"] = send_across(n + 2)
        if n + 1 < len(MIDDLE_SENDS):
            flight[n + 1]["m"] = send_middle(n + 1)
        if n == 4:
            flight[6]["up"] = lax.all_to_all(
                extra.pop("up").reshape(16, rank, -1),
                ("tensor", "store"),
                split_axis=0,
                concat_axis=0,
                tiled=True,
            )
        if n < 6:
            shrunk = shrink(shrunk, waiting[-2:] if n else waiting)
        if n == 5:
            early = shrunk[2:6]
            flight[6]["early"] = send(early, ACROSS)
            extra["early"] = early
        if len(waiting) == 4 and n < 6:
            bases = bases + [times_weight(waiting)]
            waiting = []

    shrunk = shrink(shrunk, waiting[-2:])
    late = jnp.concatenate([shrunk[:2], shrunk[6:]])
    late = late + send(late, ACROSS)
    early = extra["early"] + got["early"]
    for pairs in ALONG:
        early = early + send(extra["early"] + got["early"], pairs)
    lates = [late] + [send(late, pairs) for pairs in ALONG]
    bases = bases + [times_weight(waiting)]
    late = sum(lates[1:], lates[0])
    total = jnp.concatenate([late[:2], early, late[2:]])
    total = total.transpose(0, 2, 1, 3).reshape(8, rank, BLOCK)

    up_mine = take_call(owner_row, got["up"])
    up_other = swap(up_mine, "groups")
    table = jnp.stack([blocks, halves, jnp.broadcast_to(group, (16,))]).astype(jnp.int32)
    return finish_call(table, bases, total, up_mine, up_other)[None]


def body(tokens, *rest):
    sizes = tuple(lax.axis_size(name) for name in ("groups", "tensor", "store"))
    fits = sizes == (2, 8, 2) and tokens.shape[1] == BLOCK
    return (chain_body if fits else general_body)(tokens, *rest)


def solution(mesh):
    placed = (
        P(("groups", "store"), "tensor", None),
        P(None, "tensor"),
        P(("tensor", "store"), None, None),
        P(("tensor", "store"), None, None),
        P(),
        P(),
    )
    return jax.shard_map(
        body,
        mesh=mesh,
        in_specs=placed,
        out_specs=P(("groups", "store"), None, "tensor"),
        check_vma=False,
    )
```

```python
import functools

import jax
import jax.numpy as jnp
import numpy as np
from jax import lax
from jax.experimental import pallas as pl
from jax.experimental.pallas import tpu as pltpu
from jax.sharding import PartitionSpec as P

BLOCK = 128


def find_slots(adapter_home_slot, adapter_per_block):
    catalog = jnp.arange(adapter_home_slot.shape[0], dtype=jnp.int32)
    return jnp.sum(
        jnp.where(
            adapter_per_block[:, :, None] == catalog[None, None, :],
            adapter_home_slot[None, None, :],
            0,
        ),
        axis=2,
    )


def general_body(
    tokens, query_weight, adapter_down_maps, adapter_up_maps, adapter_home_slot, adapter_per_block
):
    shard_count = lax.axis_size("tensor")
    store_count = lax.axis_size("store")
    devices_all = shard_count * store_count
    my_tensor = lax.axis_index("tensor")
    my_store = lax.axis_index("store")
    myself = lax.axis_index(("tensor", "store"))
    held_adapters, rank_index, feature_width = adapter_down_maps.shape
    feature_index = query_weight.shape[1]
    own_rows = tokens[0]
    group_rows = own_rows.shape[0] * shard_count
    blocks = group_rows // BLOCK
    store_slots = find_slots(adapter_home_slot, adapter_per_block)
    owner = store_slots // held_adapters
    inside = store_slots % held_adapters
    picked = jnp.max(jnp.where(owner == myself, inside, -1), axis=1)
    select = (picked[:, None] == jnp.arange(held_adapters, dtype=jnp.int32)[None, :]).astype(
        jnp.bfloat16
    )
    down_map_parts = adapter_down_maps.reshape(
        held_adapters, rank_index, shard_count, feature_index
    )
    up_map_parts = adapter_up_maps.reshape(held_adapters, rank_index, shard_count, feature_index)
    send_down = jnp.einsum(
        "sl,lrtf->tsrf", select, down_map_parts, preferred_element_type=jnp.float32
    ).astype(jnp.bfloat16)
    send_up = jnp.einsum(
        "sl,lrtf->tsrf", select, up_map_parts, preferred_element_type=jnp.float32
    ).astype(jnp.bfloat16)
    recv_down, recv_up = (
        lax.all_to_all(
            sent.reshape(devices_all, rank_index, feature_index),
            ("tensor", "store"),
            split_axis=0,
            concat_axis=0,
            tiled=True,
        )
        for sent in (send_down, send_up)
    )
    owner_row = lax.dynamic_index_in_dim(owner, my_store, 0, keepdims=False)
    source_pick = (owner_row[:, None] == jnp.arange(devices_all, dtype=jnp.int32)[None, :]).astype(
        jnp.bfloat16
    )
    block_down = jnp.einsum(
        "bj,jrf->brf", source_pick, recv_down, preferred_element_type=jnp.float32
    ).astype(jnp.bfloat16)
    block_up = jnp.einsum(
        "bj,jrf->brf", source_pick, recv_up, preferred_element_type=jnp.float32
    ).astype(jnp.bfloat16)
    piece = lax.all_gather(own_rows, "tensor", axis=0, tiled=True)
    product = jnp.dot(piece, query_weight, preferred_element_type=jnp.float32)
    features = lax.dynamic_slice_in_dim(piece, my_tensor * feature_index, feature_index, 1)
    partial_value = jnp.einsum(
        "bnf,brf->bnr",
        features.reshape(blocks, BLOCK, feature_index),
        block_down,
        preferred_element_type=jnp.float32,
    )
    shrunk = lax.psum(partial_value, "tensor").astype(jnp.bfloat16)
    grown = jnp.einsum(
        "bnr,brf->bnf", shrunk, block_up, preferred_element_type=jnp.float32
    ).reshape(group_rows, feature_index)
    query = (product + 0.5 * grown).astype(jnp.bfloat16)
    return query[None]


def both_ways(pairs):
    return pairs + [(b, a) for a, b in pairs]


ACROSS = [(i, i ^ 1) for i in range(8)]
ALONG = {"x%d" % d: [(i, i ^ (2 * d)) for i in range(8)] for d in (1, 2, 3)}
HALF = BLOCK // 2
DEPTH = 1024
VMEM_LIMIT = 16 * 1024 * 1024


def send(value, pairs):
    return lax.ppermute(value, "tensor", pairs)


def swap(value, axis):
    return lax.ppermute(value, axis, [(0, 1), (1, 0)])


def settings():
    return dict(
        compiler_params=pltpu.CompilerParams(vmem_limit_bytes=VMEM_LIMIT),
        cost_estimate=pl.CostEstimate(flops=1, bytes_accessed=1, transcendentals=0),
    )


def in_vmem(count):
    return [pl.BlockSpec(memory_space=pltpu.VMEM)] * count


def pin_kernel(weight, own, swapped, out, sem):
    columns = weight.shape[1]
    copy = pltpu.make_async_copy(weight, out.at[:, pl.ds(0, columns)], sem)
    copy.start()
    for at in range(0, weight.shape[0], DEPTH):
        cut = pl.ds(at, DEPTH)
        out[cut, columns:] = jnp.concatenate([own[:, cut], swapped[:, cut]], axis=0).T
    copy.wait()


def pin_call(weight, own, swapped):
    width, columns = weight.shape
    return pl.pallas_call(
        pin_kernel,
        in_specs=[pl.BlockSpec(memory_space=pltpu.HBM)] + in_vmem(2),
        out_specs=in_vmem(1)[0],
        out_shape=pltpu.VMEM((width, columns + 2 * own.shape[0]), weight.dtype),
        scratch_shapes=[pltpu.SemaphoreType.DMA],
        name="pin",
        **settings(),
    )(pltpu.with_memory_space_constraint(weight, pltpu.HBM), own, swapped)


def rows_kernel(first, table, weights, *refs):
    *pieces, base, small = refs
    columns = base.shape[1]
    total = None
    for at in range(0, weights.shape[0], DEPTH):
        cut = pl.ds(at, DEPTH)
        x = [p[:, cut] for p in pieces]
        x = x[0] if len(x) == 1 else jnp.concatenate(x, axis=0)
        part = jnp.dot(x, weights[cut, :], preferred_element_type=jnp.float32)
        total = part if total is None else total + part
    base[...] = total[:, :columns]
    lane = lax.broadcasted_iota(jnp.int32, small.shape, 1)
    row = lax.broadcasted_iota(jnp.int32, small.shape, 0)
    use = jnp.where(
        row < HALF,
        jnp.where(lane < 64, table[0, first], table[1, first]),
        jnp.where(lane < 64, table[0, first + 1], table[1, first + 1]),
    )
    small[...] = jnp.where(use > 0, total[:, columns:], 0.0).astype(jnp.bfloat16)


def rows_call(first, table, weights, pieces):
    columns = weights.shape[1] - 128
    operands = [pltpu.with_memory_space_constraint(weights, pltpu.VMEM)] + pieces
    return pl.pallas_call(
        functools.partial(rows_kernel, first),
        in_specs=[pl.BlockSpec(memory_space=pltpu.SMEM)] + in_vmem(len(operands)),
        out_specs=in_vmem(2),
        out_shape=[
            jax.ShapeDtypeStruct((BLOCK, columns), jnp.float32),
            jax.ShapeDtypeStruct((BLOCK, 128), jnp.bfloat16),
        ],
        name="rows",
        **settings(),
    )(table, *operands)


def pack_kernel(table, up, out):
    part = out.shape[3]
    for t in range(8):
        at = pl.multiple_of((2 * t + table[2]) * part, part)
        out[t, 0] = up[0, :, pl.ds(at, part)]


def pack_call(table, up_maps):
    _, rank, width = up_maps.shape
    part = width // 16
    return pl.pallas_call(
        pack_kernel,
        grid_spec=pltpu.PrefetchScalarGridSpec(
            num_scalar_prefetch=1,
            grid=(2,),
            in_specs=[pl.BlockSpec((1, rank, width), lambda s, t: (t[s], 0, 0))],
            out_specs=pl.BlockSpec((8, 1, rank, part), lambda s, t: (0, s, 0, 0)),
        ),
        out_shape=jax.ShapeDtypeStruct((8, 2, rank, part), jnp.bfloat16),
        name="pack",
        **settings(),
    )(table, up_maps)


def take_kernel(table, got, out):
    out[...] = got[...]


def take_call(table, got):
    _, rank, part = got.shape
    return pl.pallas_call(
        take_kernel,
        grid_spec=pltpu.PrefetchScalarGridSpec(
            num_scalar_prefetch=1,
            grid=(8,),
            in_specs=[pl.BlockSpec((1, rank, part), lambda b, t: (t[b], 0, 0))],
            out_specs=pl.BlockSpec((1, rank, part), lambda b, t: (b, 0, 0)),
        ),
        out_shape=jax.ShapeDtypeStruct((8, rank, part), jnp.bfloat16),
        name="take",
        **settings(),
    )(table, got)


def finish_kernel(sources, table, *refs):
    bases = refs[: max(sources) + 1]
    shrunk, up_mine, up_other, out = refs[len(bases)], refs[len(bases) + 1], refs[len(bases) + 2], refs[-1]
    at = pl.program_id(0)
    part = up_mine.shape[2]
    both = shrunk[...].astype(jnp.float32)
    both = (both[:, :64] + both[:, 64:]).astype(jnp.bfloat16)
    group = table[8]
    for g, base in enumerate(bases):
        steps = [i for i, source in enumerate(sources) if source == g]

        @pl.when((at >= steps[0]) & (at <= steps[-1]))
        def _():
            for up, side in ((up_mine, group), (up_other, 1 - group)):
                cut = pl.ds(pl.multiple_of(side * part, part), part)
                grown = jnp.dot(both, up[0], preferred_element_type=jnp.float32)
                out[:, cut] = (base[:, cut] + 0.5 * grown).astype(out.dtype)


def finish_call(table, half, bases, shrunk, up_mine, up_other, into):
    columns = bases[0].shape[1]
    _, rank, part = up_mine.shape
    sources = [0, 1, 2, 2, 3, 3, 4, 4]

    def base_spec(g):
        if g < 2:
            return pl.BlockSpec((HALF, columns), lambda i, t: (half, 0))
        return pl.BlockSpec((HALF, columns), lambda i, t: (jnp.clip(i - 2 * g + 2, 0, 1), 0))

    up = pl.BlockSpec((1, rank, part), lambda i, t: (t[i], 0, 0))
    specs = [base_spec(g) for g in range(5)]
    specs += [pl.BlockSpec((HALF, 2 * rank), lambda i, t: (t[i], 0)), up, up]
    operands = [*bases, shrunk, up_mine, up_other]
    aliases = {}
    if into is not None:
        aliases = {1 + len(operands): 0}
        operands.append(into)
        specs.append(pl.BlockSpec(memory_space=pltpu.HBM))
    return pl.pallas_call(
        functools.partial(finish_kernel, sources),
        grid_spec=pltpu.PrefetchScalarGridSpec(
            num_scalar_prefetch=1,
            grid=(8,),
            in_specs=specs,
            out_specs=pl.BlockSpec((HALF, columns), lambda i, t: (2 * t[i] + half, 0)),
        ),
        out_shape=jax.ShapeDtypeStruct((8 * BLOCK, columns), jnp.bfloat16),
        input_output_aliases=aliases,
        name="finish",
        **settings(),
    )(table, *operands)


CUTS = {"": (0, 128), "0": (0, 64), "1": (64, 128), "1a": (64, 96), "1b": (96, 128)}
GROUPS = [
    [("own", "")],
    [("own_y", "")],
    [("x1", "0"), ("x2", "0")],
    [("x1", "1"), ("x2", "1")],
    [("x1_y", "0"), ("x2_y", "0")],
    [("x1_y", "1"), ("x2_y", "1")],
    [("x3", "0"), ("x3_y", "0")],
    [("x3", "1a"), ("x3", "1b"), ("x3_y", "1a"), ("x3_y", "1b")],
]
HALVES = [
    ("own", 0), ("own", 1), ("own_y", 0), ("own_y", 1), ("x1", 0), ("x2", 0), ("x1", 1), ("x2", 1),
    ("x1_y", 0), ("x2_y", 0), ("x1_y", 1), ("x2_y", 1), ("x3", 0), ("x3_y", 0), ("x3", 1), ("x3_y", 1),
]
EVENTS = [
    ([], [("x1", "0"), ("x2", "0")], [("own", "")], []),
    ([("x1", "0")], [("x2", "1")], [("x1", "0")], [0]),
    ([("x2", "0")], [("x1", "1")], [("x2", "0")], [2]),
    ([("own_y", "")], [], [], [1]),
    ([("x2", "1")], [("x3", "0")], [("x2", "1")], []),
    ([("x1_y", "0"), ("x2_y", "0"), ("x1", "1")], [("x3", "1a")], [("x1", "1")], [3, 4]),
    ([("x3", "0"), ("x2_y", "1")], [("x3", "1b")], [("x3", "0")], []),
    ([("x1_y", "1"), ("x3", "1a")], [], [("x3", "1a")], [5]),
    ([("x3", "1b")], [], [("x3", "1b")], []),
    ([("x3_y", "0")], [], [], [6]),
    ([("x3_y", "1a"), ("x3_y", "1b")], [], [], [7]),
]


def chain_body(
    tokens, query_weight, adapter_down_maps, adapter_up_maps, adapter_home_slot, adapter_per_block
):
    me = lax.axis_index("tensor")
    z, y = me // 2, me % 2
    store = lax.axis_index("store")
    group = lax.axis_index("groups")
    myself = me * 2 + store
    held, rank, width = adapter_down_maps.shape
    columns = query_weight.shape[1]
    rows = tokens[0]
    have = {("own", name): rows[slice(*cut)] for name, cut in CUTS.items()}
    flight = {}

    def issue(along, across):
        for name, piece in along:
            flight[name, piece] = send(have["own", piece], ALONG[name])
        for name, piece in across:
            flight[name + "_y", piece] = send(have[name, piece], ACROSS)

    issue(*EVENTS[0][1:3])

    store_slots = find_slots(adapter_home_slot, adapter_per_block)
    owner = store_slots // held
    inside = store_slots % held
    picked = jnp.max(jnp.where(owner == myself, inside, 0), axis=1)
    owner_row = lax.dynamic_index_in_dim(owner, store, 0, keepdims=False).astype(jnp.int32)
    pick_own = lax.dynamic_index_in_dim(picked, store, 0, keepdims=False)
    pick_lent = lax.dynamic_index_in_dim(picked, 1 - store, 0, keepdims=False)

    down_own = lax.dynamic_index_in_dim(adapter_down_maps, pick_own, 0, keepdims=False)
    down_lent = lax.dynamic_index_in_dim(adapter_down_maps, pick_lent, 0, keepdims=False)
    weights = pin_call(query_weight, down_own, swap(down_lent, "store"))
    up_sent = pack_call(jnp.concatenate([picked, group[None]]).astype(jnp.int32), adapter_up_maps)

    blocks = jnp.stack(
        [
            (z if name[0] == "o" else z ^ int(name[1])) * 2 + (1 - y if name.endswith("_y") else y)
            for name, _ in HALVES
        ]
    ).astype(jnp.int32)
    hit = blocks[:, None] == jnp.arange(8, dtype=jnp.int32)[None, :]
    owners = jnp.sum(jnp.where(hit, owner_row[None, :], 0), axis=1)
    table = jnp.stack([owners == myself, owners == me * 2 + 1 - store]).astype(jnp.int32)

    bases = [None] * 8
    shrunk = [jnp.zeros((8, HALF, 2 * rank), jnp.bfloat16) for _ in range(2)]
    extra = {"up": up_sent}
    for at, (waits, along, across, groups) in enumerate(EVENTS[1:], 1):
        got = {key: flight.pop(key) for key in waits}
        if at >= len(EVENTS) - 2:
            extra.update(flight.pop("late"))
        got, have, bases, shrunk, extra = lax.optimization_barrier(
            (got, have, bases, shrunk, extra)
        )
        have.update({key: got[key] for key in waits})
        issue(along, across)
        if at == 6:
            sent = extra.pop("up").reshape(16, rank, -1)
            flight["late"] = {
                "up": lax.all_to_all(
                    sent, ("tensor", "store"), split_axis=0, concat_axis=0, tiled=True
                )
            }
        for g in groups:
            base, small = rows_call(2 * g, table, weights, [have[key] for key in GROUPS[g]])
            bases[g] = base
            for i in range(2):
                half = HALVES[2 * g + i][1]
                shrunk[half] = lax.dynamic_update_slice(
                    shrunk[half], small[None, i * HALF : (i + 1) * HALF], (blocks[2 * g + i], 0, 0)
                )
        if at == len(EVENTS) - 2:
            flight["late"] = {"first": send(shrunk[0], ACROSS)}

    up_mine = take_call(owner_row, extra["up"])
    up_other = swap(up_mine, "groups")

    def total(value):
        arrived = [send(value, pairs) for pairs in ALONG.values()]
        return (value + arrived[0] + arrived[1] + arrived[2]).reshape(8 * HALF, 2 * rank)

    first = total(shrunk[0] + extra["first"])
    second = total(shrunk[1] + send(shrunk[1], ACROSS))
    query = None
    for half, value in enumerate((first, second)):
        chosen = [0, 1] + [g for g in range(2, 8) if HALVES[2 * g][1] == half]
        places = [2 * g + half for g in (0, 1)] + [2 * g + i for g in chosen[2:] for i in range(2)]
        order = jnp.concatenate([blocks[np.array(places)], group[None]]).astype(jnp.int32)
        query = finish_call(
            order, half, [bases[g] for g in chosen], value, up_mine, up_other, query
        )
    return query[None]


def body(tokens, *rest):
    sizes = tuple(lax.axis_size(name) for name in ("groups", "tensor", "store"))
    fits = sizes == (2, 8, 2) and tokens.shape[1] == BLOCK
    return (chain_body if fits else general_body)(tokens, *rest)


def solution(mesh):
    placed = (
        P(("groups", "store"), "tensor", None),
        P(None, "tensor"),
        P(("tensor", "store"), None, None),
        P(("tensor", "store"), None, None),
        P(),
        P(),
    )
    return jax.shard_map(
        body,
        mesh=mesh,
        in_specs=placed,
        out_specs=P(("groups", "store"), None, "tensor"),
        check_vma=False,
    )
```

```python
import functools

import jax
import jax.numpy as jnp
from jax import lax
from jax.experimental import pallas as pl
from jax.experimental.pallas import tpu as pltpu
from jax.sharding import PartitionSpec as P

BLOCK = 128


def find_slots(adapter_home_slot, adapter_per_block):
    catalog = jnp.arange(adapter_home_slot.shape[0], dtype=jnp.int32)
    return jnp.sum(
        jnp.where(
            adapter_per_block[:, :, None] == catalog[None, None, :],
            adapter_home_slot[None, None, :],
            0,
        ),
        axis=2,
    )


def general_body(
    tokens, query_weight, adapter_down_maps, adapter_up_maps, adapter_home_slot, adapter_per_block
):
    shard_count = lax.axis_size("tensor")
    store_count = lax.axis_size("store")
    devices_all = shard_count * store_count
    my_tensor = lax.axis_index("tensor")
    my_store = lax.axis_index("store")
    myself = lax.axis_index(("tensor", "store"))
    held_adapters, rank_index, feature_width = adapter_down_maps.shape
    feature_index = query_weight.shape[1]
    own_rows = tokens[0]
    group_rows = own_rows.shape[0] * shard_count
    blocks = group_rows // BLOCK
    store_slots = find_slots(adapter_home_slot, adapter_per_block)
    owner = store_slots // held_adapters
    inside = store_slots % held_adapters
    picked = jnp.max(jnp.where(owner == myself, inside, -1), axis=1)
    select = (picked[:, None] == jnp.arange(held_adapters, dtype=jnp.int32)[None, :]).astype(
        jnp.bfloat16
    )
    down_map_parts = adapter_down_maps.reshape(
        held_adapters, rank_index, shard_count, feature_index
    )
    up_map_parts = adapter_up_maps.reshape(held_adapters, rank_index, shard_count, feature_index)
    send_down = jnp.einsum(
        "sl,lrtf->tsrf", select, down_map_parts, preferred_element_type=jnp.float32
    ).astype(jnp.bfloat16)
    send_up = jnp.einsum(
        "sl,lrtf->tsrf", select, up_map_parts, preferred_element_type=jnp.float32
    ).astype(jnp.bfloat16)
    recv_down, recv_up = (
        lax.all_to_all(
            sent.reshape(devices_all, rank_index, feature_index),
            ("tensor", "store"),
            split_axis=0,
            concat_axis=0,
            tiled=True,
        )
        for sent in (send_down, send_up)
    )
    owner_row = lax.dynamic_index_in_dim(owner, my_store, 0, keepdims=False)
    source_pick = (owner_row[:, None] == jnp.arange(devices_all, dtype=jnp.int32)[None, :]).astype(
        jnp.bfloat16
    )
    block_down = jnp.einsum(
        "bj,jrf->brf", source_pick, recv_down, preferred_element_type=jnp.float32
    ).astype(jnp.bfloat16)
    block_up = jnp.einsum(
        "bj,jrf->brf", source_pick, recv_up, preferred_element_type=jnp.float32
    ).astype(jnp.bfloat16)
    piece = lax.all_gather(own_rows, "tensor", axis=0, tiled=True)
    product = jnp.dot(piece, query_weight, preferred_element_type=jnp.float32)
    features = lax.dynamic_slice_in_dim(piece, my_tensor * feature_index, feature_index, 1)
    partial_value = jnp.einsum(
        "bnf,brf->bnr",
        features.reshape(blocks, BLOCK, feature_index),
        block_down,
        preferred_element_type=jnp.float32,
    )
    shrunk = lax.psum(partial_value, "tensor").astype(jnp.bfloat16)
    grown = jnp.einsum(
        "bnr,brf->bnf", shrunk, block_up, preferred_element_type=jnp.float32
    ).reshape(group_rows, feature_index)
    query = (product + 0.5 * grown).astype(jnp.bfloat16)
    return query[None]


def both_ways(pairs):
    return pairs + [(b, a) for a, b in pairs]


RING = [0, 2, 4, 6, 7, 5, 3, 1]
AHEAD = [(RING[i], RING[(i + 1) % 8]) for i in range(8)]
BACK = [(b, a) for a, b in AHEAD]
ACROSS = [(i, i ^ 1) for i in range(8)]
ALONG = [[(i, i ^ (2 * d)) for i in range(8)] for d in (1, 2, 3)]
HALF = BLOCK // 2
DEPTH = 1024
VMEM_LIMIT = 16 * 1024 * 1024


def send(value, pairs):
    return lax.ppermute(value, "tensor", pairs)


def swap(value, axis):
    return lax.ppermute(value, axis, [(0, 1), (1, 0)])


def settings():
    return dict(
        compiler_params=pltpu.CompilerParams(vmem_limit_bytes=VMEM_LIMIT),
        cost_estimate=pl.CostEstimate(flops=1, bytes_accessed=1, transcendentals=0),
    )


def in_vmem(count):
    return [pl.BlockSpec(memory_space=pltpu.VMEM)] * count


def pin_kernel(weight, own, swapped, out, sem):
    columns = weight.shape[1]
    copy = pltpu.make_async_copy(weight, out.at[:, pl.ds(0, columns)], sem)
    copy.start()
    for at in range(0, weight.shape[0], DEPTH):
        cut = pl.ds(at, DEPTH)
        out[cut, columns:] = jnp.concatenate([own[:, cut], swapped[:, cut]], axis=0).T
    copy.wait()


def pin_call(weight, own, swapped):
    width, columns = weight.shape
    return pl.pallas_call(
        pin_kernel,
        in_specs=[pl.BlockSpec(memory_space=pltpu.HBM)] + in_vmem(2),
        out_specs=in_vmem(1)[0],
        out_shape=pltpu.VMEM((width, columns + 2 * own.shape[0]), weight.dtype),
        scratch_shapes=[pltpu.SemaphoreType.DMA],
        name="pin",
        **settings(),
    )(weight, own, swapped)


def rows_kernel(group, table, weights, *refs):
    *pieces, shrunk, base, shrunk_out = refs
    columns = base.shape[1]
    total = None
    for at in range(0, weights.shape[0], DEPTH):
        cut = pl.ds(at, DEPTH)
        x = [p[:, cut] for p in pieces]
        x = x[0] if len(x) == 1 else jnp.concatenate(x, axis=0)
        part = jnp.dot(x, weights[cut, :], preferred_element_type=jnp.float32)
        total = part if total is None else total + part
    base[...] = total[:, :columns]
    lane = lax.broadcasted_iota(jnp.int32, shrunk.shape, 1)
    row = lax.broadcasted_iota(jnp.int32, shrunk.shape, 0)
    use = jnp.where(
        row < HALF,
        jnp.where(lane < 64, table[0, 2 * group], table[1, 2 * group]),
        jnp.where(lane < 64, table[0, 2 * group + 1], table[1, 2 * group + 1]),
    )
    small = total[:, columns:].astype(jnp.bfloat16).astype(jnp.float32)
    old = shrunk[...].astype(jnp.float32)
    shrunk_out[...] = jnp.where(use > 0, small, old).astype(jnp.bfloat16)


def rows_call(group, table, weights, pieces, shrunk):
    columns = weights.shape[1] - 128
    operands = [pltpu.with_memory_space_constraint(weights, pltpu.VMEM)] + pieces + [shrunk]
    return pl.pallas_call(
        functools.partial(rows_kernel, group),
        in_specs=[pl.BlockSpec(memory_space=pltpu.SMEM)] + in_vmem(len(operands)),
        out_specs=in_vmem(2),
        out_shape=[
            jax.ShapeDtypeStruct((BLOCK, columns), jnp.float32),
            jax.ShapeDtypeStruct((BLOCK, 128), jnp.bfloat16),
        ],
        name="rows",
        **settings(),
    )(table, *operands)


def pack_kernel(table, up, out):
    part = out.shape[3]
    for t in range(8):
        at = pl.multiple_of((2 * t + table[2]) * part, part)
        out[t, 0] = up[0, :, pl.ds(at, part)]


def pack_call(table, up_maps):
    _, rank, width = up_maps.shape
    part = width // 16
    return pl.pallas_call(
        pack_kernel,
        grid_spec=pltpu.PrefetchScalarGridSpec(
            num_scalar_prefetch=1,
            grid=(2,),
            in_specs=[pl.BlockSpec((1, rank, width), lambda s, t: (t[s], 0, 0))],
            out_specs=pl.BlockSpec((8, 1, rank, part), lambda s, t: (0, s, 0, 0)),
        ),
        out_shape=jax.ShapeDtypeStruct((8, 2, rank, part), jnp.bfloat16),
        name="pack",
        **settings(),
    )(table, pltpu.with_memory_space_constraint(up_maps, pltpu.HBM))


def take_kernel(table, got, out):
    out[...] = got[...]


def take_call(table, got):
    _, rank, part = got.shape
    return pl.pallas_call(
        take_kernel,
        grid_spec=pltpu.PrefetchScalarGridSpec(
            num_scalar_prefetch=1,
            grid=(8,),
            in_specs=[pl.BlockSpec((1, rank, part), lambda b, t: (t[b], 0, 0))],
            out_specs=pl.BlockSpec((1, rank, part), lambda b, t: (b, 0, 0)),
        ),
        out_shape=jax.ShapeDtypeStruct((8, rank, part), jnp.bfloat16),
        name="take",
        **settings(),
    )(table, got)


def finish_kernel(table, *refs):
    *bases, shrunk, up_mine, up_other, out = refs
    at = pl.program_id(0)
    part = up_mine.shape[2]
    both = shrunk[0].astype(jnp.float32)
    value = jnp.where(table[2, at] > 0, both[:, 64:], both[:, :64]).astype(jnp.bfloat16)
    group = table[3, at]
    for g, base in enumerate(bases):

        @pl.when(at // 2 == g)
        def _():
            for up, side in ((up_mine, group), (up_other, 1 - group)):
                cut = pl.ds(pl.multiple_of(side * part, part), part)
                grown = jnp.dot(value, up[0], preferred_element_type=jnp.float32)
                out[:, cut] = (base[:, cut] + 0.5 * grown).astype(out.dtype)


def finish_call(table, bases, shrunk, up_mine, up_other):
    columns = bases[0].shape[1]
    _, rank, part = up_mine.shape

    def base_spec(g):
        return pl.BlockSpec((HALF, columns), lambda i, t: (jnp.clip(i - 2 * g, 0, 1), 0))

    up = pl.BlockSpec((1, rank, part), lambda i, t: (t[0, i], 0, 0))
    return pl.pallas_call(
        finish_kernel,
        grid_spec=pltpu.PrefetchScalarGridSpec(
            num_scalar_prefetch=1,
            grid=(16,),
            in_specs=[base_spec(g) for g in range(8)]
            + [pl.BlockSpec((1, HALF, 2 * rank), lambda i, t: (t[1, i], i % 2, 0)), up, up],
            out_specs=pl.BlockSpec((HALF, columns), lambda i, t: (2 * t[0, i] + i % 2, 0)),
        ),
        out_shape=jax.ShapeDtypeStruct((8 * BLOCK, columns), jnp.bfloat16),
        name="finish",
        **settings(),
    )(table, *bases, shrunk, up_mine, up_other)


def chain_body(
    tokens, query_weight, adapter_down_maps, adapter_up_maps, adapter_home_slot, adapter_per_block
):
    me = lax.axis_index("tensor")
    z, y = me // 2, me % 2
    store = lax.axis_index("store")
    group = lax.axis_index("groups")
    myself = me * 2 + store
    held, rank, width = adapter_down_maps.shape
    rows = tokens[0]
    halves = [rows[:HALF], rows[HALF:]]

    ahead, back = list(halves), list(halves[::-1])
    flight = [(send(ahead[k], AHEAD), send(back[k], BACK)) for k in range(2)]

    store_slots = find_slots(adapter_home_slot, adapter_per_block)
    owner = store_slots // held
    inside = store_slots % held
    picked = jnp.max(jnp.where(owner == myself, inside, 0), axis=1)
    owner_row = lax.dynamic_index_in_dim(owner, store, 0, keepdims=False).astype(jnp.int32)
    pick_own = lax.dynamic_index_in_dim(picked, store, 0, keepdims=False)
    pick_lent = lax.dynamic_index_in_dim(picked, 1 - store, 0, keepdims=False)

    down_own = lax.dynamic_index_in_dim(adapter_down_maps, pick_own, 0, keepdims=False)
    down_lent = lax.dynamic_index_in_dim(adapter_down_maps, pick_lent, 0, keepdims=False)
    weights = pin_call(query_weight, down_own, swap(down_lent, "store"))
    up_sent = pack_call(jnp.concatenate([picked, group[None]]).astype(jnp.int32), adapter_up_maps)

    position = jnp.where(y == 0, z, 7 - z)
    places = []
    for k in range(8):
        step = (k + 1) // 2
        places += [position - step, position + step] if k % 2 else [position + step, position - step]
    places = jnp.stack(places) % 8
    blocks = jnp.where(places < 4, 2 * places, 15 - 2 * places).astype(jnp.int32)
    hit = blocks[:, None] == jnp.arange(8, dtype=jnp.int32)[None, :]
    owners = jnp.sum(jnp.where(hit, owner_row[None, :], 0), axis=1)
    table = jnp.stack([owners == myself, owners == me * 2 + 1 - store]).astype(jnp.int32)

    bases = []
    shrunk = jnp.zeros((BLOCK, 2 * rank), jnp.bfloat16)
    pieces = [rows]
    extra = {"up": up_sent}
    for k in range(7):
        base, shrunk = rows_call(k, table, weights, pieces, shrunk)
        bases.append(base)
        if k == 6:
            extra["up"] = up_got
        (got_ahead, got_back), ahead, back, bases, shrunk, extra = lax.optimization_barrier(
            (flight[k], ahead, back, bases, shrunk, extra)
        )
        ahead.append(got_ahead)
        back.append(got_back)
        if k < 5:
            flight.append((send(ahead[k + 2], AHEAD), send(back[k + 2], BACK)))
        if k == 4:
            up_got = lax.all_to_all(
                extra["up"].reshape(16, rank, -1),
                ("tensor", "store"),
                split_axis=0,
                concat_axis=0,
                tiled=True,
            )
        pieces = [got_ahead, got_back] if k % 2 == 0 else [got_back, got_ahead]
    base, shrunk = rows_call(7, table, weights, pieces, shrunk)
    bases.append(base)

    up_mine = take_call(owner_row, extra["up"])
    up_other = swap(up_mine, "groups")
    pair = jnp.stack([shrunk, send(shrunk, ACROSS)])
    everyone = jnp.concatenate([pair] + [send(pair, pairs) for pairs in ALONG])
    home, core = owners // 2, owners % 2
    where = 2 * ((home // 2) ^ z) + ((home % 2) ^ y)
    table = jnp.stack([blocks, where, core != store, jnp.broadcast_to(group, (16,))])
    return finish_call(table.astype(jnp.int32), bases, everyone, up_mine, up_other)[None]


def body(tokens, *rest):
    sizes = tuple(lax.axis_size(name) for name in ("groups", "tensor", "store"))
    fits = sizes == (2, 8, 2) and tokens.shape[1] == BLOCK
    return (chain_body if fits else general_body)(tokens, *rest)


def solution(mesh):
    placed = (
        P(("groups", "store"), "tensor", None),
        P(None, "tensor"),
        P(("tensor", "store"), None, None),
        P(("tensor", "store"), None, None),
        P(),
        P(),
    )
    return jax.shard_map(
        body,
        mesh=mesh,
        in_specs=placed,
        out_specs=P(("groups", "store"), None, "tensor"),
        check_vma=False,
    )
```

```python
import functools

import jax
import jax.numpy as jnp
from jax import lax
from jax.experimental import pallas as pl
from jax.experimental.pallas import tpu as pltpu
from jax.sharding import PartitionSpec as P

BLOCK = 128


def find_slots(adapter_home_slot, adapter_per_block):
    catalog = jnp.arange(adapter_home_slot.shape[0], dtype=jnp.int32)
    return jnp.sum(
        jnp.where(
            adapter_per_block[:, :, None] == catalog[None, None, :],
            adapter_home_slot[None, None, :],
            0,
        ),
        axis=2,
    )


def general_body(
    tokens, query_weight, adapter_down_maps, adapter_up_maps, adapter_home_slot, adapter_per_block
):
    shard_count = lax.axis_size("tensor")
    store_count = lax.axis_size("store")
    devices_all = shard_count * store_count
    my_tensor = lax.axis_index("tensor")
    my_store = lax.axis_index("store")
    myself = lax.axis_index(("tensor", "store"))
    held_adapters, rank_index, feature_width = adapter_down_maps.shape
    feature_index = query_weight.shape[1]
    own_rows = tokens[0]
    group_rows = own_rows.shape[0] * shard_count
    blocks = group_rows // BLOCK
    store_slots = find_slots(adapter_home_slot, adapter_per_block)
    owner = store_slots // held_adapters
    inside = store_slots % held_adapters
    picked = jnp.max(jnp.where(owner == myself, inside, -1), axis=1)
    select = (picked[:, None] == jnp.arange(held_adapters, dtype=jnp.int32)[None, :]).astype(
        jnp.bfloat16
    )
    down_map_parts = adapter_down_maps.reshape(
        held_adapters, rank_index, shard_count, feature_index
    )
    up_map_parts = adapter_up_maps.reshape(held_adapters, rank_index, shard_count, feature_index)
    send_down = jnp.einsum(
        "sl,lrtf->tsrf", select, down_map_parts, preferred_element_type=jnp.float32
    ).astype(jnp.bfloat16)
    send_up = jnp.einsum(
        "sl,lrtf->tsrf", select, up_map_parts, preferred_element_type=jnp.float32
    ).astype(jnp.bfloat16)
    recv_down, recv_up = (
        lax.all_to_all(
            sent.reshape(devices_all, rank_index, feature_index),
            ("tensor", "store"),
            split_axis=0,
            concat_axis=0,
            tiled=True,
        )
        for sent in (send_down, send_up)
    )
    owner_row = lax.dynamic_index_in_dim(owner, my_store, 0, keepdims=False)
    source_pick = (owner_row[:, None] == jnp.arange(devices_all, dtype=jnp.int32)[None, :]).astype(
        jnp.bfloat16
    )
    block_down = jnp.einsum(
        "bj,jrf->brf", source_pick, recv_down, preferred_element_type=jnp.float32
    ).astype(jnp.bfloat16)
    block_up = jnp.einsum(
        "bj,jrf->brf", source_pick, recv_up, preferred_element_type=jnp.float32
    ).astype(jnp.bfloat16)
    piece = lax.all_gather(own_rows, "tensor", axis=0, tiled=True)
    product = jnp.dot(piece, query_weight, preferred_element_type=jnp.float32)
    features = lax.dynamic_slice_in_dim(piece, my_tensor * feature_index, feature_index, 1)
    partial_value = jnp.einsum(
        "bnf,brf->bnr",
        features.reshape(blocks, BLOCK, feature_index),
        block_down,
        preferred_element_type=jnp.float32,
    )
    shrunk = lax.psum(partial_value, "tensor").astype(jnp.bfloat16)
    grown = jnp.einsum(
        "bnr,brf->bnf", shrunk, block_up, preferred_element_type=jnp.float32
    ).reshape(group_rows, feature_index)
    query = (product + 0.5 * grown).astype(jnp.bfloat16)
    return query[None]


def both_ways(pairs):
    return pairs + [(b, a) for a, b in pairs]


RING = [0, 2, 4, 6, 7, 5, 3, 1]
AHEAD = [(RING[i], RING[(i + 1) % 8]) for i in range(8)]
BACK = [(b, a) for a, b in AHEAD]
ACROSS = [(i, i ^ 1) for i in range(8)]
ALONG = [[(i, i ^ (2 * d)) for i in range(8)] for d in (1, 2, 3)]
HALF = BLOCK // 2
DEPTH = 1024
VMEM_LIMIT = 16 * 1024 * 1024


def send(value, pairs):
    return lax.ppermute(value, "tensor", pairs)


def swap(value, axis):
    return lax.ppermute(value, axis, [(0, 1), (1, 0)])


def settings():
    return dict(
        compiler_params=pltpu.CompilerParams(vmem_limit_bytes=VMEM_LIMIT),
        cost_estimate=pl.CostEstimate(flops=1, bytes_accessed=1, transcendentals=0),
    )


def in_vmem(count):
    return [pl.BlockSpec(memory_space=pltpu.VMEM)] * count


def pin_kernel(weight, own, swapped, out, sem):
    columns = weight.shape[1]
    copy = pltpu.make_async_copy(weight, out.at[:, pl.ds(0, columns)], sem)
    copy.start()
    for at in range(0, weight.shape[0], DEPTH):
        cut = pl.ds(at, DEPTH)
        out[cut, columns:] = jnp.concatenate([own[:, cut], swapped[:, cut]], axis=0).T
    copy.wait()


def pin_call(weight, own, swapped):
    width, columns = weight.shape
    return pl.pallas_call(
        pin_kernel,
        in_specs=[pl.BlockSpec(memory_space=pltpu.HBM)] + in_vmem(2),
        out_specs=in_vmem(1)[0],
        out_shape=pltpu.VMEM((width, columns + 2 * own.shape[0]), weight.dtype),
        scratch_shapes=[pltpu.SemaphoreType.DMA],
        name="pin",
        **settings(),
    )(weight, own, swapped)


def rows_kernel(group, table, weights, *refs):
    *pieces, shrunk, base, shrunk_out = refs
    columns = base.shape[1]
    total = None
    for at in range(0, weights.shape[0], DEPTH):
        cut = pl.ds(at, DEPTH)
        x = [p[:, cut] for p in pieces]
        x = x[0] if len(x) == 1 else jnp.concatenate(x, axis=0)
        part = jnp.dot(x, weights[cut, :], preferred_element_type=jnp.float32)
        total = part if total is None else total + part
    base[...] = total[:, :columns]
    lane = lax.broadcasted_iota(jnp.int32, shrunk.shape, 1)
    row = lax.broadcasted_iota(jnp.int32, shrunk.shape, 0)
    use = jnp.where(
        row < HALF,
        jnp.where(lane < 64, table[0, 2 * group], table[1, 2 * group]),
        jnp.where(lane < 64, table[0, 2 * group + 1], table[1, 2 * group + 1]),
    )
    small = total[:, columns:].astype(jnp.bfloat16).astype(jnp.float32)
    old = shrunk[...].astype(jnp.float32)
    shrunk_out[...] = jnp.where(use > 0, small, old).astype(jnp.bfloat16)


def rows_call(group, table, weights, pieces, shrunk):
    columns = weights.shape[1] - 128
    operands = [pltpu.with_memory_space_constraint(weights, pltpu.VMEM)] + pieces + [shrunk]
    return pl.pallas_call(
        functools.partial(rows_kernel, group),
        in_specs=[pl.BlockSpec(memory_space=pltpu.SMEM)] + in_vmem(len(operands)),
        out_specs=in_vmem(2),
        out_shape=[
            jax.ShapeDtypeStruct((BLOCK, columns), jnp.float32),
            jax.ShapeDtypeStruct((BLOCK, 128), jnp.bfloat16),
        ],
        name="rows",
        **settings(),
    )(table, *operands)


def pack_kernel(table, up, out):
    part = out.shape[3]
    for t in range(8):
        at = pl.multiple_of((2 * t + table[2]) * part, part)
        out[t, 0] = up[0, :, pl.ds(at, part)]


def pack_call(table, up_maps):
    _, rank, width = up_maps.shape
    part = width // 16
    return pl.pallas_call(
        pack_kernel,
        grid_spec=pltpu.PrefetchScalarGridSpec(
            num_scalar_prefetch=1,
            grid=(2,),
            in_specs=[pl.BlockSpec((1, rank, width), lambda s, t: (t[s], 0, 0))],
            out_specs=pl.BlockSpec((8, 1, rank, part), lambda s, t: (0, s, 0, 0)),
        ),
        out_shape=jax.ShapeDtypeStruct((8, 2, rank, part), jnp.bfloat16),
        name="pack",
        **settings(),
    )(table, pltpu.with_memory_space_constraint(up_maps, pltpu.HBM))


def take_kernel(table, got, out):
    out[...] = got[...]


def take_call(table, got):
    _, rank, part = got.shape
    return pl.pallas_call(
        take_kernel,
        grid_spec=pltpu.PrefetchScalarGridSpec(
            num_scalar_prefetch=1,
            grid=(8,),
            in_specs=[pl.BlockSpec((1, rank, part), lambda b, t: (t[b], 0, 0))],
            out_specs=pl.BlockSpec((1, rank, part), lambda b, t: (b, 0, 0)),
        ),
        out_shape=jax.ShapeDtypeStruct((8, rank, part), jnp.bfloat16),
        name="take",
        **settings(),
    )(table, got)


def finish_kernel(table, *refs):
    *bases, shrunk, up_mine, up_other, out, rows, sems = refs
    part = up_mine.shape[2]
    group = table[3, 0]
    copies = []
    for i in range(16):
        block, half = table[0, i], i % 2
        own = pl.ds(half * HALF, HALF)
        both = shrunk[table[1, i], own, :].astype(jnp.float32)
        value = jnp.where(table[2, i] > 0, both[:, 64:], both[:, :64]).astype(jnp.bfloat16)
        for up, side in ((up_mine, group), (up_other, 1 - group)):
            cut = pl.ds(pl.multiple_of(side * part, part), part)
            grown = jnp.dot(value, up[block], preferred_element_type=jnp.float32)
            rows[i, :, cut] = (bases[i // 2][own, cut] + 0.5 * grown).astype(rows.dtype)
        to = pl.ds(pl.multiple_of((2 * block + half) * HALF, HALF), HALF)
        copies.append(pltpu.make_async_copy(rows.at[i], out.at[to], sems.at[i]))
        copies[-1].start()
    for copy in copies:
        copy.wait()


def finish_call(table, bases, shrunk, up_mine, up_other):
    columns = bases[0].shape[1]
    return pl.pallas_call(
        finish_kernel,
        in_specs=[pl.BlockSpec(memory_space=pltpu.SMEM)] + in_vmem(11),
        out_specs=pl.BlockSpec(memory_space=pltpu.HBM),
        out_shape=jax.ShapeDtypeStruct((8 * BLOCK, columns), jnp.bfloat16),
        scratch_shapes=[
            pltpu.VMEM((16, HALF, columns), jnp.bfloat16),
            pltpu.SemaphoreType.DMA((16,)),
        ],
        name="finish",
        **settings(),
    )(table, *bases, shrunk, up_mine, up_other)


def chain_body(
    tokens, query_weight, adapter_down_maps, adapter_up_maps, adapter_home_slot, adapter_per_block
):
    me = lax.axis_index("tensor")
    z, y = me // 2, me % 2
    store = lax.axis_index("store")
    group = lax.axis_index("groups")
    myself = me * 2 + store
    held, rank, width = adapter_down_maps.shape
    rows = tokens[0]
    halves = [rows[:HALF], rows[HALF:]]

    ahead, back = list(halves), list(halves[::-1])
    flight = [(send(ahead[k], AHEAD), send(back[k], BACK)) for k in range(2)]
    got, ahead, back, adapter_home_slot, adapter_per_block = lax.optimization_barrier(
        (flight[0], ahead, back, adapter_home_slot, adapter_per_block)
    )
    ahead.append(got[0])
    back.append(got[1])
    flight.append((send(ahead[2], AHEAD), send(back[2], BACK)))

    store_slots = find_slots(adapter_home_slot, adapter_per_block)
    owner = store_slots // held
    inside = store_slots % held
    picked = jnp.max(jnp.where(owner == myself, inside, 0), axis=1)
    owner_row = lax.dynamic_index_in_dim(owner, store, 0, keepdims=False).astype(jnp.int32)
    pick_own = lax.dynamic_index_in_dim(picked, store, 0, keepdims=False)
    pick_lent = lax.dynamic_index_in_dim(picked, 1 - store, 0, keepdims=False)

    down_own = lax.dynamic_index_in_dim(adapter_down_maps, pick_own, 0, keepdims=False)
    down_lent = lax.dynamic_index_in_dim(adapter_down_maps, pick_lent, 0, keepdims=False)
    down_swapped = swap(down_lent, "store")
    weights = pin_call(query_weight, down_own, down_swapped)
    up_sent = pack_call(jnp.concatenate([picked, group[None]]).astype(jnp.int32), adapter_up_maps)

    position = jnp.where(y == 0, z, 7 - z)
    places = []
    for k in range(8):
        step = (k + 1) // 2
        places += [position - step, position + step] if k % 2 else [position + step, position - step]
    places = jnp.stack(places) % 8
    blocks = jnp.where(places < 4, 2 * places, 15 - 2 * places).astype(jnp.int32)
    hit = blocks[:, None] == jnp.arange(8, dtype=jnp.int32)[None, :]
    owners = jnp.sum(jnp.where(hit, owner_row[None, :], 0), axis=1)
    table = jnp.stack([owners == myself, owners == me * 2 + 1 - store]).astype(jnp.int32)

    bases = []
    shrunk = jnp.zeros((BLOCK, 2 * rank), jnp.bfloat16)
    groups = [[rows], [ahead[2], back[2]]]
    for k in range(1, 7):
        (got_ahead, got_back), ahead, back, bases, shrunk, up_sent = lax.optimization_barrier(
            (flight[k], ahead, back, bases, shrunk, up_sent)
        )
        ahead.append(got_ahead)
        back.append(got_back)
        if k < 5:
            flight.append((send(ahead[k + 2], AHEAD), send(back[k + 2], BACK)))
        groups.append([got_ahead, got_back] if k % 2 == 0 else [got_back, got_ahead])
        for g in range(len(bases), min(len(bases) + 2, k + 2)):
            base, shrunk = rows_call(g, table, weights, groups[g], shrunk)
            bases.append(base)
    shrunk, up_sent = lax.optimization_barrier((shrunk, up_sent))
    up_got = lax.all_to_all(
        up_sent.reshape(16, rank, -1), ("tensor", "store"), split_axis=0, concat_axis=0, tiled=True
    )

    up_mine = take_call(owner_row, up_got)
    up_other = swap(up_mine, "groups")
    pair = jnp.stack([shrunk, send(shrunk, ACROSS)])
    everyone = jnp.concatenate([pair] + [send(pair, pairs) for pairs in ALONG])
    home, core = owners // 2, owners % 2
    where = 2 * ((home // 2) ^ z) + ((home % 2) ^ y)
    table = jnp.stack([blocks, where, core != store, jnp.broadcast_to(group, (16,))])
    return finish_call(table.astype(jnp.int32), bases, everyone, up_mine, up_other)[None]


def body(tokens, *rest):
    sizes = tuple(lax.axis_size(name) for name in ("groups", "tensor", "store"))
    fits = sizes == (2, 8, 2) and tokens.shape[1] == BLOCK
    return (chain_body if fits else general_body)(tokens, *rest)


def solution(mesh):
    placed = (
        P(("groups", "store"), "tensor", None),
        P(None, "tensor"),
        P(("tensor", "store"), None, None),
        P(("tensor", "store"), None, None),
        P(),
        P(),
    )
    return jax.shard_map(
        body,
        mesh=mesh,
        in_specs=placed,
        out_specs=P(("groups", "store"), None, "tensor"),
        check_vma=False,
    )
```

```python
import functools

import jax
import jax.numpy as jnp
from jax import lax
from jax.experimental import pallas as pl
from jax.experimental.pallas import tpu as pltpu
from jax.sharding import PartitionSpec as P

BLOCK = 128


def find_slots(adapter_home_slot, adapter_per_block):
    catalog = jnp.arange(adapter_home_slot.shape[0], dtype=jnp.int32)
    return jnp.sum(
        jnp.where(
            adapter_per_block[:, :, None] == catalog[None, None, :],
            adapter_home_slot[None, None, :],
            0,
        ),
        axis=2,
    )


def general_body(
    tokens, query_weight, adapter_down_maps, adapter_up_maps, adapter_home_slot, adapter_per_block
):
    shard_count = lax.axis_size("tensor")
    store_count = lax.axis_size("store")
    devices_all = shard_count * store_count
    my_tensor = lax.axis_index("tensor")
    my_store = lax.axis_index("store")
    myself = lax.axis_index(("tensor", "store"))
    held_adapters, rank_index, feature_width = adapter_down_maps.shape
    feature_index = query_weight.shape[1]
    own_rows = tokens[0]
    group_rows = own_rows.shape[0] * shard_count
    blocks = group_rows // BLOCK
    store_slots = find_slots(adapter_home_slot, adapter_per_block)
    owner = store_slots // held_adapters
    inside = store_slots % held_adapters
    picked = jnp.max(jnp.where(owner == myself, inside, -1), axis=1)
    select = (picked[:, None] == jnp.arange(held_adapters, dtype=jnp.int32)[None, :]).astype(
        jnp.bfloat16
    )
    down_map_parts = adapter_down_maps.reshape(
        held_adapters, rank_index, shard_count, feature_index
    )
    up_map_parts = adapter_up_maps.reshape(held_adapters, rank_index, shard_count, feature_index)
    send_down = jnp.einsum(
        "sl,lrtf->tsrf", select, down_map_parts, preferred_element_type=jnp.float32
    ).astype(jnp.bfloat16)
    send_up = jnp.einsum(
        "sl,lrtf->tsrf", select, up_map_parts, preferred_element_type=jnp.float32
    ).astype(jnp.bfloat16)
    recv_down, recv_up = (
        lax.all_to_all(
            sent.reshape(devices_all, rank_index, feature_index),
            ("tensor", "store"),
            split_axis=0,
            concat_axis=0,
            tiled=True,
        )
        for sent in (send_down, send_up)
    )
    owner_row = lax.dynamic_index_in_dim(owner, my_store, 0, keepdims=False)
    source_pick = (owner_row[:, None] == jnp.arange(devices_all, dtype=jnp.int32)[None, :]).astype(
        jnp.bfloat16
    )
    block_down = jnp.einsum(
        "bj,jrf->brf", source_pick, recv_down, preferred_element_type=jnp.float32
    ).astype(jnp.bfloat16)
    block_up = jnp.einsum(
        "bj,jrf->brf", source_pick, recv_up, preferred_element_type=jnp.float32
    ).astype(jnp.bfloat16)
    piece = lax.all_gather(own_rows, "tensor", axis=0, tiled=True)
    product = jnp.dot(piece, query_weight, preferred_element_type=jnp.float32)
    features = lax.dynamic_slice_in_dim(piece, my_tensor * feature_index, feature_index, 1)
    partial_value = jnp.einsum(
        "bnf,brf->bnr",
        features.reshape(blocks, BLOCK, feature_index),
        block_down,
        preferred_element_type=jnp.float32,
    )
    shrunk = lax.psum(partial_value, "tensor").astype(jnp.bfloat16)
    grown = jnp.einsum(
        "bnr,brf->bnf", shrunk, block_up, preferred_element_type=jnp.float32
    ).reshape(group_rows, feature_index)
    query = (product + 0.5 * grown).astype(jnp.bfloat16)
    return query[None]


def both_ways(pairs):
    return pairs + [(b, a) for a, b in pairs]


RING = [0, 2, 4, 6, 7, 5, 3, 1]
AHEAD = [(RING[i], RING[(i + 1) % 8]) for i in range(8)]
BACK = [(b, a) for a, b in AHEAD]
ACROSS = [(i, i ^ 1) for i in range(8)]
ALONG = [[(i, i ^ (2 * d)) for i in range(8)] for d in (1, 2, 3)]
HALF = BLOCK // 2
DEPTH = 1024
VMEM_LIMIT = 16 * 1024 * 1024


def send(value, pairs):
    return lax.ppermute(value, "tensor", pairs)


def swap(value, axis):
    return lax.ppermute(value, axis, [(0, 1), (1, 0)])


def settings():
    return dict(
        compiler_params=pltpu.CompilerParams(vmem_limit_bytes=VMEM_LIMIT),
        cost_estimate=pl.CostEstimate(flops=1, bytes_accessed=1, transcendentals=0),
    )


def in_vmem(count):
    return [pl.BlockSpec(memory_space=pltpu.VMEM)] * count


def pin_kernel(weight, own, swapped, out, sem):
    columns = weight.shape[1]
    copy = pltpu.make_async_copy(weight, out.at[:, pl.ds(0, columns)], sem)
    copy.start()
    for at in range(0, weight.shape[0], DEPTH):
        cut = pl.ds(at, DEPTH)
        out[cut, columns:] = jnp.concatenate([own[:, cut], swapped[:, cut]], axis=0).T
    copy.wait()


def pin_call(weight, own, swapped):
    width, columns = weight.shape
    return pl.pallas_call(
        pin_kernel,
        in_specs=[pl.BlockSpec(memory_space=pltpu.HBM)] + in_vmem(2),
        out_specs=in_vmem(1)[0],
        out_shape=pltpu.VMEM((width, columns + 2 * own.shape[0]), weight.dtype),
        scratch_shapes=[pltpu.SemaphoreType.DMA],
        name="pin",
        **settings(),
    )(weight, own, swapped)


def rows_kernel(group, table, weights, *refs):
    *pieces, shrunk, base, shrunk_out = refs
    columns = base.shape[1]
    total = None
    for at in range(0, weights.shape[0], DEPTH):
        cut = pl.ds(at, DEPTH)
        x = [p[:, cut] for p in pieces]
        x = x[0] if len(x) == 1 else jnp.concatenate(x, axis=0)
        part = jnp.dot(x, weights[cut, :], preferred_element_type=jnp.float32)
        total = part if total is None else total + part
    base[...] = total[:, :columns]
    lane = lax.broadcasted_iota(jnp.int32, shrunk.shape, 1)
    row = lax.broadcasted_iota(jnp.int32, shrunk.shape, 0)
    use = jnp.where(
        row < HALF,
        jnp.where(lane < 64, table[0, 2 * group], table[1, 2 * group]),
        jnp.where(lane < 64, table[0, 2 * group + 1], table[1, 2 * group + 1]),
    )
    small = total[:, columns:].astype(jnp.bfloat16).astype(jnp.float32)
    old = shrunk[...].astype(jnp.float32)
    shrunk_out[...] = jnp.where(use > 0, small, old).astype(jnp.bfloat16)


def rows_call(group, table, weights, pieces, shrunk):
    columns = weights.shape[1] - 128
    operands = [pltpu.with_memory_space_constraint(weights, pltpu.VMEM)] + pieces + [shrunk]
    return pl.pallas_call(
        functools.partial(rows_kernel, group),
        in_specs=[pl.BlockSpec(memory_space=pltpu.SMEM)] + in_vmem(len(operands)),
        out_specs=in_vmem(2),
        out_shape=[
            jax.ShapeDtypeStruct((BLOCK, columns), jnp.float32),
            jax.ShapeDtypeStruct((BLOCK, 128), jnp.bfloat16),
        ],
        name="rows",
        **settings(),
    )(table, *operands)


def pack_kernel(table, up, out):
    part = out.shape[3]
    for t in range(8):
        at = pl.multiple_of((2 * t + table[2]) * part, part)
        out[t, 0] = up[0, :, pl.ds(at, part)]


def pack_call(table, up_maps):
    _, rank, width = up_maps.shape
    part = width // 16
    return pl.pallas_call(
        pack_kernel,
        grid_spec=pltpu.PrefetchScalarGridSpec(
            num_scalar_prefetch=1,
            grid=(2,),
            in_specs=[pl.BlockSpec((1, rank, width), lambda s, t: (t[s], 0, 0))],
            out_specs=pl.BlockSpec((8, 1, rank, part), lambda s, t: (0, s, 0, 0)),
        ),
        out_shape=jax.ShapeDtypeStruct((8, 2, rank, part), jnp.bfloat16),
        name="pack",
        **settings(),
    )(table, pltpu.with_memory_space_constraint(up_maps, pltpu.HBM))


def take_kernel(table, got, out):
    out[...] = got[...]


def take_call(table, got):
    _, rank, part = got.shape
    return pl.pallas_call(
        take_kernel,
        grid_spec=pltpu.PrefetchScalarGridSpec(
            num_scalar_prefetch=1,
            grid=(8,),
            in_specs=[pl.BlockSpec((1, rank, part), lambda b, t: (t[b], 0, 0))],
            out_specs=pl.BlockSpec((1, rank, part), lambda b, t: (b, 0, 0)),
        ),
        out_shape=jax.ShapeDtypeStruct((8, rank, part), jnp.bfloat16),
        name="take",
        **settings(),
    )(table, got)


def finish_kernel(table, *refs):
    bases, gathered, refs = refs[:8], refs[8:12], refs[12:]
    up_mine, up_other, out, base, shrunk, rows, base_sems, sems = refs
    part = up_mine.shape[2]
    group = table[3, 0]
    fetches = [pltpu.make_async_copy(bases[g], base.at[g], base_sems.at[g]) for g in range(8)]
    for fetch in fetches:
        fetch.start()
    for i, pair in enumerate(gathered):
        shrunk[pl.ds(2 * i, 2)] = pair[...]
    copies = []
    for i in range(16):
        block, half = table[0, i], i % 2
        if half == 0:
            fetches[i // 2].wait()
        own = pl.ds(half * HALF, HALF)
        both = shrunk[table[1, i], own, :].astype(jnp.float32)
        value = jnp.where(table[2, i] > 0, both[:, 64:], both[:, :64]).astype(jnp.bfloat16)
        for up, side in ((up_mine, group), (up_other, 1 - group)):
            cut = pl.ds(pl.multiple_of(side * part, part), part)
            grown = jnp.dot(value, up[block], preferred_element_type=jnp.float32)
            rows[i, :, cut] = (base[i // 2, own, cut] + 0.5 * grown).astype(rows.dtype)
        to = pl.ds(pl.multiple_of((2 * block + half) * HALF, HALF), HALF)
        copies.append(pltpu.make_async_copy(rows.at[i], out.at[to], sems.at[i]))
        copies[-1].start()
    for copy in copies:
        copy.wait()


def finish_call(table, bases, gathered, up_mine, up_other):
    columns = bases[0].shape[1]
    return pl.pallas_call(
        finish_kernel,
        in_specs=[pl.BlockSpec(memory_space=pltpu.SMEM)]
        + [pl.BlockSpec(memory_space=pl.ANY)] * 8
        + in_vmem(6),
        out_specs=pl.BlockSpec(memory_space=pltpu.HBM),
        out_shape=jax.ShapeDtypeStruct((8 * BLOCK, columns), jnp.bfloat16),
        scratch_shapes=[
            pltpu.VMEM((8, BLOCK, columns), jnp.float32),
            pltpu.VMEM((8,) + gathered[0].shape[1:], jnp.bfloat16),
            pltpu.VMEM((16, HALF, columns), jnp.bfloat16),
            pltpu.SemaphoreType.DMA((8,)),
            pltpu.SemaphoreType.DMA((16,)),
        ],
        name="finish",
        **settings(),
    )(table, *bases, *gathered, up_mine, up_other)


def chain_body(
    tokens, query_weight, adapter_down_maps, adapter_up_maps, adapter_home_slot, adapter_per_block
):
    me = lax.axis_index("tensor")
    z, y = me // 2, me % 2
    store = lax.axis_index("store")
    group = lax.axis_index("groups")
    myself = me * 2 + store
    held, rank, width = adapter_down_maps.shape
    rows = tokens[0]
    halves = [rows[:HALF], rows[HALF:]]

    ahead, back = list(halves), list(halves[::-1])
    flight = [(send(ahead[k], AHEAD), send(back[k], BACK)) for k in range(2)]
    got, ahead, back, adapter_home_slot, adapter_per_block = lax.optimization_barrier(
        (flight[0], ahead, back, adapter_home_slot, adapter_per_block)
    )
    ahead.append(got[0])
    back.append(got[1])
    flight.append((send(ahead[2], AHEAD), send(back[2], BACK)))

    store_slots = find_slots(adapter_home_slot, adapter_per_block)
    owner = store_slots // held
    inside = store_slots % held
    picked = jnp.max(jnp.where(owner == myself, inside, 0), axis=1)
    owner_row = lax.dynamic_index_in_dim(owner, store, 0, keepdims=False).astype(jnp.int32)
    pick_own = lax.dynamic_index_in_dim(picked, store, 0, keepdims=False)
    pick_lent = lax.dynamic_index_in_dim(picked, 1 - store, 0, keepdims=False)

    down_own = lax.dynamic_index_in_dim(adapter_down_maps, pick_own, 0, keepdims=False)
    down_lent = lax.dynamic_index_in_dim(adapter_down_maps, pick_lent, 0, keepdims=False)
    down_swapped = swap(down_lent, "store")
    weights = pin_call(query_weight, down_own, down_swapped)
    up_sent = pack_call(jnp.concatenate([picked, group[None]]).astype(jnp.int32), adapter_up_maps)

    position = jnp.where(y == 0, z, 7 - z)
    places = []
    for k in range(8):
        step = (k + 1) // 2
        places += [position - step, position + step] if k % 2 else [position + step, position - step]
    places = jnp.stack(places) % 8
    blocks = jnp.where(places < 4, 2 * places, 15 - 2 * places).astype(jnp.int32)
    hit = blocks[:, None] == jnp.arange(8, dtype=jnp.int32)[None, :]
    owners = jnp.sum(jnp.where(hit, owner_row[None, :], 0), axis=1)
    table = jnp.stack([owners == myself, owners == me * 2 + 1 - store]).astype(jnp.int32)

    bases = []
    shrunk = jnp.zeros((BLOCK, 2 * rank), jnp.bfloat16)
    groups = [[rows], [ahead[2], back[2]]]
    for k in range(1, 6):
        (got_ahead, got_back), ahead, back, bases, shrunk, up_sent = lax.optimization_barrier(
            (flight[k], ahead, back, bases, shrunk, up_sent)
        )
        ahead.append(got_ahead)
        back.append(got_back)
        if k < 4:
            flight.append((send(ahead[k + 2], AHEAD), send(back[k + 2], BACK)))
        else:
            cut = slice(0, HALF // 2) if k == 4 else slice(HALF // 2, HALF)
            flight.append((send(ahead[6][cut], AHEAD), send(back[6][cut], BACK)))
        groups.append([got_ahead, got_back] if k % 2 == 0 else [got_back, got_ahead])
        for g in range(len(bases), min(len(bases) + 2, k + 2)):
            base, shrunk = rows_call(g, table, weights, groups[g], shrunk)
            bases.append(base)
    first, bases, shrunk, up_sent = lax.optimization_barrier((flight[6], bases, shrunk, up_sent))
    up_got = lax.all_to_all(
        up_sent.reshape(16, rank, -1), ("tensor", "store"), split_axis=0, concat_axis=0, tiled=True
    )
    first, second, bases, shrunk = lax.optimization_barrier((first, flight[7], bases, shrunk))
    base, shrunk = rows_call(7, table, weights, [first[0], second[0], first[1], second[1]], shrunk)
    bases.append(base)

    across, up_got = lax.optimization_barrier((send(shrunk, ACROSS), up_got))
    pair = jnp.stack([shrunk, across])
    everyone = [pair] + [send(pair, pairs) for pairs in ALONG]
    up_mine = take_call(owner_row, up_got)
    up_other = swap(up_mine, "groups")
    home, core = owners // 2, owners % 2
    where = 2 * ((home // 2) ^ z) + ((home % 2) ^ y)
    table = jnp.stack([blocks, where, core != store, jnp.broadcast_to(group, (16,))])
    return finish_call(table.astype(jnp.int32), bases, everyone, up_mine, up_other)[None]


def body(tokens, *rest):
    sizes = tuple(lax.axis_size(name) for name in ("groups", "tensor", "store"))
    fits = sizes == (2, 8, 2) and tokens.shape[1] == BLOCK
    return (chain_body if fits else general_body)(tokens, *rest)


def solution(mesh):
    placed = (
        P(("groups", "store"), "tensor", None),
        P(None, "tensor"),
        P(("tensor", "store"), None, None),
        P(("tensor", "store"), None, None),
        P(),
        P(),
    )
    return jax.shard_map(
        body,
        mesh=mesh,
        in_specs=placed,
        out_specs=P(("groups", "store"), None, "tensor"),
        check_vma=False,
    )
```

```python
import functools

import jax
import jax.numpy as jnp
from jax import lax
from jax.experimental import pallas as pl
from jax.experimental.pallas import tpu as pltpu
from jax.sharding import PartitionSpec as P

BLOCK = 128


def find_slots(adapter_home_slot, adapter_per_block):
    catalog = jnp.arange(adapter_home_slot.shape[0], dtype=jnp.int32)
    return jnp.sum(
        jnp.where(
            adapter_per_block[:, :, None] == catalog[None, None, :],
            adapter_home_slot[None, None, :],
            0,
        ),
        axis=2,
    )


def general_body(
    tokens, query_weight, adapter_down_maps, adapter_up_maps, adapter_home_slot, adapter_per_block
):
    shard_count = lax.axis_size("tensor")
    store_count = lax.axis_size("store")
    devices_all = shard_count * store_count
    my_tensor = lax.axis_index("tensor")
    my_store = lax.axis_index("store")
    myself = lax.axis_index(("tensor", "store"))
    held_adapters, rank_index, feature_width = adapter_down_maps.shape
    feature_index = query_weight.shape[1]
    own_rows = tokens[0]
    group_rows = own_rows.shape[0] * shard_count
    blocks = group_rows // BLOCK
    store_slots = find_slots(adapter_home_slot, adapter_per_block)
    owner = store_slots // held_adapters
    inside = store_slots % held_adapters
    picked = jnp.max(jnp.where(owner == myself, inside, -1), axis=1)
    select = (picked[:, None] == jnp.arange(held_adapters, dtype=jnp.int32)[None, :]).astype(
        jnp.bfloat16
    )
    down_map_parts = adapter_down_maps.reshape(
        held_adapters, rank_index, shard_count, feature_index
    )
    up_map_parts = adapter_up_maps.reshape(held_adapters, rank_index, shard_count, feature_index)
    send_down = jnp.einsum(
        "sl,lrtf->tsrf", select, down_map_parts, preferred_element_type=jnp.float32
    ).astype(jnp.bfloat16)
    send_up = jnp.einsum(
        "sl,lrtf->tsrf", select, up_map_parts, preferred_element_type=jnp.float32
    ).astype(jnp.bfloat16)
    recv_down, recv_up = (
        lax.all_to_all(
            sent.reshape(devices_all, rank_index, feature_index),
            ("tensor", "store"),
            split_axis=0,
            concat_axis=0,
            tiled=True,
        )
        for sent in (send_down, send_up)
    )
    owner_row = lax.dynamic_index_in_dim(owner, my_store, 0, keepdims=False)
    source_pick = (owner_row[:, None] == jnp.arange(devices_all, dtype=jnp.int32)[None, :]).astype(
        jnp.bfloat16
    )
    block_down = jnp.einsum(
        "bj,jrf->brf", source_pick, recv_down, preferred_element_type=jnp.float32
    ).astype(jnp.bfloat16)
    block_up = jnp.einsum(
        "bj,jrf->brf", source_pick, recv_up, preferred_element_type=jnp.float32
    ).astype(jnp.bfloat16)
    piece = lax.all_gather(own_rows, "tensor", axis=0, tiled=True)
    product = jnp.dot(piece, query_weight, preferred_element_type=jnp.float32)
    features = lax.dynamic_slice_in_dim(piece, my_tensor * feature_index, feature_index, 1)
    partial_value = jnp.einsum(
        "bnf,brf->bnr",
        features.reshape(blocks, BLOCK, feature_index),
        block_down,
        preferred_element_type=jnp.float32,
    )
    shrunk = lax.psum(partial_value, "tensor").astype(jnp.bfloat16)
    grown = jnp.einsum(
        "bnr,brf->bnf", shrunk, block_up, preferred_element_type=jnp.float32
    ).reshape(group_rows, feature_index)
    query = (product + 0.5 * grown).astype(jnp.bfloat16)
    return query[None]


def both_ways(pairs):
    return pairs + [(b, a) for a, b in pairs]


RING = [0, 2, 4, 6, 7, 5, 3, 1]
AHEAD = [(RING[i], RING[(i + 1) % 8]) for i in range(8)]
BACK = [(b, a) for a, b in AHEAD]
ACROSS = [(i, i ^ 1) for i in range(8)]
ALONG = [[(i, i ^ (2 * d)) for i in range(8)] for d in (1, 2, 3)]
SHARED = 32
HALF = (BLOCK - SHARED) // 2
STARTS = [SHARED, SHARED + HALF]
DEPTH = 1024
VMEM_LIMIT = 16 * 1024 * 1024


def send(value, pairs):
    return lax.ppermute(value, "tensor", pairs)


def swap(value, axis):
    return lax.ppermute(value, axis, [(0, 1), (1, 0)])


def settings():
    return dict(
        compiler_params=pltpu.CompilerParams(vmem_limit_bytes=VMEM_LIMIT),
        cost_estimate=pl.CostEstimate(flops=1, bytes_accessed=1, transcendentals=0),
    )


def in_vmem(count):
    return [pl.BlockSpec(memory_space=pltpu.VMEM)] * count


def pin_kernel(weight, own, swapped, out, sem):
    columns = weight.shape[1]
    copy = pltpu.make_async_copy(weight, out.at[:, pl.ds(0, columns)], sem)
    copy.start()
    for at in range(0, weight.shape[0], DEPTH):
        cut = pl.ds(at, DEPTH)
        out[cut, columns:] = jnp.concatenate([own[:, cut], swapped[:, cut]], axis=0).T
    copy.wait()


def pin_call(weight, own, swapped):
    width, columns = weight.shape
    return pl.pallas_call(
        pin_kernel,
        in_specs=[pl.BlockSpec(memory_space=pltpu.HBM)] + in_vmem(2),
        out_specs=in_vmem(1)[0],
        out_shape=pltpu.VMEM((width, columns + 2 * own.shape[0]), weight.dtype),
        scratch_shapes=[pltpu.SemaphoreType.DMA],
        name="pin",
        **settings(),
    )(weight, own, swapped)


def rows_kernel(sections, table, weights, *refs):
    *pieces, shrunk, base, shrunk_out = refs
    columns = base.shape[1]
    total = None
    for at in range(0, weights.shape[0], DEPTH):
        cut = pl.ds(at, DEPTH)
        x = [p[:, cut] for p in pieces]
        x = x[0] if len(x) == 1 else jnp.concatenate(x, axis=0)
        part = jnp.dot(x, weights[cut, :], preferred_element_type=jnp.float32)
        total = part if total is None else total + part
    base[...] = total[:, :columns]
    small = total[:, columns:].astype(jnp.bfloat16).astype(jnp.float32)
    values = {}
    for at, rows, start, entry in sections:
        lane = lax.broadcasted_iota(jnp.int32, (rows, 128), 1)
        use = jnp.where(lane < 64, table[0, entry], table[1, entry])
        old = values.get(start)
        if old is None:
            old = shrunk[start : start + rows].astype(jnp.float32)
        values[start] = jnp.where(use > 0, small[at : at + rows], old)
    shrunk_out[...] = shrunk[...]
    for start, value in values.items():
        shrunk_out[start : start + value.shape[0]] = value.astype(jnp.bfloat16)


def rows_call(sections, table, weights, pieces, shrunk):
    columns = weights.shape[1] - 128
    count = sum(rows for _, rows, _, _ in sections)
    operands = [pltpu.with_memory_space_constraint(weights, pltpu.VMEM)] + pieces + [shrunk]
    return pl.pallas_call(
        functools.partial(rows_kernel, sections),
        in_specs=[pl.BlockSpec(memory_space=pltpu.SMEM)] + in_vmem(len(operands)),
        out_specs=in_vmem(2),
        out_shape=[
            jax.ShapeDtypeStruct((count, columns), jnp.float32),
            jax.ShapeDtypeStruct((BLOCK, 128), jnp.bfloat16),
        ],
        name="rows",
        **settings(),
    )(table, *operands)


def pack_kernel(table, up, out):
    part = out.shape[3]
    for t in range(8):
        at = pl.multiple_of((2 * t + table[2]) * part, part)
        out[t, 0] = up[0, :, pl.ds(at, part)]


def pack_call(table, up_maps):
    _, rank, width = up_maps.shape
    part = width // 16
    return pl.pallas_call(
        pack_kernel,
        grid_spec=pltpu.PrefetchScalarGridSpec(
            num_scalar_prefetch=1,
            grid=(2,),
            in_specs=[pl.BlockSpec((1, rank, width), lambda s, t: (t[s], 0, 0))],
            out_specs=pl.BlockSpec((8, 1, rank, part), lambda s, t: (0, s, 0, 0)),
        ),
        out_shape=jax.ShapeDtypeStruct((8, 2, rank, part), jnp.bfloat16),
        name="pack",
        **settings(),
    )(table, pltpu.with_memory_space_constraint(up_maps, pltpu.HBM))


def take_kernel(table, got, out):
    out[...] = got[...]


def take_call(table, got):
    _, rank, part = got.shape
    return pl.pallas_call(
        take_kernel,
        grid_spec=pltpu.PrefetchScalarGridSpec(
            num_scalar_prefetch=1,
            grid=(8,),
            in_specs=[pl.BlockSpec((1, rank, part), lambda b, t: (t[b], 0, 0))],
            out_specs=pl.BlockSpec((1, rank, part), lambda b, t: (b, 0, 0)),
        ),
        out_shape=jax.ShapeDtypeStruct((8, rank, part), jnp.bfloat16),
        name="take",
        **settings(),
    )(table, got)


def finish_kernel(jobs, table, *refs):
    count = len(refs) - 12
    bases, gathered, refs = refs[:count], refs[count : count + 4], refs[count + 4 :]
    up_mine, up_other, out, base, shrunk, rows, base_sems, sems = refs
    part = up_mine.shape[2]
    group = table[3, 0]
    fetches = []
    for g, source in enumerate(bases):
        to = base.at[g, pl.ds(0, source.shape[0])]
        fetches.append(pltpu.make_async_copy(source, to, base_sems.at[g]))
        fetches[-1].start()
    for i, pair in enumerate(gathered):
        shrunk[pl.ds(2 * i, 2)] = pair[...]
    copies, fetched = [], set()
    for entry, (g, at, count, start) in enumerate(jobs):
        block = table[0, entry]
        if g not in fetched:
            fetches[g].wait()
            fetched.add(g)
        own = pl.ds(at, count)
        both = shrunk[table[1, entry], start : start + count, :].astype(jnp.float32)
        value = jnp.where(table[2, entry] > 0, both[:, 64:], both[:, :64]).astype(jnp.bfloat16)
        for up, side in ((up_mine, group), (up_other, 1 - group)):
            cut = pl.ds(pl.multiple_of(side * part, part), part)
            grown = jnp.dot(value, up[block], preferred_element_type=jnp.float32)
            rows[entry, :count, cut] = (base[g, own, cut] + 0.5 * grown).astype(rows.dtype)
        to = pl.ds(pl.multiple_of(block * BLOCK + start, 16), count)
        copies.append(
            pltpu.make_async_copy(rows.at[entry, pl.ds(0, count)], out.at[to], sems.at[entry])
        )
        copies[-1].start()
    for copy in copies:
        copy.wait()


def finish_call(jobs, table, bases, gathered, up_mine, up_other):
    columns = bases[0].shape[1]
    return pl.pallas_call(
        functools.partial(finish_kernel, jobs),
        in_specs=[pl.BlockSpec(memory_space=pltpu.SMEM)]
        + [pl.BlockSpec(memory_space=pl.ANY)] * len(bases)
        + in_vmem(6),
        out_specs=pl.BlockSpec(memory_space=pltpu.HBM),
        out_shape=jax.ShapeDtypeStruct((8 * BLOCK, columns), jnp.bfloat16),
        scratch_shapes=[
            pltpu.VMEM((len(bases), BLOCK, columns), jnp.float32),
            pltpu.VMEM((8,) + gathered[0].shape[1:], jnp.bfloat16),
            pltpu.VMEM((len(jobs), HALF, columns), jnp.bfloat16),
            pltpu.SemaphoreType.DMA((len(bases),)),
            pltpu.SemaphoreType.DMA((len(jobs),)),
        ],
        name="finish",
        compiler_params=pltpu.CompilerParams(vmem_limit_bytes=48 * 1024 * 1024),
        cost_estimate=pl.CostEstimate(flops=1, bytes_accessed=1, transcendentals=0),
    )(table, *bases, *gathered, up_mine, up_other)


def chain_body(
    tokens, query_weight, adapter_down_maps, adapter_up_maps, adapter_home_slot, adapter_per_block
):
    me = lax.axis_index("tensor")
    z, y = me // 2, me % 2
    store = lax.axis_index("store")
    group = lax.axis_index("groups")
    myself = me * 2 + store
    held, rank, width = adapter_down_maps.shape
    rows = tokens[0]
    shared = lax.all_gather(rows[:SHARED], "tensor", axis=0)
    halves = [rows[start : start + HALF] for start in STARTS]

    ahead, back = list(halves), list(halves[::-1])
    flight = [(send(ahead[k], AHEAD), send(back[k], BACK)) for k in range(2)]
    got, ahead, back, adapter_home_slot, adapter_per_block = lax.optimization_barrier(
        (flight[0], ahead, back, adapter_home_slot, adapter_per_block)
    )
    ahead.append(got[0])
    back.append(got[1])
    flight.append((send(ahead[2], AHEAD), send(back[2], BACK)))

    store_slots = find_slots(adapter_home_slot, adapter_per_block)
    owner = store_slots // held
    inside = store_slots % held
    picked = jnp.max(jnp.where(owner == myself, inside, 0), axis=1)
    owner_row = lax.dynamic_index_in_dim(owner, store, 0, keepdims=False).astype(jnp.int32)
    pick_own = lax.dynamic_index_in_dim(picked, store, 0, keepdims=False)
    pick_lent = lax.dynamic_index_in_dim(picked, 1 - store, 0, keepdims=False)

    down_own = lax.dynamic_index_in_dim(adapter_down_maps, pick_own, 0, keepdims=False)
    down_lent = lax.dynamic_index_in_dim(adapter_down_maps, pick_lent, 0, keepdims=False)
    down_swapped = swap(down_lent, "store")
    weights = pin_call(query_weight, down_own, down_swapped)
    up_sent = pack_call(jnp.concatenate([picked, group[None]]).astype(jnp.int32), adapter_up_maps)

    position = jnp.where(y == 0, z, 7 - z)
    places = []
    for k in range(8):
        step = (k + 1) // 2
        places += [position - step, position + step] if k % 2 else [position + step, position - step]
    places = jnp.stack(places) % 8
    blocks = jnp.where(places < 4, 2 * places, 15 - 2 * places).astype(jnp.int32)
    hit = blocks[:, None] == jnp.arange(8, dtype=jnp.int32)[None, :]
    owners = jnp.sum(jnp.where(hit, owner_row[None, :], 0), axis=1)
    blocks = jnp.concatenate([blocks, jnp.arange(8, dtype=jnp.int32)])
    owners = jnp.concatenate([owners, owner_row])
    table = jnp.stack([owners == myself, owners == me * 2 + 1 - store]).astype(jnp.int32)

    sections = [
        [(0, HALF, STARTS[0], 2 * g), (HALF, HALF, STARTS[1], 2 * g + 1)] for g in range(8)
    ] + [[(SHARED * i, SHARED, 0, 16 + 4 * g + i) for i in range(4)] for g in range(2)]
    bases = [None] * 10
    shrunk = jnp.zeros((BLOCK, 2 * rank), jnp.bfloat16)

    def work(g, pieces):
        bases[g], value = rows_call(sections[g], table, weights, pieces, shrunk)
        return value

    groups = [halves, [ahead[2], back[2]]]
    for k in range(1, 7):
        (got_ahead, got_back), ahead, back, bases, shrunk, up_sent = lax.optimization_barrier(
            (flight[k], ahead, back, bases, shrunk, up_sent)
        )
        ahead.append(got_ahead)
        back.append(got_back)
        if k < 5:
            flight.append((send(ahead[k + 2], AHEAD), send(back[k + 2], BACK)))
        groups.append([got_ahead, got_back] if k % 2 == 0 else [got_back, got_ahead])
        for g in {1: (0, 1), 2: (2, 3)}.get(k, (k + 1,)):
            shrunk = work(g, groups[g])
        if k == 4:
            shared = shared.reshape(2, 4 * SHARED, width)
            for g in range(2):
                shrunk = work(8 + g, [shared[g]])
    shrunk, up_sent = lax.optimization_barrier((shrunk, up_sent))
    up_got = lax.all_to_all(
        up_sent.reshape(16, rank, -1), ("tensor", "store"), split_axis=0, concat_axis=0, tiled=True
    )
    across, up_got = lax.optimization_barrier((send(shrunk, ACROSS), up_got))
    pair = jnp.stack([shrunk, across])
    everyone = [pair] + [send(pair, pairs) for pairs in ALONG]
    up_mine = take_call(owner_row, up_got)
    up_other = swap(up_mine, "groups")
    home, core = owners // 2, owners % 2
    where = 2 * ((home // 2) ^ z) + ((home % 2) ^ y)
    table = jnp.stack([blocks, where, core != store, jnp.broadcast_to(group, blocks.shape)])
    jobs = [(g, at, count, start) for g in range(10) for at, count, start, _ in sections[g]]
    return finish_call(jobs, table.astype(jnp.int32), bases, everyone, up_mine, up_other)[None]


def body(tokens, *rest):
    sizes = tuple(lax.axis_size(name) for name in ("groups", "tensor", "store"))
    fits = sizes == (2, 8, 2) and tokens.shape[1] == BLOCK
    return (chain_body if fits else general_body)(tokens, *rest)


def solution(mesh):
    placed = (
        P(("groups", "store"), "tensor", None),
        P(None, "tensor"),
        P(("tensor", "store"), None, None),
        P(("tensor", "store"), None, None),
        P(),
        P(),
    )
    return jax.shard_map(
        body,
        mesh=mesh,
        in_specs=placed,
        out_specs=P(("groups", "store"), None, "tensor"),
        check_vma=False,
    )
```

```python
import functools

import jax
import jax.numpy as jnp
from jax import lax
from jax.experimental import pallas as pl
from jax.experimental.pallas import tpu as pltpu
from jax.sharding import PartitionSpec as P

BLOCK = 128


def find_slots(adapter_home_slot, adapter_per_block):
    catalog = jnp.arange(adapter_home_slot.shape[0], dtype=jnp.int32)
    return jnp.sum(
        jnp.where(
            adapter_per_block[:, :, None] == catalog[None, None, :],
            adapter_home_slot[None, None, :],
            0,
        ),
        axis=2,
    )


def general_body(
    tokens, query_weight, adapter_down_maps, adapter_up_maps, adapter_home_slot, adapter_per_block
):
    shard_count = lax.axis_size("tensor")
    store_count = lax.axis_size("store")
    devices_all = shard_count * store_count
    my_tensor = lax.axis_index("tensor")
    my_store = lax.axis_index("store")
    myself = lax.axis_index(("tensor", "store"))
    held_adapters, rank_index, feature_width = adapter_down_maps.shape
    feature_index = query_weight.shape[1]
    own_rows = tokens[0]
    group_rows = own_rows.shape[0] * shard_count
    blocks = group_rows // BLOCK
    store_slots = find_slots(adapter_home_slot, adapter_per_block)
    owner = store_slots // held_adapters
    inside = store_slots % held_adapters
    picked = jnp.max(jnp.where(owner == myself, inside, -1), axis=1)
    select = (picked[:, None] == jnp.arange(held_adapters, dtype=jnp.int32)[None, :]).astype(
        jnp.bfloat16
    )
    down_map_parts = adapter_down_maps.reshape(
        held_adapters, rank_index, shard_count, feature_index
    )
    up_map_parts = adapter_up_maps.reshape(held_adapters, rank_index, shard_count, feature_index)
    send_down = jnp.einsum(
        "sl,lrtf->tsrf", select, down_map_parts, preferred_element_type=jnp.float32
    ).astype(jnp.bfloat16)
    send_up = jnp.einsum(
        "sl,lrtf->tsrf", select, up_map_parts, preferred_element_type=jnp.float32
    ).astype(jnp.bfloat16)
    recv_down, recv_up = (
        lax.all_to_all(
            sent.reshape(devices_all, rank_index, feature_index),
            ("tensor", "store"),
            split_axis=0,
            concat_axis=0,
            tiled=True,
        )
        for sent in (send_down, send_up)
    )
    owner_row = lax.dynamic_index_in_dim(owner, my_store, 0, keepdims=False)
    source_pick = (owner_row[:, None] == jnp.arange(devices_all, dtype=jnp.int32)[None, :]).astype(
        jnp.bfloat16
    )
    block_down = jnp.einsum(
        "bj,jrf->brf", source_pick, recv_down, preferred_element_type=jnp.float32
    ).astype(jnp.bfloat16)
    block_up = jnp.einsum(
        "bj,jrf->brf", source_pick, recv_up, preferred_element_type=jnp.float32
    ).astype(jnp.bfloat16)
    piece = lax.all_gather(own_rows, "tensor", axis=0, tiled=True)
    product = jnp.dot(piece, query_weight, preferred_element_type=jnp.float32)
    features = lax.dynamic_slice_in_dim(piece, my_tensor * feature_index, feature_index, 1)
    partial_value = jnp.einsum(
        "bnf,brf->bnr",
        features.reshape(blocks, BLOCK, feature_index),
        block_down,
        preferred_element_type=jnp.float32,
    )
    shrunk = lax.psum(partial_value, "tensor").astype(jnp.bfloat16)
    grown = jnp.einsum(
        "bnr,brf->bnf", shrunk, block_up, preferred_element_type=jnp.float32
    ).reshape(group_rows, feature_index)
    query = (product + 0.5 * grown).astype(jnp.bfloat16)
    return query[None]


def both_ways(pairs):
    return pairs + [(b, a) for a, b in pairs]


RING = [0, 2, 4, 6, 7, 5, 3, 1]
AHEAD = [(RING[i], RING[(i + 1) % 8]) for i in range(8)]
BACK = [(b, a) for a, b in AHEAD]
ACROSS = [(i, i ^ 1) for i in range(8)]
ALONG = [[(i, i ^ (2 * d)) for i in range(8)] for d in (1, 2, 3)]
HALF = BLOCK // 2
DEPTH = 1024
VMEM_LIMIT = 16 * 1024 * 1024


def send(value, pairs):
    return lax.ppermute(value, "tensor", pairs)


def swap(value, axis):
    return lax.ppermute(value, axis, [(0, 1), (1, 0)])


def settings():
    return dict(
        compiler_params=pltpu.CompilerParams(vmem_limit_bytes=VMEM_LIMIT),
        cost_estimate=pl.CostEstimate(flops=1, bytes_accessed=1, transcendentals=0),
    )


def in_vmem(count):
    return [pl.BlockSpec(memory_space=pltpu.VMEM)] * count


def pin_kernel(weight, own, swapped, out, sem):
    columns = weight.shape[1]
    copy = pltpu.make_async_copy(weight, out.at[:, pl.ds(0, columns)], sem)
    copy.start()
    for at in range(0, weight.shape[0], DEPTH):
        cut = pl.ds(at, DEPTH)
        out[cut, columns:] = jnp.concatenate([own[:, cut], swapped[:, cut]], axis=0).T
    copy.wait()


def pin_call(weight, own, swapped):
    width, columns = weight.shape
    return pl.pallas_call(
        pin_kernel,
        in_specs=[pl.BlockSpec(memory_space=pl.ANY)] + in_vmem(2),
        out_specs=in_vmem(1)[0],
        out_shape=pltpu.VMEM((width, columns + 2 * own.shape[0]), weight.dtype),
        scratch_shapes=[pltpu.SemaphoreType.DMA],
        name="pin",
        **settings(),
    )(weight, own, swapped)


def rows_kernel(group, table, weights, *refs):
    *pieces, shrunk, base, shrunk_out = refs
    columns = base.shape[1]
    total = None
    for at in range(0, weights.shape[0], DEPTH):
        cut = pl.ds(at, DEPTH)
        x = [p[:, cut] for p in pieces]
        x = x[0] if len(x) == 1 else jnp.concatenate(x, axis=0)
        part = jnp.dot(x, weights[cut, :], preferred_element_type=jnp.float32)
        total = part if total is None else total + part
    base[...] = total[:, :columns]
    lane = lax.broadcasted_iota(jnp.int32, shrunk.shape, 1)
    row = lax.broadcasted_iota(jnp.int32, shrunk.shape, 0)
    use = jnp.where(
        row < HALF,
        jnp.where(lane < 64, table[0, 2 * group], table[1, 2 * group]),
        jnp.where(lane < 64, table[0, 2 * group + 1], table[1, 2 * group + 1]),
    )
    small = total[:, columns:].astype(jnp.bfloat16).astype(jnp.float32)
    old = shrunk[...].astype(jnp.float32)
    shrunk_out[...] = jnp.where(use > 0, small, old).astype(jnp.bfloat16)


def rows_call(group, table, weights, pieces, shrunk):
    columns = weights.shape[1] - 128
    operands = [pltpu.with_memory_space_constraint(weights, pltpu.VMEM)] + pieces + [shrunk]
    return pl.pallas_call(
        functools.partial(rows_kernel, group),
        in_specs=[pl.BlockSpec(memory_space=pltpu.SMEM)] + in_vmem(len(operands)),
        out_specs=in_vmem(2),
        out_shape=[
            jax.ShapeDtypeStruct((BLOCK, columns), jnp.float32),
            jax.ShapeDtypeStruct((BLOCK, 128), jnp.bfloat16),
        ],
        name="rows",
        **settings(),
    )(table, *operands)


def pack_kernel(table, up, out):
    part = out.shape[3]
    for t in range(8):
        at = pl.multiple_of((2 * t + table[2]) * part, part)
        out[t, 0] = up[0, :, pl.ds(at, part)]


def pack_call(table, up_maps):
    _, rank, width = up_maps.shape
    part = width // 16
    return pl.pallas_call(
        pack_kernel,
        grid_spec=pltpu.PrefetchScalarGridSpec(
            num_scalar_prefetch=1,
            grid=(2,),
            in_specs=[pl.BlockSpec((1, rank, width), lambda s, t: (t[s], 0, 0))],
            out_specs=pl.BlockSpec((8, 1, rank, part), lambda s, t: (0, s, 0, 0)),
        ),
        out_shape=jax.ShapeDtypeStruct((8, 2, rank, part), jnp.bfloat16),
        name="pack",
        **settings(),
    )(table, pltpu.with_memory_space_constraint(up_maps, pltpu.HBM))


def take_kernel(table, got, out):
    out[...] = got[...]


def take_call(table, got):
    _, rank, part = got.shape
    return pl.pallas_call(
        take_kernel,
        grid_spec=pltpu.PrefetchScalarGridSpec(
            num_scalar_prefetch=1,
            grid=(8,),
            in_specs=[pl.BlockSpec((1, rank, part), lambda b, t: (t[b], 0, 0))],
            out_specs=pl.BlockSpec((1, rank, part), lambda b, t: (b, 0, 0)),
        ),
        out_shape=jax.ShapeDtypeStruct((8, rank, part), jnp.bfloat16),
        name="take",
        **settings(),
    )(table, got)


def finish_kernel(table, *refs):
    bases, gathered, refs = refs[:8], refs[8:12], refs[12:]
    up_mine, up_other, out, base, shrunk, rows, base_sems, sems = refs
    part = up_mine.shape[2]
    group = table[3, 0]
    fetches = [pltpu.make_async_copy(bases[g], base.at[g], base_sems.at[g]) for g in range(8)]
    for fetch in fetches:
        fetch.start()
    for i, pair in enumerate(gathered):
        shrunk[pl.ds(2 * i, 2)] = pair[...]
    copies = []
    for i in range(16):
        block, half = table[0, i], i % 2
        if half == 0:
            fetches[i // 2].wait()
        own = pl.ds(half * HALF, HALF)
        both = shrunk[table[1, i], own, :].astype(jnp.float32)
        value = jnp.where(table[2, i] > 0, both[:, 64:], both[:, :64]).astype(jnp.bfloat16)
        for up, side in ((up_mine, group), (up_other, 1 - group)):
            cut = pl.ds(pl.multiple_of(side * part, part), part)
            grown = jnp.dot(value, up[block], preferred_element_type=jnp.float32)
            rows[i, :, cut] = (base[i // 2, own, cut] + 0.5 * grown).astype(rows.dtype)
        to = pl.ds(pl.multiple_of((2 * block + half) * HALF, HALF), HALF)
        copies.append(pltpu.make_async_copy(rows.at[i], out.at[to], sems.at[i]))
        copies[-1].start()
    for copy in copies:
        copy.wait()


def finish_call(table, bases, gathered, up_mine, up_other):
    columns = bases[0].shape[1]
    return pl.pallas_call(
        finish_kernel,
        in_specs=[pl.BlockSpec(memory_space=pltpu.SMEM)]
        + [pl.BlockSpec(memory_space=pl.ANY)] * 8
        + in_vmem(6),
        out_specs=pl.BlockSpec(memory_space=pltpu.HBM),
        out_shape=jax.ShapeDtypeStruct((8 * BLOCK, columns), jnp.bfloat16),
        scratch_shapes=[
            pltpu.VMEM((8, BLOCK, columns), jnp.float32),
            pltpu.VMEM((8,) + gathered[0].shape[1:], jnp.bfloat16),
            pltpu.VMEM((16, HALF, columns), jnp.bfloat16),
            pltpu.SemaphoreType.DMA((8,)),
            pltpu.SemaphoreType.DMA((16,)),
        ],
        name="finish",
        **settings(),
    )(
        table,
        *[pltpu.with_memory_space_constraint(base, pltpu.HBM) for base in bases],
        *gathered,
        up_mine,
        up_other,
    )


def chain_body(
    tokens, query_weight, adapter_down_maps, adapter_up_maps, adapter_home_slot, adapter_per_block
):
    me = lax.axis_index("tensor")
    z, y = me // 2, me % 2
    store = lax.axis_index("store")
    group = lax.axis_index("groups")
    myself = me * 2 + store
    held, rank, width = adapter_down_maps.shape
    rows = tokens[0]
    halves = [rows[:HALF], rows[HALF:]]

    ahead, back = list(halves), list(halves[::-1])
    flight = [(send(ahead[k], AHEAD), send(back[k], BACK)) for k in range(2)]
    got, ahead, back, adapter_home_slot, adapter_per_block = lax.optimization_barrier(
        (flight[0], ahead, back, adapter_home_slot, adapter_per_block)
    )
    ahead.append(got[0])
    back.append(got[1])
    flight.append((send(ahead[2], AHEAD), send(back[2], BACK)))

    store_slots = find_slots(adapter_home_slot, adapter_per_block)
    owner = store_slots // held
    inside = store_slots % held
    picked = jnp.max(jnp.where(owner == myself, inside, 0), axis=1)
    owner_row = lax.dynamic_index_in_dim(owner, store, 0, keepdims=False).astype(jnp.int32)
    pick_own = lax.dynamic_index_in_dim(picked, store, 0, keepdims=False)
    pick_lent = lax.dynamic_index_in_dim(picked, 1 - store, 0, keepdims=False)

    down_own = lax.dynamic_index_in_dim(adapter_down_maps, pick_own, 0, keepdims=False)
    down_lent = lax.dynamic_index_in_dim(adapter_down_maps, pick_lent, 0, keepdims=False)
    down_swapped = swap(down_lent, "store")
    weights = pin_call(query_weight, down_own, down_swapped)
    up_sent = pack_call(jnp.concatenate([picked, group[None]]).astype(jnp.int32), adapter_up_maps)

    position = jnp.where(y == 0, z, 7 - z)
    places = []
    for k in range(8):
        step = (k + 1) // 2
        places += [position - step, position + step] if k % 2 else [position + step, position - step]
    places = jnp.stack(places) % 8
    blocks = jnp.where(places < 4, 2 * places, 15 - 2 * places).astype(jnp.int32)
    hit = blocks[:, None] == jnp.arange(8, dtype=jnp.int32)[None, :]
    owners = jnp.sum(jnp.where(hit, owner_row[None, :], 0), axis=1)
    table = jnp.stack([owners == myself, owners == me * 2 + 1 - store]).astype(jnp.int32)

    bases = []
    shrunk = jnp.zeros((BLOCK, 2 * rank), jnp.bfloat16)
    groups = [[rows], [ahead[2], back[2]]]
    for k in range(1, 7):
        (got_ahead, got_back), ahead, back, bases, shrunk, up_sent = lax.optimization_barrier(
            (flight[k], ahead, back, bases, shrunk, up_sent)
        )
        ahead.append(got_ahead)
        back.append(got_back)
        if k < 5:
            flight.append((send(ahead[k + 2], AHEAD), send(back[k + 2], BACK)))
        groups.append([got_ahead, got_back] if k % 2 == 0 else [got_back, got_ahead])
        for g in range(len(bases), min(len(bases) + 2, k + 2, 7)):
            base, shrunk = rows_call(g, table, weights, groups[g], shrunk)
            bases.append(base)
    up_got = lax.all_to_all(
        up_sent.reshape(16, rank, -1), ("tensor", "store"), split_axis=0, concat_axis=0, tiled=True
    )
    base, shrunk = rows_call(7, table, weights, groups[7], shrunk)
    bases.append(base)

    across = send(shrunk, ACROSS)
    pair = jnp.stack([shrunk, across])
    everyone = [pair] + [send(pair, pairs) for pairs in ALONG]
    up_got, _ = lax.optimization_barrier((up_got, across))
    up_mine = take_call(owner_row, up_got)
    up_other = swap(up_mine, "groups")
    home, core = owners // 2, owners % 2
    where = 2 * ((home // 2) ^ z) + ((home % 2) ^ y)
    table = jnp.stack([blocks, where, core != store, jnp.broadcast_to(group, (16,))])
    return finish_call(table.astype(jnp.int32), bases, everyone, up_mine, up_other)[None]


def body(tokens, *rest):
    sizes = tuple(lax.axis_size(name) for name in ("groups", "tensor", "store"))
    fits = sizes == (2, 8, 2) and tokens.shape[1] == BLOCK
    return (chain_body if fits else general_body)(tokens, *rest)


def solution(mesh):
    placed = (
        P(("groups", "store"), "tensor", None),
        P(None, "tensor"),
        P(("tensor", "store"), None, None),
        P(("tensor", "store"), None, None),
        P(),
        P(),
    )
    return jax.shard_map(
        body,
        mesh=mesh,
        in_specs=placed,
        out_specs=P(("groups", "store"), None, "tensor"),
        check_vma=False,
    )
```

```python
import functools

import jax
import jax.numpy as jnp
from jax import lax
from jax.experimental import pallas as pl
from jax.experimental.pallas import tpu as pltpu
from jax.sharding import PartitionSpec as P

BLOCK = 128


def find_slots(adapter_home_slot, adapter_per_block):
    catalog = jnp.arange(adapter_home_slot.shape[0], dtype=jnp.int32)
    return jnp.sum(
        jnp.where(
            adapter_per_block[:, :, None] == catalog[None, None, :],
            adapter_home_slot[None, None, :],
            0,
        ),
        axis=2,
    )


def general_body(
    tokens, query_weight, adapter_down_maps, adapter_up_maps, adapter_home_slot, adapter_per_block
):
    shard_count = lax.axis_size("tensor")
    store_count = lax.axis_size("store")
    devices_all = shard_count * store_count
    my_tensor = lax.axis_index("tensor")
    my_store = lax.axis_index("store")
    myself = lax.axis_index(("tensor", "store"))
    held_adapters, rank_index, feature_width = adapter_down_maps.shape
    feature_index = query_weight.shape[1]
    own_rows = tokens[0]
    group_rows = own_rows.shape[0] * shard_count
    blocks = group_rows // BLOCK
    store_slots = find_slots(adapter_home_slot, adapter_per_block)
    owner = store_slots // held_adapters
    inside = store_slots % held_adapters
    picked = jnp.max(jnp.where(owner == myself, inside, -1), axis=1)
    select = (picked[:, None] == jnp.arange(held_adapters, dtype=jnp.int32)[None, :]).astype(
        jnp.bfloat16
    )
    down_map_parts = adapter_down_maps.reshape(
        held_adapters, rank_index, shard_count, feature_index
    )
    up_map_parts = adapter_up_maps.reshape(held_adapters, rank_index, shard_count, feature_index)
    send_down = jnp.einsum(
        "sl,lrtf->tsrf", select, down_map_parts, preferred_element_type=jnp.float32
    ).astype(jnp.bfloat16)
    send_up = jnp.einsum(
        "sl,lrtf->tsrf", select, up_map_parts, preferred_element_type=jnp.float32
    ).astype(jnp.bfloat16)
    recv_down, recv_up = (
        lax.all_to_all(
            sent.reshape(devices_all, rank_index, feature_index),
            ("tensor", "store"),
            split_axis=0,
            concat_axis=0,
            tiled=True,
        )
        for sent in (send_down, send_up)
    )
    owner_row = lax.dynamic_index_in_dim(owner, my_store, 0, keepdims=False)
    source_pick = (owner_row[:, None] == jnp.arange(devices_all, dtype=jnp.int32)[None, :]).astype(
        jnp.bfloat16
    )
    block_down = jnp.einsum(
        "bj,jrf->brf", source_pick, recv_down, preferred_element_type=jnp.float32
    ).astype(jnp.bfloat16)
    block_up = jnp.einsum(
        "bj,jrf->brf", source_pick, recv_up, preferred_element_type=jnp.float32
    ).astype(jnp.bfloat16)
    piece = lax.all_gather(own_rows, "tensor", axis=0, tiled=True)
    product = jnp.dot(piece, query_weight, preferred_element_type=jnp.float32)
    features = lax.dynamic_slice_in_dim(piece, my_tensor * feature_index, feature_index, 1)
    partial_value = jnp.einsum(
        "bnf,brf->bnr",
        features.reshape(blocks, BLOCK, feature_index),
        block_down,
        preferred_element_type=jnp.float32,
    )
    shrunk = lax.psum(partial_value, "tensor").astype(jnp.bfloat16)
    grown = jnp.einsum(
        "bnr,brf->bnf", shrunk, block_up, preferred_element_type=jnp.float32
    ).reshape(group_rows, feature_index)
    query = (product + 0.5 * grown).astype(jnp.bfloat16)
    return query[None]


def both_ways(pairs):
    return pairs + [(b, a) for a, b in pairs]


RING = [0, 2, 4, 6, 7, 5, 3, 1]
AHEAD = [(RING[i], RING[(i + 1) % 8]) for i in range(8)]
BACK = [(b, a) for a, b in AHEAD]
ACROSS = [(i, i ^ 1) for i in range(8)]
ALONG = [[(i, i ^ (2 * d)) for i in range(8)] for d in (1, 2, 3)]
HALF = BLOCK // 2
DEPTH = 1024
VMEM_LIMIT = 16 * 1024 * 1024


def send(value, pairs):
    return lax.ppermute(value, "tensor", pairs)


def swap(value, axis):
    return lax.ppermute(value, axis, [(0, 1), (1, 0)])


def settings():
    return dict(
        compiler_params=pltpu.CompilerParams(vmem_limit_bytes=VMEM_LIMIT),
        cost_estimate=pl.CostEstimate(flops=1, bytes_accessed=1, transcendentals=0),
    )


def in_vmem(count):
    return [pl.BlockSpec(memory_space=pltpu.VMEM)] * count


def pin_kernel(weight, own, swapped, out, sem):
    columns = weight.shape[1]
    copy = pltpu.make_async_copy(weight, out.at[:, pl.ds(0, columns)], sem)
    copy.start()
    for at in range(0, weight.shape[0], DEPTH):
        cut = pl.ds(at, DEPTH)
        out[cut, columns:] = jnp.concatenate([own[:, cut], swapped[:, cut]], axis=0).T
    copy.wait()


def pin_call(weight, own, swapped):
    width, columns = weight.shape
    return pl.pallas_call(
        pin_kernel,
        in_specs=[pl.BlockSpec(memory_space=pl.ANY)] + in_vmem(2),
        out_specs=in_vmem(1)[0],
        out_shape=pltpu.VMEM((width, columns + 2 * own.shape[0]), weight.dtype),
        scratch_shapes=[pltpu.SemaphoreType.DMA],
        name="pin",
        **settings(),
    )(weight, own, swapped)


def rows_kernel(group, table, weights, *refs):
    *pieces, shrunk, base, shrunk_out = refs
    columns = base.shape[1]
    total = None
    for at in range(0, weights.shape[0], DEPTH):
        cut = pl.ds(at, DEPTH)
        x = [p[:, cut] for p in pieces]
        x = x[0] if len(x) == 1 else jnp.concatenate(x, axis=0)
        part = jnp.dot(x, weights[cut, :], preferred_element_type=jnp.float32)
        total = part if total is None else total + part
    base[...] = total[:, :columns]
    lane = lax.broadcasted_iota(jnp.int32, shrunk.shape, 1)
    use = jnp.where(lane < 64, table[0, group], table[1, group])
    small = total[:, columns:].astype(jnp.bfloat16).astype(jnp.float32)
    old = shrunk[...].astype(jnp.float32)
    shrunk_out[...] = jnp.where(use > 0, small, old).astype(jnp.bfloat16)


def rows_call(group, table, weights, pieces, shrunk):
    columns = weights.shape[1] - 128
    operands = [pltpu.with_memory_space_constraint(weights, pltpu.VMEM)] + pieces + [shrunk]
    return pl.pallas_call(
        functools.partial(rows_kernel, group),
        in_specs=[pl.BlockSpec(memory_space=pltpu.SMEM)] + in_vmem(len(operands)),
        out_specs=in_vmem(2),
        out_shape=[
            jax.ShapeDtypeStruct((BLOCK, columns), jnp.float32),
            jax.ShapeDtypeStruct((BLOCK, 128), jnp.bfloat16),
        ],
        name="rows",
        **settings(),
    )(table, *operands)


def pack_kernel(table, up, out):
    part = out.shape[3]
    for t in range(8):
        at = pl.multiple_of((2 * t + table[2]) * part, part)
        out[t, 0] = up[0, :, pl.ds(at, part)]


def pack_call(table, up_maps):
    _, rank, width = up_maps.shape
    part = width // 16
    return pl.pallas_call(
        pack_kernel,
        grid_spec=pltpu.PrefetchScalarGridSpec(
            num_scalar_prefetch=1,
            grid=(2,),
            in_specs=[pl.BlockSpec((1, rank, width), lambda s, t: (t[s], 0, 0))],
            out_specs=pl.BlockSpec((8, 1, rank, part), lambda s, t: (0, s, 0, 0)),
        ),
        out_shape=jax.ShapeDtypeStruct((8, 2, rank, part), jnp.bfloat16),
        name="pack",
        **settings(),
    )(table, pltpu.with_memory_space_constraint(up_maps, pltpu.HBM))


def take_kernel(table, got, out):
    out[...] = got[...]


def take_call(table, got):
    _, rank, part = got.shape
    return pl.pallas_call(
        take_kernel,
        grid_spec=pltpu.PrefetchScalarGridSpec(
            num_scalar_prefetch=1,
            grid=(8,),
            in_specs=[pl.BlockSpec((1, rank, part), lambda b, t: (t[b], 0, 0))],
            out_specs=pl.BlockSpec((1, rank, part), lambda b, t: (b, 0, 0)),
        ),
        out_shape=jax.ShapeDtypeStruct((8, rank, part), jnp.bfloat16),
        name="take",
        **settings(),
    )(table, got)


def finish_kernel(table, *refs):
    bases, gathered, refs = refs[:8], refs[8:12], refs[12:]
    up_mine, up_other, out, base, shrunk, rows, base_sems, sems = refs
    part = up_mine.shape[2]
    group = table[3, 0]
    fetches = [pltpu.make_async_copy(bases[g], base.at[g], base_sems.at[g]) for g in range(8)]
    for fetch in fetches:
        fetch.start()
    for i, pair in enumerate(gathered):
        shrunk[pl.ds(2 * i, 2)] = pair[...]
    copies = []
    for i in range(8):
        block = table[0, i]
        both = shrunk[table[1, i]].astype(jnp.float32)
        value = jnp.where(table[2, i] > 0, both[:, 64:], both[:, :64]).astype(jnp.bfloat16)
        fetches[i].wait()
        for up, side in ((up_mine, group), (up_other, 1 - group)):
            cut = pl.ds(pl.multiple_of(side * part, part), part)
            grown = jnp.dot(value, up[block], preferred_element_type=jnp.float32)
            rows[i, :, cut] = (base[i, :, cut] + 0.5 * grown).astype(rows.dtype)
        to = pl.ds(pl.multiple_of(block * BLOCK, BLOCK), BLOCK)
        copies.append(pltpu.make_async_copy(rows.at[i], out.at[to], sems.at[i]))
        copies[-1].start()
    for copy in copies:
        copy.wait()


def finish_call(table, bases, gathered, up_mine, up_other):
    columns = bases[0].shape[1]
    return pl.pallas_call(
        finish_kernel,
        in_specs=[pl.BlockSpec(memory_space=pltpu.SMEM)]
        + [pl.BlockSpec(memory_space=pl.ANY)] * 8
        + in_vmem(6),
        out_specs=pl.BlockSpec(memory_space=pltpu.HBM),
        out_shape=jax.ShapeDtypeStruct((8 * BLOCK, columns), jnp.bfloat16),
        scratch_shapes=[
            pltpu.VMEM((8, BLOCK, columns), jnp.float32),
            pltpu.VMEM((8,) + gathered[0].shape[1:], jnp.bfloat16),
            pltpu.VMEM((8, BLOCK, columns), jnp.bfloat16),
            pltpu.SemaphoreType.DMA((8,)),
            pltpu.SemaphoreType.DMA((8,)),
        ],
        name="finish",
        **settings(),
    )(
        table,
        *[pltpu.with_memory_space_constraint(base, pltpu.HBM) for base in bases],
        *gathered,
        up_mine,
        up_other,
    )


def chain_body(
    tokens, query_weight, adapter_down_maps, adapter_up_maps, adapter_home_slot, adapter_per_block
):
    me = lax.axis_index("tensor")
    z, y = me // 2, me % 2
    store = lax.axis_index("store")
    group = lax.axis_index("groups")
    myself = me * 2 + store
    held, rank, width = adapter_down_maps.shape
    rows = tokens[0]

    flight = (send(rows, AHEAD), send(rows, BACK))

    store_slots = find_slots(adapter_home_slot, adapter_per_block)
    owner = store_slots // held
    inside = store_slots % held
    picked = jnp.max(jnp.where(owner == myself, inside, 0), axis=1)
    owner_row = lax.dynamic_index_in_dim(owner, store, 0, keepdims=False).astype(jnp.int32)
    pick_own = lax.dynamic_index_in_dim(picked, store, 0, keepdims=False)
    pick_lent = lax.dynamic_index_in_dim(picked, 1 - store, 0, keepdims=False)

    down_own = lax.dynamic_index_in_dim(adapter_down_maps, pick_own, 0, keepdims=False)
    down_lent = lax.dynamic_index_in_dim(adapter_down_maps, pick_lent, 0, keepdims=False)
    up_sent = pack_call(jnp.concatenate([picked, group[None]]).astype(jnp.int32), adapter_up_maps)

    position = jnp.where(y == 0, z, 7 - z)
    places = jnp.stack([position + d for d in (0, -1, 1, -2, 2, -3, 3, 4)]) % 8
    blocks = jnp.where(places < 4, 2 * places, 15 - 2 * places).astype(jnp.int32)
    hit = blocks[:, None] == jnp.arange(8, dtype=jnp.int32)[None, :]
    owners = jnp.sum(jnp.where(hit, owner_row[None, :], 0), axis=1)
    table = jnp.stack([owners == myself, owners == me * 2 + 1 - store]).astype(jnp.int32)

    bases = []
    shrunk = jnp.zeros((BLOCK, 2 * rank), jnp.bfloat16)
    groups = [[rows]]
    extra = (down_own, down_lent, up_sent)
    for k in range(4):
        (ahead, back), bases, shrunk, extra = lax.optimization_barrier(
            (flight, bases, shrunk, extra)
        )
        if k == 3:
            break
        cut = (slice(None), slice(None)) if k < 2 else (slice(0, HALF), slice(HALF, BLOCK))
        flight = (send(ahead[cut[0]], AHEAD), send(back[cut[1]], BACK))
        groups += [[ahead], [back]]
        if k == 0:
            down_swapped = swap(extra[1], "store")
        if k == 1:
            weights = pin_call(query_weight, extra[0], down_swapped)
        for g in {0: (), 1: range(3), 2: range(3, 7)}[k]:
            base, shrunk = rows_call(g, table, weights, groups[g], shrunk)
            bases.append(base)
    up_got = lax.all_to_all(
        extra[2].reshape(16, rank, -1), ("tensor", "store"), split_axis=0, concat_axis=0, tiled=True
    )
    base, shrunk = rows_call(7, table, weights, [ahead, back], shrunk)
    bases.append(base)

    across = send(shrunk, ACROSS)
    pair = jnp.stack([shrunk, across])
    everyone = [pair] + [send(pair, pairs) for pairs in ALONG]
    up_got, _ = lax.optimization_barrier((up_got, across))
    up_mine = take_call(owner_row, up_got)
    up_other = swap(up_mine, "groups")
    home, core = owners // 2, owners % 2
    where = 2 * ((home // 2) ^ z) + ((home % 2) ^ y)
    table = jnp.stack([blocks, where, core != store, jnp.broadcast_to(group, (8,))])
    return finish_call(table.astype(jnp.int32), bases, everyone, up_mine, up_other)[None]


def body(tokens, *rest):
    sizes = tuple(lax.axis_size(name) for name in ("groups", "tensor", "store"))
    fits = sizes == (2, 8, 2) and tokens.shape[1] == BLOCK
    return (chain_body if fits else general_body)(tokens, *rest)


def solution(mesh):
    placed = (
        P(("groups", "store"), "tensor", None),
        P(None, "tensor"),
        P(("tensor", "store"), None, None),
        P(("tensor", "store"), None, None),
        P(),
        P(),
    )
    return jax.shard_map(
        body,
        mesh=mesh,
        in_specs=placed,
        out_specs=P(("groups", "store"), None, "tensor"),
        check_vma=False,
    )
```

```python
import functools

import jax
import jax.numpy as jnp
from jax import lax
from jax.experimental import pallas as pl
from jax.experimental.pallas import tpu as pltpu
from jax.sharding import PartitionSpec as P

BLOCK = 128


def find_slots(adapter_home_slot, adapter_per_block):
    catalog = jnp.arange(adapter_home_slot.shape[0], dtype=jnp.int32)
    return jnp.sum(
        jnp.where(
            adapter_per_block[:, :, None] == catalog[None, None, :],
            adapter_home_slot[None, None, :],
            0,
        ),
        axis=2,
    )


def general_body(
    tokens, query_weight, adapter_down_maps, adapter_up_maps, adapter_home_slot, adapter_per_block
):
    shard_count = lax.axis_size("tensor")
    store_count = lax.axis_size("store")
    devices_all = shard_count * store_count
    my_tensor = lax.axis_index("tensor")
    my_store = lax.axis_index("store")
    myself = lax.axis_index(("tensor", "store"))
    held_adapters, rank_index, feature_width = adapter_down_maps.shape
    feature_index = query_weight.shape[1]
    own_rows = tokens[0]
    group_rows = own_rows.shape[0] * shard_count
    blocks = group_rows // BLOCK
    store_slots = find_slots(adapter_home_slot, adapter_per_block)
    owner = store_slots // held_adapters
    inside = store_slots % held_adapters
    picked = jnp.max(jnp.where(owner == myself, inside, -1), axis=1)
    select = (picked[:, None] == jnp.arange(held_adapters, dtype=jnp.int32)[None, :]).astype(
        jnp.bfloat16
    )
    down_map_parts = adapter_down_maps.reshape(
        held_adapters, rank_index, shard_count, feature_index
    )
    up_map_parts = adapter_up_maps.reshape(held_adapters, rank_index, shard_count, feature_index)
    send_down = jnp.einsum(
        "sl,lrtf->tsrf", select, down_map_parts, preferred_element_type=jnp.float32
    ).astype(jnp.bfloat16)
    send_up = jnp.einsum(
        "sl,lrtf->tsrf", select, up_map_parts, preferred_element_type=jnp.float32
    ).astype(jnp.bfloat16)
    recv_down, recv_up = (
        lax.all_to_all(
            sent.reshape(devices_all, rank_index, feature_index),
            ("tensor", "store"),
            split_axis=0,
            concat_axis=0,
            tiled=True,
        )
        for sent in (send_down, send_up)
    )
    owner_row = lax.dynamic_index_in_dim(owner, my_store, 0, keepdims=False)
    source_pick = (owner_row[:, None] == jnp.arange(devices_all, dtype=jnp.int32)[None, :]).astype(
        jnp.bfloat16
    )
    block_down = jnp.einsum(
        "bj,jrf->brf", source_pick, recv_down, preferred_element_type=jnp.float32
    ).astype(jnp.bfloat16)
    block_up = jnp.einsum(
        "bj,jrf->brf", source_pick, recv_up, preferred_element_type=jnp.float32
    ).astype(jnp.bfloat16)
    piece = lax.all_gather(own_rows, "tensor", axis=0, tiled=True)
    product = jnp.dot(piece, query_weight, preferred_element_type=jnp.float32)
    features = lax.dynamic_slice_in_dim(piece, my_tensor * feature_index, feature_index, 1)
    partial_value = jnp.einsum(
        "bnf,brf->bnr",
        features.reshape(blocks, BLOCK, feature_index),
        block_down,
        preferred_element_type=jnp.float32,
    )
    shrunk = lax.psum(partial_value, "tensor").astype(jnp.bfloat16)
    grown = jnp.einsum(
        "bnr,brf->bnf", shrunk, block_up, preferred_element_type=jnp.float32
    ).reshape(group_rows, feature_index)
    query = (product + 0.5 * grown).astype(jnp.bfloat16)
    return query[None]


def both_ways(pairs):
    return pairs + [(b, a) for a, b in pairs]


RING = [0, 2, 4, 6, 7, 5, 3, 1]
AHEAD = [(RING[i], RING[(i + 1) % 8]) for i in range(8)]
BACK = [(b, a) for a, b in AHEAD]
ACROSS = [(i, i ^ 1) for i in range(8)]
ALONG = [[(i, i ^ (2 * d)) for i in range(8)] for d in (1, 2, 3)]
HALF = BLOCK // 2
DEPTH = 1024
VMEM_LIMIT = 16 * 1024 * 1024


def send(value, pairs):
    return lax.ppermute(value, "tensor", pairs)


def swap(value, axis):
    return lax.ppermute(value, axis, [(0, 1), (1, 0)])


def settings():
    return dict(
        compiler_params=pltpu.CompilerParams(vmem_limit_bytes=VMEM_LIMIT),
        cost_estimate=pl.CostEstimate(flops=1, bytes_accessed=1, transcendentals=0),
    )


def in_vmem(count):
    return [pl.BlockSpec(memory_space=pltpu.VMEM)] * count


def pin_kernel(weight, own, swapped, out, sem):
    columns = weight.shape[1]
    copy = pltpu.make_async_copy(weight, out.at[:, pl.ds(0, columns)], sem)
    copy.start()
    for at in range(0, weight.shape[0], DEPTH):
        cut = pl.ds(at, DEPTH)
        out[cut, columns:] = jnp.concatenate([own[:, cut], swapped[:, cut]], axis=0).T
    copy.wait()


def pin_call(weight, own, swapped):
    width, columns = weight.shape
    return pl.pallas_call(
        pin_kernel,
        in_specs=[pl.BlockSpec(memory_space=pl.ANY)] + in_vmem(2),
        out_specs=in_vmem(1)[0],
        out_shape=pltpu.VMEM((width, columns + 2 * own.shape[0]), weight.dtype),
        scratch_shapes=[pltpu.SemaphoreType.DMA],
        name="pin",
        **settings(),
    )(weight, own, swapped)


def rows_kernel(group, table, weights, *refs):
    *pieces, shrunk, base, shrunk_out = refs
    columns = base.shape[1]
    total = None
    for at in range(0, weights.shape[0], DEPTH):
        cut = pl.ds(at, DEPTH)
        x = [p[:, cut] for p in pieces]
        x = x[0] if len(x) == 1 else jnp.concatenate(x, axis=0)
        part = jnp.dot(x, weights[cut, :], preferred_element_type=jnp.float32)
        total = part if total is None else total + part
    base[...] = total[:, :columns]
    lane = lax.broadcasted_iota(jnp.int32, shrunk.shape, 1)
    use = jnp.where(lane < 64, table[0, group], table[1, group])
    small = total[:, columns:].astype(jnp.bfloat16).astype(jnp.float32)
    old = shrunk[...].astype(jnp.float32)
    shrunk_out[...] = jnp.where(use > 0, small, old).astype(jnp.bfloat16)


def rows_call(group, table, weights, pieces, shrunk):
    columns = weights.shape[1] - 128
    operands = [pltpu.with_memory_space_constraint(weights, pltpu.VMEM)] + pieces + [shrunk]
    return pl.pallas_call(
        functools.partial(rows_kernel, group),
        in_specs=[pl.BlockSpec(memory_space=pltpu.SMEM)] + in_vmem(len(operands)),
        out_specs=in_vmem(2),
        out_shape=[
            jax.ShapeDtypeStruct((BLOCK, columns), jnp.float32),
            jax.ShapeDtypeStruct((BLOCK, 128), jnp.bfloat16),
        ],
        name="rows",
        **settings(),
    )(table, *operands)


def pack_kernel(table, up, out):
    part = out.shape[3]
    for t in range(8):
        at = pl.multiple_of((2 * t + table[2]) * part, part)
        out[0, t] = up[0, :, pl.ds(at, part)]


def pack_call(table, up_maps):
    _, rank, width = up_maps.shape
    part = width // 16
    return pl.pallas_call(
        pack_kernel,
        grid_spec=pltpu.PrefetchScalarGridSpec(
            num_scalar_prefetch=1,
            grid=(2,),
            in_specs=[pl.BlockSpec((1, rank, width), lambda s, t: (t[s], 0, 0))],
            out_specs=pl.BlockSpec((1, 8, rank, part), lambda s, t: (s, 0, 0, 0)),
        ),
        out_shape=jax.ShapeDtypeStruct((2, 8, rank, part), jnp.bfloat16),
        name="pack",
        **settings(),
    )(table, pltpu.with_memory_space_constraint(up_maps, pltpu.HBM))


def take_kernel(table, got, out):
    out[...] = got[...]


def take_call(table, got):
    _, rank, part = got.shape
    return pl.pallas_call(
        take_kernel,
        grid_spec=pltpu.PrefetchScalarGridSpec(
            num_scalar_prefetch=1,
            grid=(8,),
            in_specs=[pl.BlockSpec((1, rank, part), lambda b, t: (t[b], 0, 0))],
            out_specs=pl.BlockSpec((1, rank, part), lambda b, t: (b, 0, 0)),
        ),
        out_shape=jax.ShapeDtypeStruct((8, rank, part), jnp.bfloat16),
        name="take",
        **settings(),
    )(table, got)


def finish_kernel(table, *refs):
    bases, gathered, refs = refs[:8], refs[8:12], refs[12:]
    up_mine, up_other, out, base, shrunk, rows, base_sems, sems = refs
    part = up_mine.shape[2]
    group = table[3, 0]
    fetches = [pltpu.make_async_copy(bases[g], base.at[g], base_sems.at[g]) for g in range(8)]
    for fetch in fetches:
        fetch.start()
    for i, pair in enumerate(gathered):
        shrunk[pl.ds(2 * i, 2)] = pair[...]
    copies = []
    for i in range(8):
        block = table[0, i]
        both = shrunk[table[1, i]].astype(jnp.float32)
        value = jnp.where(table[2, i] > 0, both[:, 64:], both[:, :64]).astype(jnp.bfloat16)
        fetches[i].wait()
        for up, side in ((up_mine, group), (up_other, 1 - group)):
            cut = pl.ds(pl.multiple_of(side * part, part), part)
            grown = jnp.dot(value, up[block], preferred_element_type=jnp.float32)
            rows[i, :, cut] = (base[i, :, cut] + 0.5 * grown).astype(rows.dtype)
        to = pl.ds(pl.multiple_of(block * BLOCK, BLOCK), BLOCK)
        copies.append(pltpu.make_async_copy(rows.at[i], out.at[to], sems.at[i]))
        copies[-1].start()
    for copy in copies:
        copy.wait()


def finish_call(table, bases, gathered, up_mine, up_other):
    columns = bases[0].shape[1]
    return pl.pallas_call(
        finish_kernel,
        in_specs=[pl.BlockSpec(memory_space=pltpu.SMEM)]
        + [pl.BlockSpec(memory_space=pl.ANY)] * 8
        + in_vmem(6),
        out_specs=pl.BlockSpec(memory_space=pltpu.HBM),
        out_shape=jax.ShapeDtypeStruct((8 * BLOCK, columns), jnp.bfloat16),
        scratch_shapes=[
            pltpu.VMEM((8, BLOCK, columns), jnp.float32),
            pltpu.VMEM((8,) + gathered[0].shape[1:], jnp.bfloat16),
            pltpu.VMEM((8, BLOCK, columns), jnp.bfloat16),
            pltpu.SemaphoreType.DMA((8,)),
            pltpu.SemaphoreType.DMA((8,)),
        ],
        name="finish",
        **settings(),
    )(
        table,
        *[pltpu.with_memory_space_constraint(base, pltpu.HBM) for base in bases],
        *gathered,
        up_mine,
        up_other,
    )


def chain_body(
    tokens, query_weight, adapter_down_maps, adapter_up_maps, adapter_home_slot, adapter_per_block
):
    me = lax.axis_index("tensor")
    z, y = me // 2, me % 2
    store = lax.axis_index("store")
    group = lax.axis_index("groups")
    myself = me * 2 + store
    held, rank, width = adapter_down_maps.shape
    rows = tokens[0]

    flight = (send(rows, AHEAD), send(rows, BACK))

    store_slots = find_slots(adapter_home_slot, adapter_per_block)
    owner = store_slots // held
    inside = store_slots % held
    picked = jnp.max(jnp.where(owner == myself, inside, 0), axis=1)
    owner_row = lax.dynamic_index_in_dim(owner, store, 0, keepdims=False).astype(jnp.int32)
    pick_own = lax.dynamic_index_in_dim(picked, store, 0, keepdims=False)
    pick_lent = lax.dynamic_index_in_dim(picked, 1 - store, 0, keepdims=False)

    down_own = lax.dynamic_index_in_dim(adapter_down_maps, pick_own, 0, keepdims=False)
    down_lent = lax.dynamic_index_in_dim(adapter_down_maps, pick_lent, 0, keepdims=False)
    choice = jnp.stack([pick_own, pick_lent, group.astype(pick_own.dtype)]).astype(jnp.int32)
    up_sent = pack_call(choice, adapter_up_maps)

    position = jnp.where(y == 0, z, 7 - z)
    places = jnp.stack([position + d for d in (0, -1, 1, -2, 2, -3, 3, 4)]) % 8
    blocks = jnp.where(places < 4, 2 * places, 15 - 2 * places).astype(jnp.int32)
    hit = blocks[:, None] == jnp.arange(8, dtype=jnp.int32)[None, :]
    owners = jnp.sum(jnp.where(hit, owner_row[None, :], 0), axis=1)
    table = jnp.stack([owners == myself, owners == me * 2 + 1 - store]).astype(jnp.int32)

    bases = []
    shrunk = jnp.zeros((BLOCK, 2 * rank), jnp.bfloat16)
    groups = [[rows]]
    extra = (down_own, down_lent, up_sent)
    for k in range(4):
        (ahead, back), bases, shrunk, extra = lax.optimization_barrier(
            (flight, bases, shrunk, extra)
        )
        if k == 3:
            break
        cut = (slice(None), slice(None)) if k < 2 else (slice(0, HALF), slice(HALF, BLOCK))
        flight = (send(ahead[cut[0]], AHEAD), send(back[cut[1]], BACK))
        groups += [[ahead], [back]]
        if k == 0:
            down_own, down_lent, up_sent = extra
            extra = (down_own, swap(down_lent, "store"), up_sent[0], swap(up_sent[1], "store"))
        if k == 1:
            weights = pin_call(query_weight, extra[0], extra[1])
            pieces = jnp.stack([extra[2], extra[3]], axis=1)

            def piece(other):
                return lax.dynamic_index_in_dim(pieces, me ^ other, 0, keepdims=False)

            extra = [piece(0)] + [
                send(piece(d), [(i, i ^ d) for i in range(8)]) for d in (1, 2, 4, 6, 3, 5, 7)
            ]
        if k == 2:
            found = [extra[n] for n in (0, 1, 2, 5, 3, 6, 4, 7)]
            found = jnp.stack(found).reshape(16, rank, -1)
            home, core = owner_row // 2, owner_row % 2
            chosen = 2 * (home ^ me) + jnp.where(core == store, 0, 1)
            up_mine = take_call(chosen.astype(jnp.int32), found)
            extra = (up_mine, swap(up_mine, "groups"))
        for g in {0: (), 1: range(3), 2: range(3, 7)}[k]:
            base, shrunk = rows_call(g, table, weights, groups[g], shrunk)
            bases.append(base)
    up_mine, up_other = extra
    base, shrunk = rows_call(7, table, weights, [ahead, back], shrunk)
    bases.append(base)

    pair = jnp.stack([shrunk, send(shrunk, ACROSS)])
    everyone = [pair] + [send(pair, pairs) for pairs in ALONG]
    home, core = owners // 2, owners % 2
    where = 2 * ((home // 2) ^ z) + ((home % 2) ^ y)
    table = jnp.stack([blocks, where, core != store, jnp.broadcast_to(group, (8,))])
    return finish_call(table.astype(jnp.int32), bases, everyone, up_mine, up_other)[None]


def body(tokens, *rest):
    sizes = tuple(lax.axis_size(name) for name in ("groups", "tensor", "store"))
    fits = sizes == (2, 8, 2) and tokens.shape[1] == BLOCK
    return (chain_body if fits else general_body)(tokens, *rest)


def solution(mesh):
    placed = (
        P(("groups", "store"), "tensor", None),
        P(None, "tensor"),
        P(("tensor", "store"), None, None),
        P(("tensor", "store"), None, None),
        P(),
        P(),
    )
    return jax.shard_map(
        body,
        mesh=mesh,
        in_specs=placed,
        out_specs=P(("groups", "store"), None, "tensor"),
        check_vma=False,
    )
```

```python
import functools

import jax
import jax.numpy as jnp
from jax import lax
from jax.experimental import pallas as pl
from jax.experimental.pallas import tpu as pltpu
from jax.sharding import PartitionSpec as P

BLOCK = 128


def find_slots(adapter_home_slot, adapter_per_block):
    catalog = jnp.arange(adapter_home_slot.shape[0], dtype=jnp.int32)
    return jnp.sum(
        jnp.where(
            adapter_per_block[:, :, None] == catalog[None, None, :],
            adapter_home_slot[None, None, :],
            0,
        ),
        axis=2,
    )


def general_body(
    tokens, query_weight, adapter_down_maps, adapter_up_maps, adapter_home_slot, adapter_per_block
):
    shard_count = lax.axis_size("tensor")
    store_count = lax.axis_size("store")
    devices_all = shard_count * store_count
    my_tensor = lax.axis_index("tensor")
    my_store = lax.axis_index("store")
    myself = lax.axis_index(("tensor", "store"))
    held_adapters, rank_index, feature_width = adapter_down_maps.shape
    feature_index = query_weight.shape[1]
    own_rows = tokens[0]
    group_rows = own_rows.shape[0] * shard_count
    blocks = group_rows // BLOCK
    store_slots = find_slots(adapter_home_slot, adapter_per_block)
    owner = store_slots // held_adapters
    inside = store_slots % held_adapters
    picked = jnp.max(jnp.where(owner == myself, inside, -1), axis=1)
    select = (picked[:, None] == jnp.arange(held_adapters, dtype=jnp.int32)[None, :]).astype(
        jnp.bfloat16
    )
    down_map_parts = adapter_down_maps.reshape(
        held_adapters, rank_index, shard_count, feature_index
    )
    up_map_parts = adapter_up_maps.reshape(held_adapters, rank_index, shard_count, feature_index)
    send_down = jnp.einsum(
        "sl,lrtf->tsrf", select, down_map_parts, preferred_element_type=jnp.float32
    ).astype(jnp.bfloat16)
    send_up = jnp.einsum(
        "sl,lrtf->tsrf", select, up_map_parts, preferred_element_type=jnp.float32
    ).astype(jnp.bfloat16)
    recv_down, recv_up = (
        lax.all_to_all(
            sent.reshape(devices_all, rank_index, feature_index),
            ("tensor", "store"),
            split_axis=0,
            concat_axis=0,
            tiled=True,
        )
        for sent in (send_down, send_up)
    )
    owner_row = lax.dynamic_index_in_dim(owner, my_store, 0, keepdims=False)
    source_pick = (owner_row[:, None] == jnp.arange(devices_all, dtype=jnp.int32)[None, :]).astype(
        jnp.bfloat16
    )
    block_down = jnp.einsum(
        "bj,jrf->brf", source_pick, recv_down, preferred_element_type=jnp.float32
    ).astype(jnp.bfloat16)
    block_up = jnp.einsum(
        "bj,jrf->brf", source_pick, recv_up, preferred_element_type=jnp.float32
    ).astype(jnp.bfloat16)
    piece = lax.all_gather(own_rows, "tensor", axis=0, tiled=True)
    product = jnp.dot(piece, query_weight, preferred_element_type=jnp.float32)
    features = lax.dynamic_slice_in_dim(piece, my_tensor * feature_index, feature_index, 1)
    partial_value = jnp.einsum(
        "bnf,brf->bnr",
        features.reshape(blocks, BLOCK, feature_index),
        block_down,
        preferred_element_type=jnp.float32,
    )
    shrunk = lax.psum(partial_value, "tensor").astype(jnp.bfloat16)
    grown = jnp.einsum(
        "bnr,brf->bnf", shrunk, block_up, preferred_element_type=jnp.float32
    ).reshape(group_rows, feature_index)
    query = (product + 0.5 * grown).astype(jnp.bfloat16)
    return query[None]


def both_ways(pairs):
    return pairs + [(b, a) for a, b in pairs]


RING = [0, 2, 4, 6, 7, 5, 3, 1]
AHEAD = [(RING[i], RING[(i + 1) % 8]) for i in range(8)]
BACK = [(b, a) for a, b in AHEAD]
ACROSS = [(i, i ^ 1) for i in range(8)]
ALONG = [[(i, i ^ (2 * d)) for i in range(8)] for d in (1, 2, 3)]
HALF = BLOCK // 2
DEPTH = 1024
VMEM_LIMIT = 16 * 1024 * 1024


def send(value, pairs):
    return lax.ppermute(value, "tensor", pairs)


def swap(value, axis):
    return lax.ppermute(value, axis, [(0, 1), (1, 0)])


def settings():
    return dict(
        compiler_params=pltpu.CompilerParams(vmem_limit_bytes=VMEM_LIMIT),
        cost_estimate=pl.CostEstimate(flops=1, bytes_accessed=1, transcendentals=0),
    )


def in_vmem(count):
    return [pl.BlockSpec(memory_space=pltpu.VMEM)] * count


def pin_kernel(weight, own, swapped, out, sem):
    columns = weight.shape[1]
    copy = pltpu.make_async_copy(weight, out.at[:, pl.ds(0, columns)], sem)
    copy.start()
    for at in range(0, weight.shape[0], DEPTH):
        cut = pl.ds(at, DEPTH)
        out[cut, columns:] = jnp.concatenate([own[:, cut], swapped[:, cut]], axis=0).T
    copy.wait()


def pin_call(weight, own, swapped):
    width, columns = weight.shape
    return pl.pallas_call(
        pin_kernel,
        in_specs=[pl.BlockSpec(memory_space=pl.ANY)] + in_vmem(2),
        out_specs=in_vmem(1)[0],
        out_shape=pltpu.VMEM((width, columns + 2 * own.shape[0]), weight.dtype),
        scratch_shapes=[pltpu.SemaphoreType.DMA],
        name="pin",
        **settings(),
    )(weight, own, swapped)


def rows_kernel(group, table, weights, *refs):
    *pieces, shrunk, base, shrunk_out = refs
    columns = base.shape[1]
    total = None
    for at in range(0, weights.shape[0], DEPTH):
        cut = pl.ds(at, DEPTH)
        x = [p[:, cut] for p in pieces]
        x = x[0] if len(x) == 1 else jnp.concatenate(x, axis=0)
        part = jnp.dot(x, weights[cut, :], preferred_element_type=jnp.float32)
        total = part if total is None else total + part
    base[...] = total[:, :columns]
    lane = lax.broadcasted_iota(jnp.int32, shrunk.shape, 1)
    row = lax.broadcasted_iota(jnp.int32, shrunk.shape, 0)
    use = jnp.where(
        row < HALF,
        jnp.where(lane < 64, table[0, 2 * group], table[1, 2 * group]),
        jnp.where(lane < 64, table[0, 2 * group + 1], table[1, 2 * group + 1]),
    )
    small = total[:, columns:].astype(jnp.bfloat16).astype(jnp.float32)
    old = shrunk[...].astype(jnp.float32)
    shrunk_out[...] = jnp.where(use > 0, small, old).astype(jnp.bfloat16)


def rows_call(group, table, weights, pieces, shrunk):
    columns = weights.shape[1] - 128
    operands = [pltpu.with_memory_space_constraint(weights, pltpu.VMEM)] + pieces + [shrunk]
    return pl.pallas_call(
        functools.partial(rows_kernel, group),
        in_specs=[pl.BlockSpec(memory_space=pltpu.SMEM)] + in_vmem(len(operands)),
        out_specs=in_vmem(2),
        out_shape=[
            jax.ShapeDtypeStruct((BLOCK, columns), jnp.float32),
            jax.ShapeDtypeStruct((BLOCK, 128), jnp.bfloat16),
        ],
        name="rows",
        **settings(),
    )(table, *operands)


def pack_kernel(table, up, out):
    part = out.shape[3]
    for t in range(8):
        at = pl.multiple_of((2 * t + table[2]) * part, part)
        out[0, t] = up[0, :, pl.ds(at, part)]


def pack_call(table, up_maps):
    _, rank, width = up_maps.shape
    part = width // 16
    return pl.pallas_call(
        pack_kernel,
        grid_spec=pltpu.PrefetchScalarGridSpec(
            num_scalar_prefetch=1,
            grid=(2,),
            in_specs=[pl.BlockSpec((1, rank, width), lambda s, t: (t[s], 0, 0))],
            out_specs=pl.BlockSpec((1, 8, rank, part), lambda s, t: (s, 0, 0, 0)),
        ),
        out_shape=jax.ShapeDtypeStruct((2, 8, rank, part), jnp.bfloat16),
        name="pack",
        **settings(),
    )(table, pltpu.with_memory_space_constraint(up_maps, pltpu.HBM))


def take_kernel(table, got, out):
    out[...] = got[...]


def take_call(table, got):
    _, rank, part = got.shape
    return pl.pallas_call(
        take_kernel,
        grid_spec=pltpu.PrefetchScalarGridSpec(
            num_scalar_prefetch=1,
            grid=(8,),
            in_specs=[pl.BlockSpec((1, rank, part), lambda b, t: (t[b], 0, 0))],
            out_specs=pl.BlockSpec((1, rank, part), lambda b, t: (b, 0, 0)),
        ),
        out_shape=jax.ShapeDtypeStruct((8, rank, part), jnp.bfloat16),
        name="take",
        **settings(),
    )(table, got)


def finish_kernel(table, *refs):
    bases, gathered, refs = refs[:8], refs[8:12], refs[12:]
    up_mine, up_other, out, base, shrunk, rows, base_sems, sems = refs
    part = up_mine.shape[2]
    group = table[3, 0]
    fetches = [pltpu.make_async_copy(bases[g], base.at[g], base_sems.at[g]) for g in range(8)]
    for fetch in fetches:
        fetch.start()
    for i, pair in enumerate(gathered):
        shrunk[pl.ds(2 * i, 2)] = pair[...]
    copies = []
    for i in range(16):
        block, half = table[0, i], i % 2
        if half == 0:
            fetches[i // 2].wait()
        own = pl.ds(half * HALF, HALF)
        both = shrunk[table[1, i], own, :].astype(jnp.float32)
        value = jnp.where(table[2, i] > 0, both[:, 64:], both[:, :64]).astype(jnp.bfloat16)
        for up, side in ((up_mine, group), (up_other, 1 - group)):
            cut = pl.ds(pl.multiple_of(side * part, part), part)
            grown = jnp.dot(value, up[block], preferred_element_type=jnp.float32)
            rows[i, :, cut] = (base[i // 2, own, cut] + 0.5 * grown).astype(rows.dtype)
        to = pl.ds(pl.multiple_of((2 * block + half) * HALF, HALF), HALF)
        copies.append(pltpu.make_async_copy(rows.at[i], out.at[to], sems.at[i]))
        copies[-1].start()
    for copy in copies:
        copy.wait()


def finish_call(table, bases, gathered, up_mine, up_other):
    columns = bases[0].shape[1]
    return pl.pallas_call(
        finish_kernel,
        in_specs=[pl.BlockSpec(memory_space=pltpu.SMEM)]
        + [pl.BlockSpec(memory_space=pl.ANY)] * 8
        + in_vmem(6),
        out_specs=pl.BlockSpec(memory_space=pltpu.HBM),
        out_shape=jax.ShapeDtypeStruct((8 * BLOCK, columns), jnp.bfloat16),
        scratch_shapes=[
            pltpu.VMEM((8, BLOCK, columns), jnp.float32),
            pltpu.VMEM((8,) + gathered[0].shape[1:], jnp.bfloat16),
            pltpu.VMEM((16, HALF, columns), jnp.bfloat16),
            pltpu.SemaphoreType.DMA((8,)),
            pltpu.SemaphoreType.DMA((16,)),
        ],
        name="finish",
        **settings(),
    )(
        table,
        *[pltpu.with_memory_space_constraint(base, pltpu.HBM) for base in bases],
        *gathered,
        up_mine,
        up_other,
    )


def chain_body(
    tokens, query_weight, adapter_down_maps, adapter_up_maps, adapter_home_slot, adapter_per_block
):
    me = lax.axis_index("tensor")
    z, y = me // 2, me % 2
    store = lax.axis_index("store")
    group = lax.axis_index("groups")
    myself = me * 2 + store
    held, rank, width = adapter_down_maps.shape
    rows = tokens[0]
    halves = [rows[:HALF], rows[HALF:]]

    ahead, back = list(halves), list(halves[::-1])

    def ring(k):
        return send(ahead[k], AHEAD), send(back[k], BACK)

    flight = {0: ring(0), 1: ring(1)}

    store_slots = find_slots(adapter_home_slot, adapter_per_block)
    owner = store_slots // held
    inside = store_slots % held
    picked = jnp.max(jnp.where(owner == myself, inside, 0), axis=1)
    owner_row = lax.dynamic_index_in_dim(owner, store, 0, keepdims=False).astype(jnp.int32)
    pick_own = lax.dynamic_index_in_dim(picked, store, 0, keepdims=False)
    pick_lent = lax.dynamic_index_in_dim(picked, 1 - store, 0, keepdims=False)

    down_own = lax.dynamic_index_in_dim(adapter_down_maps, pick_own, 0, keepdims=False)
    down_lent = lax.dynamic_index_in_dim(adapter_down_maps, pick_lent, 0, keepdims=False)
    choice = jnp.stack([pick_own, pick_lent, group.astype(pick_own.dtype)]).astype(jnp.int32)
    up_sent = pack_call(choice, adapter_up_maps)

    position = jnp.where(y == 0, z, 7 - z)
    places = []
    for k in range(8):
        step = (k + 1) // 2
        places += [position - step, position + step] if k % 2 else [position + step, position - step]
    places = jnp.stack(places) % 8
    blocks = jnp.where(places < 4, 2 * places, 15 - 2 * places).astype(jnp.int32)
    hit = blocks[:, None] == jnp.arange(8, dtype=jnp.int32)[None, :]
    owners = jnp.sum(jnp.where(hit, owner_row[None, :], 0), axis=1)
    table = jnp.stack([owners == myself, owners == me * 2 + 1 - store]).astype(jnp.int32)

    def piece(other):
        return lax.dynamic_index_in_dim(pieces, me ^ other, 0, keepdims=False)

    def to_chip(other):
        return send(piece(other), [(i, i ^ other) for i in range(8)])

    def arrive(got):
        ahead.append(got[0])
        back.append(got[1])
        step = len(ahead) - 2
        groups.append(list(got) if step % 2 else list(got[::-1]))

    groups = [[rows]]
    got, ahead, back, down_own, down_lent, up_sent = lax.optimization_barrier(
        (flight.pop(0), ahead, back, down_own, down_lent, up_sent)
    )
    arrive(got)
    down_swapped = swap(down_lent, "store")
    pieces = jnp.stack([up_sent[0], swap(up_sent[1], "store")], axis=1)
    ups = {0: piece(0), 7: to_chip(7), 6: to_chip(6), 5: to_chip(5)}
    got, ahead, back, down_own, down_swapped, pieces = lax.optimization_barrier(
        (flight.pop(1), ahead, back, down_own, down_swapped, pieces)
    )
    arrive(got)
    far, pieces = lax.optimization_barrier(({d: ups[d] for d in (0, 5, 6, 7)}, pieces))
    ups = far | {d: to_chip(d) for d in (4, 3, 2, 1)}
    ups, ahead, back, down_own, down_swapped = lax.optimization_barrier(
        (ups, ahead, back, down_own, down_swapped)
    )
    flight.update({2: ring(2), 3: ring(3)})
    weights = pin_call(query_weight, down_own, down_swapped)

    bases = []
    shrunk = jnp.zeros((BLOCK, 2 * rank), jnp.bfloat16)

    def work(shrunk, count):
        for g in range(len(bases), min(len(bases) + count, len(groups), 7)):
            base, shrunk = rows_call(g, table, weights, groups[g], shrunk)
            bases.append(base)
        return shrunk

    shrunk = work(shrunk, 2)
    for k in range(2, 7):
        got, ahead, back, bases, shrunk = lax.optimization_barrier(
            (flight.pop(k), ahead, back, bases, shrunk)
        )
        arrive(got)
        if k + 2 < 7:
            flight[k + 2] = ring(k + 2)
        if k == 4:
            found = jnp.stack([ups[d] for d in range(8)]).reshape(16, rank, -1)
            home, core = owner_row // 2, owner_row % 2
            chosen = 2 * (home ^ me) + jnp.where(core == store, 0, 1)
            up_mine = take_call(chosen.astype(jnp.int32), found)
            up_other = swap(up_mine, "groups")
        shrunk = work(shrunk, 2)
    base, shrunk = rows_call(7, table, weights, groups[7], shrunk)
    bases.append(base)

    pair = jnp.stack([shrunk, send(shrunk, ACROSS)])
    everyone = [pair] + [send(pair, pairs) for pairs in ALONG]
    home, core = owners // 2, owners % 2
    where = 2 * ((home // 2) ^ z) + ((home % 2) ^ y)
    table = jnp.stack([blocks, where, core != store, jnp.broadcast_to(group, (16,))])
    return finish_call(table.astype(jnp.int32), bases, everyone, up_mine, up_other)[None]


def body(tokens, *rest):
    sizes = tuple(lax.axis_size(name) for name in ("groups", "tensor", "store"))
    fits = sizes == (2, 8, 2) and tokens.shape[1] == BLOCK
    return (chain_body if fits else general_body)(tokens, *rest)


def solution(mesh):
    placed = (
        P(("groups", "store"), "tensor", None),
        P(None, "tensor"),
        P(("tensor", "store"), None, None),
        P(("tensor", "store"), None, None),
        P(),
        P(),
    )
    return jax.shard_map(
        body,
        mesh=mesh,
        in_specs=placed,
        out_specs=P(("groups", "store"), None, "tensor"),
        check_vma=False,
    )
```

```python
import functools

import jax
import jax.numpy as jnp
from jax import lax
from jax.experimental import pallas as pl
from jax.experimental.pallas import tpu as pltpu
from jax.sharding import PartitionSpec as P

BLOCK = 128


def find_slots(adapter_home_slot, adapter_per_block):
    catalog = jnp.arange(adapter_home_slot.shape[0], dtype=jnp.int32)
    return jnp.sum(
        jnp.where(
            adapter_per_block[:, :, None] == catalog[None, None, :],
            adapter_home_slot[None, None, :],
            0,
        ),
        axis=2,
    )


def general_body(
    tokens, query_weight, adapter_down_maps, adapter_up_maps, adapter_home_slot, adapter_per_block
):
    shard_count = lax.axis_size("tensor")
    store_count = lax.axis_size("store")
    devices_all = shard_count * store_count
    my_tensor = lax.axis_index("tensor")
    my_store = lax.axis_index("store")
    myself = lax.axis_index(("tensor", "store"))
    held_adapters, rank_index, feature_width = adapter_down_maps.shape
    feature_index = query_weight.shape[1]
    own_rows = tokens[0]
    group_rows = own_rows.shape[0] * shard_count
    blocks = group_rows // BLOCK
    store_slots = find_slots(adapter_home_slot, adapter_per_block)
    owner = store_slots // held_adapters
    inside = store_slots % held_adapters
    picked = jnp.max(jnp.where(owner == myself, inside, -1), axis=1)
    select = (picked[:, None] == jnp.arange(held_adapters, dtype=jnp.int32)[None, :]).astype(
        jnp.bfloat16
    )
    down_map_parts = adapter_down_maps.reshape(
        held_adapters, rank_index, shard_count, feature_index
    )
    up_map_parts = adapter_up_maps.reshape(held_adapters, rank_index, shard_count, feature_index)
    send_down = jnp.einsum(
        "sl,lrtf->tsrf", select, down_map_parts, preferred_element_type=jnp.float32
    ).astype(jnp.bfloat16)
    send_up = jnp.einsum(
        "sl,lrtf->tsrf", select, up_map_parts, preferred_element_type=jnp.float32
    ).astype(jnp.bfloat16)
    recv_down, recv_up = (
        lax.all_to_all(
            sent.reshape(devices_all, rank_index, feature_index),
            ("tensor", "store"),
            split_axis=0,
            concat_axis=0,
            tiled=True,
        )
        for sent in (send_down, send_up)
    )
    owner_row = lax.dynamic_index_in_dim(owner, my_store, 0, keepdims=False)
    source_pick = (owner_row[:, None] == jnp.arange(devices_all, dtype=jnp.int32)[None, :]).astype(
        jnp.bfloat16
    )
    block_down = jnp.einsum(
        "bj,jrf->brf", source_pick, recv_down, preferred_element_type=jnp.float32
    ).astype(jnp.bfloat16)
    block_up = jnp.einsum(
        "bj,jrf->brf", source_pick, recv_up, preferred_element_type=jnp.float32
    ).astype(jnp.bfloat16)
    piece = lax.all_gather(own_rows, "tensor", axis=0, tiled=True)
    product = jnp.dot(piece, query_weight, preferred_element_type=jnp.float32)
    features = lax.dynamic_slice_in_dim(piece, my_tensor * feature_index, feature_index, 1)
    partial_value = jnp.einsum(
        "bnf,brf->bnr",
        features.reshape(blocks, BLOCK, feature_index),
        block_down,
        preferred_element_type=jnp.float32,
    )
    shrunk = lax.psum(partial_value, "tensor").astype(jnp.bfloat16)
    grown = jnp.einsum(
        "bnr,brf->bnf", shrunk, block_up, preferred_element_type=jnp.float32
    ).reshape(group_rows, feature_index)
    query = (product + 0.5 * grown).astype(jnp.bfloat16)
    return query[None]


def both_ways(pairs):
    return pairs + [(b, a) for a, b in pairs]


RING = [0, 2, 4, 6, 7, 5, 3, 1]
AHEAD = [(RING[i], RING[(i + 1) % 8]) for i in range(8)]
BACK = [(b, a) for a, b in AHEAD]
ACROSS = [(i, i ^ 1) for i in range(8)]
ALONG = [[(i, i ^ (2 * d)) for i in range(8)] for d in (1, 2, 3)]
HALF = BLOCK // 2
DEPTH = 1024
VMEM_LIMIT = 16 * 1024 * 1024


def send(value, pairs):
    return lax.ppermute(value, "tensor", pairs)


def swap(value, axis):
    return lax.ppermute(value, axis, [(0, 1), (1, 0)])


def settings():
    return dict(
        compiler_params=pltpu.CompilerParams(vmem_limit_bytes=VMEM_LIMIT),
        cost_estimate=pl.CostEstimate(flops=1, bytes_accessed=1, transcendentals=0),
    )


def in_vmem(count):
    return [pl.BlockSpec(memory_space=pltpu.VMEM)] * count


def pin_kernel(weight, own, swapped, out, sem):
    columns = weight.shape[1]
    copy = pltpu.make_async_copy(weight, out.at[:, pl.ds(0, columns)], sem)
    copy.start()
    for at in range(0, weight.shape[0], DEPTH):
        cut = pl.ds(at, DEPTH)
        out[cut, columns:] = jnp.concatenate([own[:, cut], swapped[:, cut]], axis=0).T
    copy.wait()


def pin_call(weight, own, swapped):
    width, columns = weight.shape
    return pl.pallas_call(
        pin_kernel,
        in_specs=[pl.BlockSpec(memory_space=pl.ANY)] + in_vmem(2),
        out_specs=in_vmem(1)[0],
        out_shape=pltpu.VMEM((width, columns + 2 * own.shape[0]), weight.dtype),
        scratch_shapes=[pltpu.SemaphoreType.DMA],
        name="pin",
        **settings(),
    )(weight, own, swapped)


def rows_kernel(group, table, weights, *refs):
    *pieces, shrunk, base, shrunk_out = refs
    columns = base.shape[1]
    total = None
    for at in range(0, weights.shape[0], DEPTH):
        cut = pl.ds(at, DEPTH)
        x = [p[:, cut] for p in pieces]
        x = x[0] if len(x) == 1 else jnp.concatenate(x, axis=0)
        part = jnp.dot(x, weights[cut, :], preferred_element_type=jnp.float32)
        total = part if total is None else total + part
    base[...] = total[:, :columns]
    lane = lax.broadcasted_iota(jnp.int32, shrunk.shape, 1)
    row = lax.broadcasted_iota(jnp.int32, shrunk.shape, 0)
    use = jnp.where(
        row < HALF,
        jnp.where(lane < 64, table[0, 2 * group], table[1, 2 * group]),
        jnp.where(lane < 64, table[0, 2 * group + 1], table[1, 2 * group + 1]),
    )
    small = total[:, columns:].astype(jnp.bfloat16).astype(jnp.float32)
    old = shrunk[...].astype(jnp.float32)
    shrunk_out[...] = jnp.where(use > 0, small, old).astype(jnp.bfloat16)


def rows_call(group, table, weights, pieces, shrunk):
    columns = weights.shape[1] - 128
    operands = [pltpu.with_memory_space_constraint(weights, pltpu.VMEM)] + pieces + [shrunk]
    return pl.pallas_call(
        functools.partial(rows_kernel, group),
        in_specs=[pl.BlockSpec(memory_space=pltpu.SMEM)] + in_vmem(len(operands)),
        out_specs=in_vmem(2),
        out_shape=[
            jax.ShapeDtypeStruct((BLOCK, columns), jnp.float32),
            jax.ShapeDtypeStruct((BLOCK, 128), jnp.bfloat16),
        ],
        name="rows",
        **settings(),
    )(table, *operands)


def pack_kernel(table, up, out):
    part = out.shape[3]
    for t in range(8):
        at = pl.multiple_of((2 * t + table[2]) * part, part)
        out[0, t] = up[0, :, pl.ds(at, part)]


def pack_call(table, up_maps):
    _, rank, width = up_maps.shape
    part = width // 16
    return pl.pallas_call(
        pack_kernel,
        grid_spec=pltpu.PrefetchScalarGridSpec(
            num_scalar_prefetch=1,
            grid=(2,),
            in_specs=[pl.BlockSpec((1, rank, width), lambda s, t: (t[s], 0, 0))],
            out_specs=pl.BlockSpec((1, 8, rank, part), lambda s, t: (s, 0, 0, 0)),
        ),
        out_shape=jax.ShapeDtypeStruct((2, 8, rank, part), jnp.bfloat16),
        name="pack",
        **settings(),
    )(table, pltpu.with_memory_space_constraint(up_maps, pltpu.HBM))


def take_kernel(table, got, out):
    out[...] = got[...]


def take_call(table, got):
    _, rank, part = got.shape
    return pl.pallas_call(
        take_kernel,
        grid_spec=pltpu.PrefetchScalarGridSpec(
            num_scalar_prefetch=1,
            grid=(8,),
            in_specs=[pl.BlockSpec((1, rank, part), lambda b, t: (t[b], 0, 0))],
            out_specs=pl.BlockSpec((1, rank, part), lambda b, t: (b, 0, 0)),
        ),
        out_shape=jax.ShapeDtypeStruct((8, rank, part), jnp.bfloat16),
        name="take",
        **settings(),
    )(table, got)


def finish_kernel(table, *refs):
    bases, gathered, refs = refs[:8], refs[8:12], refs[12:]
    up_mine, up_other, out, base, shrunk, rows, base_sems, sems = refs
    part = up_mine.shape[2]
    group = table[3, 0]
    fetches = [pltpu.make_async_copy(bases[g], base.at[g], base_sems.at[g]) for g in range(8)]
    for fetch in fetches:
        fetch.start()
    for i, pair in enumerate(gathered):
        shrunk[pl.ds(2 * i, 2)] = pair[...]
    copies = []
    for i in range(16):
        block, half = table[0, i], i % 2
        if half == 0:
            fetches[i // 2].wait()
        own = pl.ds(half * HALF, HALF)
        both = shrunk[table[1, i], own, :].astype(jnp.float32)
        value = jnp.where(table[2, i] > 0, both[:, 64:], both[:, :64]).astype(jnp.bfloat16)
        for up, side in ((up_mine, group), (up_other, 1 - group)):
            cut = pl.ds(pl.multiple_of(side * part, part), part)
            grown = jnp.dot(value, up[block], preferred_element_type=jnp.float32)
            rows[i, :, cut] = (base[i // 2, own, cut] + 0.5 * grown).astype(rows.dtype)
        to = pl.ds(pl.multiple_of((2 * block + half) * HALF, HALF), HALF)
        copies.append(pltpu.make_async_copy(rows.at[i], out.at[to], sems.at[i]))
        copies[-1].start()
    for copy in copies:
        copy.wait()


def finish_call(table, bases, gathered, up_mine, up_other):
    columns = bases[0].shape[1]
    return pl.pallas_call(
        finish_kernel,
        in_specs=[pl.BlockSpec(memory_space=pltpu.SMEM)]
        + [pl.BlockSpec(memory_space=pl.ANY)] * 8
        + in_vmem(6),
        out_specs=pl.BlockSpec(memory_space=pltpu.HBM),
        out_shape=jax.ShapeDtypeStruct((8 * BLOCK, columns), jnp.bfloat16),
        scratch_shapes=[
            pltpu.VMEM((8, BLOCK, columns), jnp.float32),
            pltpu.VMEM((8,) + gathered[0].shape[1:], jnp.bfloat16),
            pltpu.VMEM((16, HALF, columns), jnp.bfloat16),
            pltpu.SemaphoreType.DMA((8,)),
            pltpu.SemaphoreType.DMA((16,)),
        ],
        name="finish",
        **settings(),
    )(
        table,
        *[pltpu.with_memory_space_constraint(base, pltpu.HBM) for base in bases],
        *gathered,
        up_mine,
        up_other,
    )


def chain_body(
    tokens, query_weight, adapter_down_maps, adapter_up_maps, adapter_home_slot, adapter_per_block
):
    me = lax.axis_index("tensor")
    z, y = me // 2, me % 2
    store = lax.axis_index("store")
    group = lax.axis_index("groups")
    myself = me * 2 + store
    held, rank, width = adapter_down_maps.shape
    rows = tokens[0]
    halves = [rows[:HALF], rows[HALF:]]

    ahead, back = list(halves), list(halves[::-1])
    flight = [(send(ahead[k], AHEAD), send(back[k], BACK)) for k in range(2)]
    got, ahead, back, adapter_home_slot, adapter_per_block = lax.optimization_barrier(
        (flight[0], ahead, back, adapter_home_slot, adapter_per_block)
    )
    ahead.append(got[0])
    back.append(got[1])
    flight.append((send(ahead[2], AHEAD), send(back[2], BACK)))

    store_slots = find_slots(adapter_home_slot, adapter_per_block)
    owner = store_slots // held
    inside = store_slots % held
    picked = jnp.max(jnp.where(owner == myself, inside, 0), axis=1)
    owner_row = lax.dynamic_index_in_dim(owner, store, 0, keepdims=False).astype(jnp.int32)
    pick_own = lax.dynamic_index_in_dim(picked, store, 0, keepdims=False)
    pick_lent = lax.dynamic_index_in_dim(picked, 1 - store, 0, keepdims=False)

    down_own = lax.dynamic_index_in_dim(adapter_down_maps, pick_own, 0, keepdims=False)
    down_lent = lax.dynamic_index_in_dim(adapter_down_maps, pick_lent, 0, keepdims=False)
    down_swapped = swap(down_lent, "store")
    weights = pin_call(query_weight, down_own, down_swapped)
    choice = jnp.stack([pick_own, pick_lent, group.astype(pick_own.dtype)]).astype(jnp.int32)
    up_sent = pack_call(choice, adapter_up_maps)
    up_sent = jnp.stack([up_sent[0], swap(up_sent[1], "store")], axis=1)

    position = jnp.where(y == 0, z, 7 - z)
    places = []
    for k in range(8):
        step = (k + 1) // 2
        places += [position - step, position + step] if k % 2 else [position + step, position - step]
    places = jnp.stack(places) % 8
    blocks = jnp.where(places < 4, 2 * places, 15 - 2 * places).astype(jnp.int32)
    hit = blocks[:, None] == jnp.arange(8, dtype=jnp.int32)[None, :]
    owners = jnp.sum(jnp.where(hit, owner_row[None, :], 0), axis=1)
    table = jnp.stack([owners == myself, owners == me * 2 + 1 - store]).astype(jnp.int32)

    bases = []
    shrunk = jnp.zeros((BLOCK, 2 * rank), jnp.bfloat16)
    groups = [[rows], [ahead[2], back[2]]]
    for k in range(1, 7):
        (got_ahead, got_back), ahead, back, bases, shrunk, up_sent = lax.optimization_barrier(
            (flight[k], ahead, back, bases, shrunk, up_sent)
        )
        ahead.append(got_ahead)
        back.append(got_back)
        if k < 5:
            flight.append((send(ahead[k + 2], AHEAD), send(back[k + 2], BACK)))
        if k == 5:
            up_got = lax.all_to_all(up_sent, "tensor", split_axis=0, concat_axis=0, tiled=True)
        groups.append([got_ahead, got_back] if k % 2 == 0 else [got_back, got_ahead])
        for g in range(len(bases), min(len(bases) + 2, k + 2, 7)):
            base, shrunk = rows_call(g, table, weights, groups[g], shrunk)
            bases.append(base)
    base, shrunk = rows_call(7, table, weights, groups[7], shrunk)
    bases.append(base)

    across = send(shrunk, ACROSS)
    pair = jnp.stack([shrunk, across])
    everyone = [pair] + [send(pair, pairs) for pairs in ALONG]
    up_got, _ = lax.optimization_barrier((up_got, across))
    home, core = owner_row // 2, owner_row % 2
    chosen = 2 * home + jnp.where(core == store, 0, 1)
    up_mine = take_call(chosen.astype(jnp.int32), up_got.reshape(16, rank, -1))
    up_other = swap(up_mine, "groups")
    home, core = owners // 2, owners % 2
    where = 2 * ((home // 2) ^ z) + ((home % 2) ^ y)
    table = jnp.stack([blocks, where, core != store, jnp.broadcast_to(group, (16,))])
    return finish_call(table.astype(jnp.int32), bases, everyone, up_mine, up_other)[None]


def body(tokens, *rest):
    sizes = tuple(lax.axis_size(name) for name in ("groups", "tensor", "store"))
    fits = sizes == (2, 8, 2) and tokens.shape[1] == BLOCK
    return (chain_body if fits else general_body)(tokens, *rest)


def solution(mesh):
    placed = (
        P(("groups", "store"), "tensor", None),
        P(None, "tensor"),
        P(("tensor", "store"), None, None),
        P(("tensor", "store"), None, None),
        P(),
        P(),
    )
    return jax.shard_map(
        body,
        mesh=mesh,
        in_specs=placed,
        out_specs=P(("groups", "store"), None, "tensor"),
        check_vma=False,
    )
```

```python
import functools

import jax
import jax.numpy as jnp
from jax import lax
from jax.experimental import pallas as pl
from jax.experimental.pallas import tpu as pltpu
from jax.sharding import PartitionSpec as P

BLOCK = 128


def find_slots(adapter_home_slot, adapter_per_block):
    catalog = jnp.arange(adapter_home_slot.shape[0], dtype=jnp.int32)
    return jnp.sum(
        jnp.where(
            adapter_per_block[:, :, None] == catalog[None, None, :],
            adapter_home_slot[None, None, :],
            0,
        ),
        axis=2,
    )


def general_body(
    tokens, query_weight, adapter_down_maps, adapter_up_maps, adapter_home_slot, adapter_per_block
):
    shard_count = lax.axis_size("tensor")
    store_count = lax.axis_size("store")
    devices_all = shard_count * store_count
    my_tensor = lax.axis_index("tensor")
    my_store = lax.axis_index("store")
    myself = lax.axis_index(("tensor", "store"))
    held_adapters, rank_index, feature_width = adapter_down_maps.shape
    feature_index = query_weight.shape[1]
    own_rows = tokens[0]
    group_rows = own_rows.shape[0] * shard_count
    blocks = group_rows // BLOCK
    store_slots = find_slots(adapter_home_slot, adapter_per_block)
    owner = store_slots // held_adapters
    inside = store_slots % held_adapters
    picked = jnp.max(jnp.where(owner == myself, inside, -1), axis=1)
    select = (picked[:, None] == jnp.arange(held_adapters, dtype=jnp.int32)[None, :]).astype(
        jnp.bfloat16
    )
    down_map_parts = adapter_down_maps.reshape(
        held_adapters, rank_index, shard_count, feature_index
    )
    up_map_parts = adapter_up_maps.reshape(held_adapters, rank_index, shard_count, feature_index)
    send_down = jnp.einsum(
        "sl,lrtf->tsrf", select, down_map_parts, preferred_element_type=jnp.float32
    ).astype(jnp.bfloat16)
    send_up = jnp.einsum(
        "sl,lrtf->tsrf", select, up_map_parts, preferred_element_type=jnp.float32
    ).astype(jnp.bfloat16)
    recv_down, recv_up = (
        lax.all_to_all(
            sent.reshape(devices_all, rank_index, feature_index),
            ("tensor", "store"),
            split_axis=0,
            concat_axis=0,
            tiled=True,
        )
        for sent in (send_down, send_up)
    )
    owner_row = lax.dynamic_index_in_dim(owner, my_store, 0, keepdims=False)
    source_pick = (owner_row[:, None] == jnp.arange(devices_all, dtype=jnp.int32)[None, :]).astype(
        jnp.bfloat16
    )
    block_down = jnp.einsum(
        "bj,jrf->brf", source_pick, recv_down, preferred_element_type=jnp.float32
    ).astype(jnp.bfloat16)
    block_up = jnp.einsum(
        "bj,jrf->brf", source_pick, recv_up, preferred_element_type=jnp.float32
    ).astype(jnp.bfloat16)
    piece = lax.all_gather(own_rows, "tensor", axis=0, tiled=True)
    product = jnp.dot(piece, query_weight, preferred_element_type=jnp.float32)
    features = lax.dynamic_slice_in_dim(piece, my_tensor * feature_index, feature_index, 1)
    partial_value = jnp.einsum(
        "bnf,brf->bnr",
        features.reshape(blocks, BLOCK, feature_index),
        block_down,
        preferred_element_type=jnp.float32,
    )
    shrunk = lax.psum(partial_value, "tensor").astype(jnp.bfloat16)
    grown = jnp.einsum(
        "bnr,brf->bnf", shrunk, block_up, preferred_element_type=jnp.float32
    ).reshape(group_rows, feature_index)
    query = (product + 0.5 * grown).astype(jnp.bfloat16)
    return query[None]


def both_ways(pairs):
    return pairs + [(b, a) for a, b in pairs]


RING = [0, 2, 4, 6, 7, 5, 3, 1]
AHEAD = [(RING[i], RING[(i + 1) % 8]) for i in range(8)]
BACK = [(b, a) for a, b in AHEAD]
ACROSS = [(i, i ^ 1) for i in range(8)]
ALONG = [[(i, i ^ (2 * d)) for i in range(8)] for d in (1, 2, 3)]
HALF = BLOCK // 2
DEPTH = 1024
VMEM_LIMIT = 16 * 1024 * 1024


def send(value, pairs):
    return lax.ppermute(value, "tensor", pairs)


def swap(value, axis):
    return lax.ppermute(value, axis, [(0, 1), (1, 0)])


def settings(flops=1):
    return dict(
        compiler_params=pltpu.CompilerParams(vmem_limit_bytes=VMEM_LIMIT),
        cost_estimate=pl.CostEstimate(flops=flops, bytes_accessed=1, transcendentals=0),
    )


def in_vmem(count):
    return [pl.BlockSpec(memory_space=pltpu.VMEM)] * count


def pin_kernel(weight, own, swapped, out, sem):
    columns = weight.shape[1]
    copy = pltpu.make_async_copy(weight, out.at[:, pl.ds(0, columns)], sem)
    copy.start()
    for at in range(0, weight.shape[0], DEPTH):
        cut = pl.ds(at, DEPTH)
        out[cut, columns:] = jnp.concatenate([own[:, cut], swapped[:, cut]], axis=0).T
    copy.wait()


def pin_call(weight, own, swapped):
    width, columns = weight.shape
    return pl.pallas_call(
        pin_kernel,
        in_specs=[pl.BlockSpec(memory_space=pl.ANY)] + in_vmem(2),
        out_specs=in_vmem(1)[0],
        out_shape=pltpu.VMEM((width, columns + 2 * own.shape[0]), weight.dtype),
        scratch_shapes=[pltpu.SemaphoreType.DMA],
        name="pin",
        **settings(),
    )(weight, own, swapped)


def rows_kernel(group, table, weights, *refs):
    *pieces, shrunk, base, shrunk_out = refs
    columns = base.shape[1]
    total = None
    for at in range(0, weights.shape[0], DEPTH):
        cut = pl.ds(at, DEPTH)
        x = [p[:, cut] for p in pieces]
        x = x[0] if len(x) == 1 else jnp.concatenate(x, axis=0)
        part = jnp.dot(x, weights[cut, :], preferred_element_type=jnp.float32)
        total = part if total is None else total + part
    base[...] = total[:, :columns]
    lane = lax.broadcasted_iota(jnp.int32, shrunk.shape, 1)
    row = lax.broadcasted_iota(jnp.int32, shrunk.shape, 0)
    use = jnp.where(
        row < HALF,
        jnp.where(lane < 64, table[0, 2 * group], table[1, 2 * group]),
        jnp.where(lane < 64, table[0, 2 * group + 1], table[1, 2 * group + 1]),
    )
    small = total[:, columns:].astype(jnp.bfloat16).astype(jnp.float32)
    old = shrunk[...].astype(jnp.float32)
    shrunk_out[...] = jnp.where(use > 0, small, old).astype(jnp.bfloat16)


def rows_call(group, table, weights, pieces, shrunk):
    columns = weights.shape[1] - 128
    operands = [pltpu.with_memory_space_constraint(weights, pltpu.VMEM)] + pieces + [shrunk]
    return pl.pallas_call(
        functools.partial(rows_kernel, group),
        in_specs=[pl.BlockSpec(memory_space=pltpu.SMEM)] + in_vmem(len(operands)),
        out_specs=in_vmem(2),
        out_shape=[
            jax.ShapeDtypeStruct((BLOCK, columns), jnp.float32),
            jax.ShapeDtypeStruct((BLOCK, 128), jnp.bfloat16),
        ],
        name="rows",
        **settings(flops=10**11 if group == 7 else 1),
    )(table, *operands)


def pack_kernel(table, up, out):
    part = out.shape[3]
    for t in range(8):
        at = pl.multiple_of((2 * t + table[2]) * part, part)
        out[0, t] = up[0, :, pl.ds(at, part)]


def pack_call(table, up_maps):
    _, rank, width = up_maps.shape
    part = width // 16
    return pl.pallas_call(
        pack_kernel,
        grid_spec=pltpu.PrefetchScalarGridSpec(
            num_scalar_prefetch=1,
            grid=(2,),
            in_specs=[pl.BlockSpec((1, rank, width), lambda s, t: (t[s], 0, 0))],
            out_specs=pl.BlockSpec((1, 8, rank, part), lambda s, t: (s, 0, 0, 0)),
        ),
        out_shape=jax.ShapeDtypeStruct((2, 8, rank, part), jnp.bfloat16),
        name="pack",
        **settings(),
    )(table, pltpu.with_memory_space_constraint(up_maps, pltpu.HBM))


def take_kernel(table, got, out):
    out[...] = got[...]


def take_call(table, got):
    _, rank, part = got.shape
    return pl.pallas_call(
        take_kernel,
        grid_spec=pltpu.PrefetchScalarGridSpec(
            num_scalar_prefetch=1,
            grid=(8,),
            in_specs=[pl.BlockSpec((1, rank, part), lambda b, t: (t[b], 0, 0))],
            out_specs=pl.BlockSpec((1, rank, part), lambda b, t: (b, 0, 0)),
        ),
        out_shape=jax.ShapeDtypeStruct((8, rank, part), jnp.bfloat16),
        name="take",
        **settings(),
    )(table, got)


def finish_kernel(table, *refs):
    bases, gathered, refs = refs[:8], refs[8:12], refs[12:]
    up_mine, up_other, out, base, shrunk, rows, base_sems, sems = refs
    part = up_mine.shape[2]
    group = table[3, 0]
    fetches = [pltpu.make_async_copy(bases[g], base.at[g], base_sems.at[g]) for g in range(8)]
    for fetch in fetches:
        fetch.start()
    for i, pair in enumerate(gathered):
        shrunk[pl.ds(2 * i, 2)] = pair[...]
    copies = []
    for i in range(16):
        block, half = table[0, i], i % 2
        if half == 0:
            fetches[i // 2].wait()
        own = pl.ds(half * HALF, HALF)
        both = shrunk[table[1, i], own, :].astype(jnp.float32)
        value = jnp.where(table[2, i] > 0, both[:, 64:], both[:, :64]).astype(jnp.bfloat16)
        for up, side in ((up_mine, group), (up_other, 1 - group)):
            cut = pl.ds(pl.multiple_of(side * part, part), part)
            grown = jnp.dot(value, up[block], preferred_element_type=jnp.float32)
            rows[i, :, cut] = (base[i // 2, own, cut] + 0.5 * grown).astype(rows.dtype)
        to = pl.ds(pl.multiple_of((2 * block + half) * HALF, HALF), HALF)
        copies.append(pltpu.make_async_copy(rows.at[i], out.at[to], sems.at[i]))
        copies[-1].start()
    for copy in copies:
        copy.wait()


def finish_call(table, bases, gathered, up_mine, up_other):
    columns = bases[0].shape[1]
    return pl.pallas_call(
        finish_kernel,
        in_specs=[pl.BlockSpec(memory_space=pltpu.SMEM)]
        + [pl.BlockSpec(memory_space=pl.ANY)] * 8
        + in_vmem(6),
        out_specs=pl.BlockSpec(memory_space=pltpu.HBM),
        out_shape=jax.ShapeDtypeStruct((8 * BLOCK, columns), jnp.bfloat16),
        scratch_shapes=[
            pltpu.VMEM((8, BLOCK, columns), jnp.float32),
            pltpu.VMEM((8,) + gathered[0].shape[1:], jnp.bfloat16),
            pltpu.VMEM((16, HALF, columns), jnp.bfloat16),
            pltpu.SemaphoreType.DMA((8,)),
            pltpu.SemaphoreType.DMA((16,)),
        ],
        name="finish",
        **settings(),
    )(
        table,
        *[pltpu.with_memory_space_constraint(base, pltpu.HBM) for base in bases],
        *gathered,
        up_mine,
        up_other,
    )


def chain_body(
    tokens, query_weight, adapter_down_maps, adapter_up_maps, adapter_home_slot, adapter_per_block
):
    me = lax.axis_index("tensor")
    z, y = me // 2, me % 2
    store = lax.axis_index("store")
    group = lax.axis_index("groups")
    myself = me * 2 + store
    held, rank, width = adapter_down_maps.shape
    rows = tokens[0]
    halves = [rows[:HALF], rows[HALF:]]

    ahead, back = list(halves), list(halves[::-1])
    flight = [(send(ahead[k], AHEAD), send(back[k], BACK)) for k in range(2)]
    got, ahead, back, adapter_home_slot, adapter_per_block = lax.optimization_barrier(
        (flight[0], ahead, back, adapter_home_slot, adapter_per_block)
    )
    ahead.append(got[0])
    back.append(got[1])
    flight.append((send(ahead[2], AHEAD), send(back[2], BACK)))

    store_slots = find_slots(adapter_home_slot, adapter_per_block)
    owner = store_slots // held
    inside = store_slots % held
    picked = jnp.max(jnp.where(owner == myself, inside, 0), axis=1)
    owner_row = lax.dynamic_index_in_dim(owner, store, 0, keepdims=False).astype(jnp.int32)
    pick_own = lax.dynamic_index_in_dim(picked, store, 0, keepdims=False)
    pick_lent = lax.dynamic_index_in_dim(picked, 1 - store, 0, keepdims=False)

    down_own = lax.dynamic_index_in_dim(adapter_down_maps, pick_own, 0, keepdims=False)
    down_lent = lax.dynamic_index_in_dim(adapter_down_maps, pick_lent, 0, keepdims=False)
    down_swapped = swap(down_lent, "store")
    weights = pin_call(query_weight, down_own, down_swapped)
    choice = jnp.stack([pick_own, pick_lent, group.astype(pick_own.dtype)]).astype(jnp.int32)
    up_sent = pack_call(choice, adapter_up_maps)
    up_sent = jnp.stack([up_sent[0], swap(up_sent[1], "store")], axis=1)

    position = jnp.where(y == 0, z, 7 - z)
    places = []
    for k in range(8):
        step = (k + 1) // 2
        places += [position - step, position + step] if k % 2 else [position + step, position - step]
    places = jnp.stack(places) % 8
    blocks = jnp.where(places < 4, 2 * places, 15 - 2 * places).astype(jnp.int32)
    hit = blocks[:, None] == jnp.arange(8, dtype=jnp.int32)[None, :]
    owners = jnp.sum(jnp.where(hit, owner_row[None, :], 0), axis=1)
    table = jnp.stack([owners == myself, owners == me * 2 + 1 - store]).astype(jnp.int32)

    bases = []
    shrunk = jnp.zeros((BLOCK, 2 * rank), jnp.bfloat16)
    groups = [[rows], [ahead[2], back[2]]]
    for k in range(1, 7):
        (got_ahead, got_back), ahead, back, bases, shrunk, up_sent = lax.optimization_barrier(
            (flight[k], ahead, back, bases, shrunk, up_sent)
        )
        ahead.append(got_ahead)
        back.append(got_back)
        if k < 5:
            flight.append((send(ahead[k + 2], AHEAD), send(back[k + 2], BACK)))
        if k == 5:
            up_got = lax.all_to_all(up_sent, "tensor", split_axis=0, concat_axis=0, tiled=True)
        groups.append([got_ahead, got_back] if k % 2 == 0 else [got_back, got_ahead])
        for g in range(len(bases), min(len(bases) + 2, k + 2, 7)):
            base, shrunk = rows_call(g, table, weights, groups[g], shrunk)
            bases.append(base)
    base, shrunk = rows_call(7, table, weights, groups[7], shrunk)
    bases.append(base)

    across = send(shrunk, ACROSS)
    pair = jnp.stack([shrunk, across])
    everyone = [pair] + [send(pair, pairs) for pairs in ALONG]
    up_got, _ = lax.optimization_barrier((up_got, across))
    home, core = owner_row // 2, owner_row % 2
    chosen = 2 * home + jnp.where(core == store, 0, 1)
    up_mine = take_call(chosen.astype(jnp.int32), up_got.reshape(16, rank, -1))
    up_other = swap(up_mine, "groups")
    home, core = owners // 2, owners % 2
    where = 2 * ((home // 2) ^ z) + ((home % 2) ^ y)
    table = jnp.stack([blocks, where, core != store, jnp.broadcast_to(group, (16,))])
    return finish_call(table.astype(jnp.int32), bases, everyone, up_mine, up_other)[None]


def body(tokens, *rest):
    sizes = tuple(lax.axis_size(name) for name in ("groups", "tensor", "store"))
    fits = sizes == (2, 8, 2) and tokens.shape[1] == BLOCK
    return (chain_body if fits else general_body)(tokens, *rest)


def solution(mesh):
    placed = (
        P(("groups", "store"), "tensor", None),
        P(None, "tensor"),
        P(("tensor", "store"), None, None),
        P(("tensor", "store"), None, None),
        P(),
        P(),
    )
    return jax.shard_map(
        body,
        mesh=mesh,
        in_specs=placed,
        out_specs=P(("groups", "store"), None, "tensor"),
        check_vma=False,
    )
```

```python
import functools

import jax
import jax.numpy as jnp
from jax import lax
from jax.experimental import pallas as pl
from jax.experimental.pallas import tpu as pltpu
from jax.sharding import PartitionSpec as P

BLOCK = 128


def find_slots(adapter_home_slot, adapter_per_block):
    catalog = jnp.arange(adapter_home_slot.shape[0], dtype=jnp.int32)
    return jnp.sum(
        jnp.where(
            adapter_per_block[:, :, None] == catalog[None, None, :],
            adapter_home_slot[None, None, :],
            0,
        ),
        axis=2,
    )


def general_body(
    tokens, query_weight, adapter_down_maps, adapter_up_maps, adapter_home_slot, adapter_per_block
):
    shard_count = lax.axis_size("tensor")
    store_count = lax.axis_size("store")
    devices_all = shard_count * store_count
    my_tensor = lax.axis_index("tensor")
    my_store = lax.axis_index("store")
    myself = lax.axis_index(("tensor", "store"))
    held_adapters, rank_index, feature_width = adapter_down_maps.shape
    feature_index = query_weight.shape[1]
    own_rows = tokens[0]
    group_rows = own_rows.shape[0] * shard_count
    blocks = group_rows // BLOCK
    store_slots = find_slots(adapter_home_slot, adapter_per_block)
    owner = store_slots // held_adapters
    inside = store_slots % held_adapters
    picked = jnp.max(jnp.where(owner == myself, inside, -1), axis=1)
    select = (picked[:, None] == jnp.arange(held_adapters, dtype=jnp.int32)[None, :]).astype(
        jnp.bfloat16
    )
    down_map_parts = adapter_down_maps.reshape(
        held_adapters, rank_index, shard_count, feature_index
    )
    up_map_parts = adapter_up_maps.reshape(held_adapters, rank_index, shard_count, feature_index)
    send_down = jnp.einsum(
        "sl,lrtf->tsrf", select, down_map_parts, preferred_element_type=jnp.float32
    ).astype(jnp.bfloat16)
    send_up = jnp.einsum(
        "sl,lrtf->tsrf", select, up_map_parts, preferred_element_type=jnp.float32
    ).astype(jnp.bfloat16)
    recv_down, recv_up = (
        lax.all_to_all(
            sent.reshape(devices_all, rank_index, feature_index),
            ("tensor", "store"),
            split_axis=0,
            concat_axis=0,
            tiled=True,
        )
        for sent in (send_down, send_up)
    )
    owner_row = lax.dynamic_index_in_dim(owner, my_store, 0, keepdims=False)
    source_pick = (owner_row[:, None] == jnp.arange(devices_all, dtype=jnp.int32)[None, :]).astype(
        jnp.bfloat16
    )
    block_down = jnp.einsum(
        "bj,jrf->brf", source_pick, recv_down, preferred_element_type=jnp.float32
    ).astype(jnp.bfloat16)
    block_up = jnp.einsum(
        "bj,jrf->brf", source_pick, recv_up, preferred_element_type=jnp.float32
    ).astype(jnp.bfloat16)
    piece = lax.all_gather(own_rows, "tensor", axis=0, tiled=True)
    product = jnp.dot(piece, query_weight, preferred_element_type=jnp.float32)
    features = lax.dynamic_slice_in_dim(piece, my_tensor * feature_index, feature_index, 1)
    partial_value = jnp.einsum(
        "bnf,brf->bnr",
        features.reshape(blocks, BLOCK, feature_index),
        block_down,
        preferred_element_type=jnp.float32,
    )
    shrunk = lax.psum(partial_value, "tensor").astype(jnp.bfloat16)
    grown = jnp.einsum(
        "bnr,brf->bnf", shrunk, block_up, preferred_element_type=jnp.float32
    ).reshape(group_rows, feature_index)
    query = (product + 0.5 * grown).astype(jnp.bfloat16)
    return query[None]


def both_ways(pairs):
    return pairs + [(b, a) for a, b in pairs]


RING = [0, 2, 4, 6, 7, 5, 3, 1]
AHEAD = [(RING[i], RING[(i + 1) % 8]) for i in range(8)]
BACK = [(b, a) for a, b in AHEAD]
ACROSS = [(i, i ^ 1) for i in range(8)]
ALONG = [[(i, i ^ (2 * d)) for i in range(8)] for d in (1, 2, 3)]
HALF = BLOCK // 2
DEPTH = 1024
VMEM_LIMIT = 16 * 1024 * 1024


def send(value, pairs):
    return lax.ppermute(value, "tensor", pairs)


def swap(value, axis):
    return lax.ppermute(value, axis, [(0, 1), (1, 0)])


def settings(flops=1):
    return dict(
        compiler_params=pltpu.CompilerParams(vmem_limit_bytes=VMEM_LIMIT),
        cost_estimate=pl.CostEstimate(flops=flops, bytes_accessed=1, transcendentals=0),
    )


def in_vmem(count):
    return [pl.BlockSpec(memory_space=pltpu.VMEM)] * count


def pin_kernel(weight, own, swapped, out, sem):
    columns = weight.shape[1]
    copy = pltpu.make_async_copy(weight, out.at[:, pl.ds(0, columns)], sem)
    copy.start()
    for at in range(0, weight.shape[0], DEPTH):
        cut = pl.ds(at, DEPTH)
        out[cut, columns:] = jnp.concatenate([own[:, cut], swapped[:, cut]], axis=0).T
    copy.wait()


def pin_call(weight, own, swapped):
    width, columns = weight.shape
    return pl.pallas_call(
        pin_kernel,
        in_specs=[pl.BlockSpec(memory_space=pl.ANY)] + in_vmem(2),
        out_specs=in_vmem(1)[0],
        out_shape=pltpu.VMEM((width, columns + 2 * own.shape[0]), weight.dtype),
        scratch_shapes=[pltpu.SemaphoreType.DMA],
        name="pin",
        **settings(),
    )(weight, own, swapped)


def rows_kernel(group, table, weights, *refs):
    *pieces, shrunk, base, shrunk_out = refs
    columns = base.shape[1]
    total = None
    for at in range(0, weights.shape[0], DEPTH):
        cut = pl.ds(at, DEPTH)
        x = [p[:, cut] for p in pieces]
        x = x[0] if len(x) == 1 else jnp.concatenate(x, axis=0)
        part = jnp.dot(x, weights[cut, :], preferred_element_type=jnp.float32)
        total = part if total is None else total + part
    base[...] = total[:, :columns]
    lane = lax.broadcasted_iota(jnp.int32, shrunk.shape, 1)
    row = lax.broadcasted_iota(jnp.int32, shrunk.shape, 0)
    use = jnp.where(
        row < HALF,
        jnp.where(lane < 64, table[0, 2 * group], table[1, 2 * group]),
        jnp.where(lane < 64, table[0, 2 * group + 1], table[1, 2 * group + 1]),
    )
    small = total[:, columns:].astype(jnp.bfloat16).astype(jnp.float32)
    old = shrunk[...].astype(jnp.float32)
    shrunk_out[...] = jnp.where(use > 0, small, old).astype(jnp.bfloat16)


def rows_call(group, table, weights, pieces, shrunk):
    columns = weights.shape[1] - 128
    operands = [pltpu.with_memory_space_constraint(weights, pltpu.VMEM)] + pieces + [shrunk]
    return pl.pallas_call(
        functools.partial(rows_kernel, group),
        in_specs=[pl.BlockSpec(memory_space=pltpu.SMEM)] + in_vmem(len(operands)),
        out_specs=in_vmem(2),
        out_shape=[
            jax.ShapeDtypeStruct((BLOCK, columns), jnp.float32),
            jax.ShapeDtypeStruct((BLOCK, 128), jnp.bfloat16),
        ],
        name="rows",
        **settings(flops=10**11 if group == 7 else 1),
    )(table, *operands)


def pack_kernel(table, up, out):
    part = out.shape[3]
    for t in range(8):
        at = pl.multiple_of((2 * t + table[2]) * part, part)
        out[0, t] = up[0, :, pl.ds(at, part)]


def pack_call(table, up_maps):
    _, rank, width = up_maps.shape
    part = width // 16
    return pl.pallas_call(
        pack_kernel,
        grid_spec=pltpu.PrefetchScalarGridSpec(
            num_scalar_prefetch=1,
            grid=(2,),
            in_specs=[pl.BlockSpec((1, rank, width), lambda s, t: (t[s], 0, 0))],
            out_specs=pl.BlockSpec((1, 8, rank, part), lambda s, t: (s, 0, 0, 0)),
        ),
        out_shape=jax.ShapeDtypeStruct((2, 8, rank, part), jnp.bfloat16),
        name="pack",
        **settings(),
    )(table, pltpu.with_memory_space_constraint(up_maps, pltpu.HBM))


def take_kernel(table, got, out):
    out[...] = got[...]


def take_call(table, got):
    _, rank, part = got.shape
    return pl.pallas_call(
        take_kernel,
        grid_spec=pltpu.PrefetchScalarGridSpec(
            num_scalar_prefetch=1,
            grid=(8,),
            in_specs=[pl.BlockSpec((1, rank, part), lambda b, t: (t[b], 0, 0))],
            out_specs=pl.BlockSpec((1, rank, part), lambda b, t: (b, 0, 0)),
        ),
        out_shape=jax.ShapeDtypeStruct((8, rank, part), jnp.bfloat16),
        name="take",
        **settings(),
    )(table, got)


def collect_kernel(*refs):
    *bases, out, sems = refs
    copies = [pltpu.make_async_copy(bases[g], out.at[g], sems.at[g]) for g in range(8)]
    for copy in copies:
        copy.start()
    for copy in copies:
        copy.wait()


def collect_call(bases):
    return pl.pallas_call(
        collect_kernel,
        in_specs=[pl.BlockSpec(memory_space=pl.ANY)] * 8,
        out_specs=in_vmem(1)[0],
        out_shape=pltpu.VMEM((8,) + bases[0].shape, jnp.float32),
        scratch_shapes=[pltpu.SemaphoreType.DMA((8,))],
        name="collect",
        **settings(),
    )(*[pltpu.with_memory_space_constraint(base, pltpu.HBM) for base in bases])


def finish_kernel(table, base, *refs):
    gathered, (mine_a, mine_b, other_a, other_b) = refs[:4], refs[4:8]
    out, shrunk, rows, sems = refs[8:]
    part = mine_a.shape[2]
    group = table[3, 0]
    for i, pair in enumerate(gathered):
        shrunk[pl.ds(2 * i, 2)] = pair[...]
    copies = []
    for i in range(16):
        block, half = table[0, i], i % 2
        own = pl.ds(half * HALF, HALF)
        both = shrunk[table[1, i], own, :].astype(jnp.float32)
        value = jnp.where(table[2, i] > 0, both[:, 64:], both[:, :64]).astype(jnp.bfloat16)
        for up, side in (((mine_a, mine_b), group), ((other_a, other_b), 1 - group)):
            cut = pl.ds(pl.multiple_of(side * part, part), part)
            up = jnp.concatenate([up[0][block], up[1][block]], axis=0)
            grown = jnp.dot(value, up, preferred_element_type=jnp.float32)
            rows[i, :, cut] = (base[i // 2, own, cut] + 0.5 * grown).astype(rows.dtype)
        to = pl.ds(pl.multiple_of((2 * block + half) * HALF, HALF), HALF)
        copies.append(pltpu.make_async_copy(rows.at[i], out.at[to], sems.at[i]))
        copies[-1].start()
    for copy in copies:
        copy.wait()


def finish_call(table, base, gathered, ups):
    columns = base.shape[2]
    return pl.pallas_call(
        finish_kernel,
        in_specs=[pl.BlockSpec(memory_space=pltpu.SMEM)] + in_vmem(9),
        out_specs=pl.BlockSpec(memory_space=pltpu.HBM),
        out_shape=jax.ShapeDtypeStruct((8 * BLOCK, columns), jnp.bfloat16),
        scratch_shapes=[
            pltpu.VMEM((8,) + gathered[0].shape[1:], jnp.bfloat16),
            pltpu.VMEM((16, HALF, columns), jnp.bfloat16),
            pltpu.SemaphoreType.DMA((16,)),
        ],
        name="finish",
        **settings(),
    )(table, pltpu.with_memory_space_constraint(base, pltpu.VMEM), *gathered, *ups)


def chain_body(
    tokens, query_weight, adapter_down_maps, adapter_up_maps, adapter_home_slot, adapter_per_block
):
    me = lax.axis_index("tensor")
    z, y = me // 2, me % 2
    store = lax.axis_index("store")
    group = lax.axis_index("groups")
    myself = me * 2 + store
    held, rank, width = adapter_down_maps.shape
    rows = tokens[0]
    halves = [rows[:HALF], rows[HALF:]]

    ahead, back = list(halves), list(halves[::-1])
    flight = [(send(ahead[k], AHEAD), send(back[k], BACK)) for k in range(2)]
    got, ahead, back, adapter_home_slot, adapter_per_block = lax.optimization_barrier(
        (flight[0], ahead, back, adapter_home_slot, adapter_per_block)
    )
    ahead.append(got[0])
    back.append(got[1])
    flight.append((send(ahead[2], AHEAD), send(back[2], BACK)))

    store_slots = find_slots(adapter_home_slot, adapter_per_block)
    owner = store_slots // held
    inside = store_slots % held
    picked = jnp.max(jnp.where(owner == myself, inside, 0), axis=1)
    owner_row = lax.dynamic_index_in_dim(owner, store, 0, keepdims=False).astype(jnp.int32)
    pick_own = lax.dynamic_index_in_dim(picked, store, 0, keepdims=False)
    pick_lent = lax.dynamic_index_in_dim(picked, 1 - store, 0, keepdims=False)

    down_own = lax.dynamic_index_in_dim(adapter_down_maps, pick_own, 0, keepdims=False)
    down_lent = lax.dynamic_index_in_dim(adapter_down_maps, pick_lent, 0, keepdims=False)
    down_swapped = swap(down_lent, "store")
    weights = pin_call(query_weight, down_own, down_swapped)
    choice = jnp.stack([pick_own, pick_lent, group.astype(pick_own.dtype)]).astype(jnp.int32)
    up_sent = pack_call(choice, adapter_up_maps)
    up_sent = jnp.stack([up_sent[0], swap(up_sent[1], "store")], axis=1)
    up_sent = [up_sent[:, :, : rank // 2], up_sent[:, :, rank // 2 :]]

    position = jnp.where(y == 0, z, 7 - z)
    places = []
    for k in range(8):
        step = (k + 1) // 2
        places += [position - step, position + step] if k % 2 else [position + step, position - step]
    places = jnp.stack(places) % 8
    blocks = jnp.where(places < 4, 2 * places, 15 - 2 * places).astype(jnp.int32)
    hit = blocks[:, None] == jnp.arange(8, dtype=jnp.int32)[None, :]
    owners = jnp.sum(jnp.where(hit, owner_row[None, :], 0), axis=1)
    table = jnp.stack([owners == myself, owners == me * 2 + 1 - store]).astype(jnp.int32)

    bases = []
    shrunk = jnp.zeros((BLOCK, 2 * rank), jnp.bfloat16)
    groups = [[rows], [ahead[2], back[2]]]
    for k in range(1, 7):
        (got_ahead, got_back), ahead, back, bases, shrunk, up_sent = lax.optimization_barrier(
            (flight[k], ahead, back, bases, shrunk, up_sent)
        )
        ahead.append(got_ahead)
        back.append(got_back)
        if k < 5:
            flight.append((send(ahead[k + 2], AHEAD), send(back[k + 2], BACK)))
        if k == 5:
            up_got = [
                lax.all_to_all(sent, "tensor", split_axis=0, concat_axis=0, tiled=True)
                for sent in up_sent
            ]
        groups.append([got_ahead, got_back] if k % 2 == 0 else [got_back, got_ahead])
        for g in range(len(bases), min(len(bases) + 2, k + 2, 7)):
            base, shrunk = rows_call(g, table, weights, groups[g], shrunk)
            bases.append(base)
    base, shrunk = rows_call(7, table, weights, groups[7], shrunk)
    bases.append(base)

    pair = jnp.stack([shrunk, send(shrunk, ACROSS)])
    everyone = [pair] + [send(pair, pairs) for pairs in ALONG]
    base = collect_call(bases)
    up_got[0], everyone, base = lax.optimization_barrier((up_got[0], everyone, base))
    home, core = owner_row // 2, owner_row % 2
    chosen = (2 * home + jnp.where(core == store, 0, 1)).astype(jnp.int32)

    def take(got):
        return take_call(chosen, got.reshape(16, rank // 2, -1))

    mine = [take(up_got[0])]
    other = [swap(mine[0], "groups")]
    up_got[1], _ = lax.optimization_barrier((up_got[1], mine[0]))
    mine.append(take(up_got[1]))
    other.append(swap(mine[1], "groups"))
    home, core = owners // 2, owners % 2
    where = 2 * ((home // 2) ^ z) + ((home % 2) ^ y)
    table = jnp.stack([blocks, where, core != store, jnp.broadcast_to(group, (16,))])
    return finish_call(table.astype(jnp.int32), base, everyone, mine + other)[None]


def body(tokens, *rest):
    sizes = tuple(lax.axis_size(name) for name in ("groups", "tensor", "store"))
    fits = sizes == (2, 8, 2) and tokens.shape[1] == BLOCK
    return (chain_body if fits else general_body)(tokens, *rest)


def solution(mesh):
    placed = (
        P(("groups", "store"), "tensor", None),
        P(None, "tensor"),
        P(("tensor", "store"), None, None),
        P(("tensor", "store"), None, None),
        P(),
        P(),
    )
    return jax.shard_map(
        body,
        mesh=mesh,
        in_specs=placed,
        out_specs=P(("groups", "store"), None, "tensor"),
        check_vma=False,
    )
```

```python
import functools

import jax
import jax.numpy as jnp
from jax import lax
from jax.experimental import pallas as pl
from jax.experimental.pallas import tpu as pltpu
from jax.sharding import PartitionSpec as P

BLOCK = 128


def find_slots(adapter_home_slot, adapter_per_block):
    catalog = jnp.arange(adapter_home_slot.shape[0], dtype=jnp.int32)
    return jnp.sum(
        jnp.where(
            adapter_per_block[:, :, None] == catalog[None, None, :],
            adapter_home_slot[None, None, :],
            0,
        ),
        axis=2,
    )


def general_body(
    tokens, query_weight, adapter_down_maps, adapter_up_maps, adapter_home_slot, adapter_per_block
):
    shard_count = lax.axis_size("tensor")
    store_count = lax.axis_size("store")
    devices_all = shard_count * store_count
    my_tensor = lax.axis_index("tensor")
    my_store = lax.axis_index("store")
    myself = lax.axis_index(("tensor", "store"))
    held_adapters, rank_index, feature_width = adapter_down_maps.shape
    feature_index = query_weight.shape[1]
    own_rows = tokens[0]
    group_rows = own_rows.shape[0] * shard_count
    blocks = group_rows // BLOCK
    store_slots = find_slots(adapter_home_slot, adapter_per_block)
    owner = store_slots // held_adapters
    inside = store_slots % held_adapters
    picked = jnp.max(jnp.where(owner == myself, inside, -1), axis=1)
    select = (picked[:, None] == jnp.arange(held_adapters, dtype=jnp.int32)[None, :]).astype(
        jnp.bfloat16
    )
    down_map_parts = adapter_down_maps.reshape(
        held_adapters, rank_index, shard_count, feature_index
    )
    up_map_parts = adapter_up_maps.reshape(held_adapters, rank_index, shard_count, feature_index)
    send_down = jnp.einsum(
        "sl,lrtf->tsrf", select, down_map_parts, preferred_element_type=jnp.float32
    ).astype(jnp.bfloat16)
    send_up = jnp.einsum(
        "sl,lrtf->tsrf", select, up_map_parts, preferred_element_type=jnp.float32
    ).astype(jnp.bfloat16)
    recv_down, recv_up = (
        lax.all_to_all(
            sent.reshape(devices_all, rank_index, feature_index),
            ("tensor", "store"),
            split_axis=0,
            concat_axis=0,
            tiled=True,
        )
        for sent in (send_down, send_up)
    )
    owner_row = lax.dynamic_index_in_dim(owner, my_store, 0, keepdims=False)
    source_pick = (owner_row[:, None] == jnp.arange(devices_all, dtype=jnp.int32)[None, :]).astype(
        jnp.bfloat16
    )
    block_down = jnp.einsum(
        "bj,jrf->brf", source_pick, recv_down, preferred_element_type=jnp.float32
    ).astype(jnp.bfloat16)
    block_up = jnp.einsum(
        "bj,jrf->brf", source_pick, recv_up, preferred_element_type=jnp.float32
    ).astype(jnp.bfloat16)
    piece = lax.all_gather(own_rows, "tensor", axis=0, tiled=True)
    product = jnp.dot(piece, query_weight, preferred_element_type=jnp.float32)
    features = lax.dynamic_slice_in_dim(piece, my_tensor * feature_index, feature_index, 1)
    partial_value = jnp.einsum(
        "bnf,brf->bnr",
        features.reshape(blocks, BLOCK, feature_index),
        block_down,
        preferred_element_type=jnp.float32,
    )
    shrunk = lax.psum(partial_value, "tensor").astype(jnp.bfloat16)
    grown = jnp.einsum(
        "bnr,brf->bnf", shrunk, block_up, preferred_element_type=jnp.float32
    ).reshape(group_rows, feature_index)
    query = (product + 0.5 * grown).astype(jnp.bfloat16)
    return query[None]


def both_ways(pairs):
    return pairs + [(b, a) for a, b in pairs]


RING = [0, 2, 4, 6, 7, 5, 3, 1]
AHEAD = [(RING[i], RING[(i + 1) % 8]) for i in range(8)]
BACK = [(b, a) for a, b in AHEAD]
ACROSS = [(i, i ^ 1) for i in range(8)]
ALONG = [[(i, i ^ (2 * d)) for i in range(8)] for d in (1, 2, 3)]
HALF = BLOCK // 2
DEPTH = 1024
VMEM_LIMIT = 16 * 1024 * 1024


def send(value, pairs):
    return lax.ppermute(value, "tensor", pairs)


def swap(value, axis):
    return lax.ppermute(value, axis, [(0, 1), (1, 0)])


def settings(flops=1):
    return dict(
        compiler_params=pltpu.CompilerParams(vmem_limit_bytes=VMEM_LIMIT),
        cost_estimate=pl.CostEstimate(flops=flops, bytes_accessed=1, transcendentals=0),
    )


def in_vmem(count):
    return [pl.BlockSpec(memory_space=pltpu.VMEM)] * count


def pin_kernel(weight, own, swapped, out, sem):
    columns = weight.shape[1]
    copy = pltpu.make_async_copy(weight, out.at[:, pl.ds(0, columns)], sem)
    copy.start()
    for at in range(0, weight.shape[0], DEPTH):
        cut = pl.ds(at, DEPTH)
        out[cut, columns:] = jnp.concatenate([own[:, cut], swapped[:, cut]], axis=0).T
    copy.wait()


def pin_call(weight, own, swapped):
    width, columns = weight.shape
    return pl.pallas_call(
        pin_kernel,
        in_specs=[pl.BlockSpec(memory_space=pl.ANY)] + in_vmem(2),
        out_specs=in_vmem(1)[0],
        out_shape=pltpu.VMEM((width, columns + 2 * own.shape[0]), weight.dtype),
        scratch_shapes=[pltpu.SemaphoreType.DMA],
        name="pin",
        **settings(),
    )(weight, own, swapped)


def rows_kernel(group, table, weights, *refs):
    *pieces, shrunk, base, shrunk_out = refs
    columns = base.shape[1]
    total = None
    for at in range(0, weights.shape[0], DEPTH):
        cut = pl.ds(at, DEPTH)
        x = [p[:, cut] for p in pieces]
        x = x[0] if len(x) == 1 else jnp.concatenate(x, axis=0)
        part = jnp.dot(x, weights[cut, :], preferred_element_type=jnp.float32)
        total = part if total is None else total + part
    base[...] = total[:, :columns]
    lane = lax.broadcasted_iota(jnp.int32, shrunk.shape, 1)
    row = lax.broadcasted_iota(jnp.int32, shrunk.shape, 0)
    use = jnp.where(
        row < HALF,
        jnp.where(lane < 64, table[0, 2 * group], table[1, 2 * group]),
        jnp.where(lane < 64, table[0, 2 * group + 1], table[1, 2 * group + 1]),
    )
    small = total[:, columns:].astype(jnp.bfloat16).astype(jnp.float32)
    old = shrunk[...].astype(jnp.float32)
    shrunk_out[...] = jnp.where(use > 0, small, old).astype(jnp.bfloat16)


def rows_call(group, table, weights, pieces, shrunk):
    columns = weights.shape[1] - 128
    operands = [pltpu.with_memory_space_constraint(weights, pltpu.VMEM)] + pieces + [shrunk]
    return pl.pallas_call(
        functools.partial(rows_kernel, group),
        in_specs=[pl.BlockSpec(memory_space=pltpu.SMEM)] + in_vmem(len(operands)),
        out_specs=in_vmem(2),
        out_shape=[
            jax.ShapeDtypeStruct((BLOCK, columns), jnp.float32),
            jax.ShapeDtypeStruct((BLOCK, 128), jnp.bfloat16),
        ],
        name="rows",
        **settings(flops=10**11 if group == 7 else 1),
    )(table, *operands)


def pack_kernel(table, up, out):
    part = out.shape[3]
    for t in range(8):
        at = pl.multiple_of((2 * t + table[2]) * part, part)
        out[0, t] = up[0, :, pl.ds(at, part)]


def pack_call(table, up_maps):
    _, rank, width = up_maps.shape
    part = width // 16
    return pl.pallas_call(
        pack_kernel,
        grid_spec=pltpu.PrefetchScalarGridSpec(
            num_scalar_prefetch=1,
            grid=(2,),
            in_specs=[pl.BlockSpec((1, rank, width), lambda s, t: (t[s], 0, 0))],
            out_specs=pl.BlockSpec((1, 8, rank, part), lambda s, t: (s, 0, 0, 0)),
        ),
        out_shape=jax.ShapeDtypeStruct((2, 8, rank, part), jnp.bfloat16),
        name="pack",
        **settings(),
    )(table, pltpu.with_memory_space_constraint(up_maps, pltpu.HBM))


def take_kernel(table, got, out):
    out[...] = got[...]


def take_call(table, got):
    _, rank, part = got.shape
    return pl.pallas_call(
        take_kernel,
        grid_spec=pltpu.PrefetchScalarGridSpec(
            num_scalar_prefetch=1,
            grid=(8,),
            in_specs=[pl.BlockSpec((1, rank, part), lambda b, t: (t[b], 0, 0))],
            out_specs=pl.BlockSpec((1, rank, part), lambda b, t: (b, 0, 0)),
        ),
        out_shape=jax.ShapeDtypeStruct((8, rank, part), jnp.bfloat16),
        name="take",
        **settings(),
    )(table, got)


def finish_kernel(table, *refs):
    bases, gathered, refs = refs[:8], refs[8:12], refs[12:]
    up_mine, up_other, out, base, shrunk, rows, base_sems, sems = refs
    part = up_mine.shape[2]
    group = table[3, 0]
    fetches = [pltpu.make_async_copy(bases[g], base.at[g], base_sems.at[g]) for g in range(8)]
    for fetch in fetches:
        fetch.start()
    for i, pair in enumerate(gathered):
        shrunk[pl.ds(2 * i, 2)] = pair[...]
    copies = []
    for i in range(16):
        block, half = table[0, i], i % 2
        if half == 0:
            fetches[i // 2].wait()
        own = pl.ds(half * HALF, HALF)
        both = shrunk[table[1, i], own, :].astype(jnp.float32)
        value = jnp.where(table[2, i] > 0, both[:, 64:], both[:, :64]).astype(jnp.bfloat16)
        for up, side in ((up_mine, group), (up_other, 1 - group)):
            cut = pl.ds(pl.multiple_of(side * part, part), part)
            grown = jnp.dot(value, up[block], preferred_element_type=jnp.float32)
            rows[i, :, cut] = (base[i // 2, own, cut] + 0.5 * grown).astype(rows.dtype)
        to = pl.ds(pl.multiple_of((2 * block + half) * HALF, HALF), HALF)
        copies.append(pltpu.make_async_copy(rows.at[i], out.at[to], sems.at[i]))
        copies[-1].start()
    for copy in copies:
        copy.wait()


def finish_call(table, bases, gathered, up_mine, up_other):
    columns = bases[0].shape[1]
    return pl.pallas_call(
        finish_kernel,
        in_specs=[pl.BlockSpec(memory_space=pltpu.SMEM)]
        + [pl.BlockSpec(memory_space=pl.ANY)] * 8
        + in_vmem(6),
        out_specs=pl.BlockSpec(memory_space=pltpu.HBM),
        out_shape=jax.ShapeDtypeStruct((8 * BLOCK, columns), jnp.bfloat16),
        scratch_shapes=[
            pltpu.VMEM((8, BLOCK, columns), jnp.float32),
            pltpu.VMEM((8,) + gathered[0].shape[1:], jnp.bfloat16),
            pltpu.VMEM((16, HALF, columns), jnp.bfloat16),
            pltpu.SemaphoreType.DMA((8,)),
            pltpu.SemaphoreType.DMA((16,)),
        ],
        name="finish",
        **settings(),
    )(
        table,
        *[pltpu.with_memory_space_constraint(base, pltpu.HBM) for base in bases],
        *gathered,
        up_mine,
        up_other,
    )


def chain_body(
    tokens, query_weight, adapter_down_maps, adapter_up_maps, adapter_home_slot, adapter_per_block
):
    me = lax.axis_index("tensor")
    z, y = me // 2, me % 2
    store = lax.axis_index("store")
    group = lax.axis_index("groups")
    myself = me * 2 + store
    held, rank, width = adapter_down_maps.shape
    rows = tokens[0]
    halves = [rows[:HALF], rows[HALF:]]

    ahead, back = list(halves), list(halves[::-1])
    flight = [(send(ahead[k], AHEAD), send(back[k], BACK)) for k in range(2)]
    got, ahead, back, adapter_home_slot, adapter_per_block = lax.optimization_barrier(
        (flight[0], ahead, back, adapter_home_slot, adapter_per_block)
    )
    ahead.append(got[0])
    back.append(got[1])
    flight.append((send(ahead[2], AHEAD), send(back[2], BACK)))

    store_slots = find_slots(adapter_home_slot, adapter_per_block)
    owner = store_slots // held
    inside = store_slots % held
    picked = jnp.max(jnp.where(owner == myself, inside, 0), axis=1)
    owner_row = lax.dynamic_index_in_dim(owner, store, 0, keepdims=False).astype(jnp.int32)
    pick_own = lax.dynamic_index_in_dim(picked, store, 0, keepdims=False)
    pick_lent = lax.dynamic_index_in_dim(picked, 1 - store, 0, keepdims=False)

    down_own = lax.dynamic_index_in_dim(adapter_down_maps, pick_own, 0, keepdims=False)
    down_lent = lax.dynamic_index_in_dim(adapter_down_maps, pick_lent, 0, keepdims=False)
    down_swapped = swap(down_lent, "store")
    weights = pin_call(query_weight, down_own, down_swapped)
    choice = jnp.stack([pick_own, pick_lent, group.astype(pick_own.dtype)]).astype(jnp.int32)
    up_sent = pack_call(choice, adapter_up_maps)
    up_sent = jnp.stack([up_sent[0], swap(up_sent[1], "store")], axis=1)

    position = jnp.where(y == 0, z, 7 - z)
    places = []
    for k in range(8):
        step = (k + 1) // 2
        places += [position - step, position + step] if k % 2 else [position + step, position - step]
    places = jnp.stack(places) % 8
    blocks = jnp.where(places < 4, 2 * places, 15 - 2 * places).astype(jnp.int32)
    hit = blocks[:, None] == jnp.arange(8, dtype=jnp.int32)[None, :]
    owners = jnp.sum(jnp.where(hit, owner_row[None, :], 0), axis=1)
    table = jnp.stack([owners == myself, owners == me * 2 + 1 - store]).astype(jnp.int32)

    bases = []
    shrunk = jnp.zeros((BLOCK, 2 * rank), jnp.bfloat16)
    groups = [[rows], [ahead[2], back[2]]]
    for k in range(1, 7):
        (got_ahead, got_back), ahead, back, bases, shrunk, up_sent = lax.optimization_barrier(
            (flight[k], ahead, back, bases, shrunk, up_sent)
        )
        ahead.append(got_ahead)
        back.append(got_back)
        if k < 5:
            flight.append((send(ahead[k + 2], AHEAD), send(back[k + 2], BACK)))
        if k == 5:
            up_got = lax.all_to_all(up_sent, "tensor", split_axis=0, concat_axis=0, tiled=True)
        groups.append([got_ahead, got_back] if k % 2 == 0 else [got_back, got_ahead])
        for g in range(len(bases), min(len(bases) + 2, k + 2, 7)):
            base, shrunk = rows_call(g, table, weights, groups[g], shrunk)
            bases.append(base)
    base, shrunk = rows_call(7, table, weights, groups[7], shrunk)
    bases.append(base)

    across = send(shrunk, ACROSS)
    pair = jnp.stack([shrunk, across])
    everyone = [pair] + [send(pair, pairs) for pairs in ALONG]
    up_got, everyone = lax.optimization_barrier((up_got, everyone))
    home, core = owner_row // 2, owner_row % 2
    chosen = 2 * home + jnp.where(core == store, 0, 1)
    up_mine = take_call(chosen.astype(jnp.int32), up_got.reshape(16, rank, -1))
    up_other = swap(up_mine, "groups")
    home, core = owners // 2, owners % 2
    where = 2 * ((home // 2) ^ z) + ((home % 2) ^ y)
    table = jnp.stack([blocks, where, core != store, jnp.broadcast_to(group, (16,))])
    return finish_call(table.astype(jnp.int32), bases, everyone, up_mine, up_other)[None]


def body(tokens, *rest):
    sizes = tuple(lax.axis_size(name) for name in ("groups", "tensor", "store"))
    fits = sizes == (2, 8, 2) and tokens.shape[1] == BLOCK
    return (chain_body if fits else general_body)(tokens, *rest)


def solution(mesh):
    placed = (
        P(("groups", "store"), "tensor", None),
        P(None, "tensor"),
        P(("tensor", "store"), None, None),
        P(("tensor", "store"), None, None),
        P(),
        P(),
    )
    return jax.shard_map(
        body,
        mesh=mesh,
        in_specs=placed,
        out_specs=P(("groups", "store"), None, "tensor"),
        check_vma=False,
    )
```

```python
import functools

import jax
import jax.numpy as jnp
from jax import lax
from jax.experimental import pallas as pl
from jax.experimental.pallas import tpu as pltpu
from jax.sharding import PartitionSpec as P

BLOCK = 128


def find_slots(adapter_home_slot, adapter_per_block):
    catalog = jnp.arange(adapter_home_slot.shape[0], dtype=jnp.int32)
    return jnp.sum(
        jnp.where(
            adapter_per_block[:, :, None] == catalog[None, None, :],
            adapter_home_slot[None, None, :],
            0,
        ),
        axis=2,
    )


def general_body(
    tokens, query_weight, adapter_down_maps, adapter_up_maps, adapter_home_slot, adapter_per_block
):
    shard_count = lax.axis_size("tensor")
    store_count = lax.axis_size("store")
    devices_all = shard_count * store_count
    my_tensor = lax.axis_index("tensor")
    my_store = lax.axis_index("store")
    myself = lax.axis_index(("tensor", "store"))
    held_adapters, rank_index, feature_width = adapter_down_maps.shape
    feature_index = query_weight.shape[1]
    own_rows = tokens[0]
    group_rows = own_rows.shape[0] * shard_count
    blocks = group_rows // BLOCK
    store_slots = find_slots(adapter_home_slot, adapter_per_block)
    owner = store_slots // held_adapters
    inside = store_slots % held_adapters
    picked = jnp.max(jnp.where(owner == myself, inside, -1), axis=1)
    select = (picked[:, None] == jnp.arange(held_adapters, dtype=jnp.int32)[None, :]).astype(
        jnp.bfloat16
    )
    down_map_parts = adapter_down_maps.reshape(
        held_adapters, rank_index, shard_count, feature_index
    )
    up_map_parts = adapter_up_maps.reshape(held_adapters, rank_index, shard_count, feature_index)
    send_down = jnp.einsum(
        "sl,lrtf->tsrf", select, down_map_parts, preferred_element_type=jnp.float32
    ).astype(jnp.bfloat16)
    send_up = jnp.einsum(
        "sl,lrtf->tsrf", select, up_map_parts, preferred_element_type=jnp.float32
    ).astype(jnp.bfloat16)
    recv_down, recv_up = (
        lax.all_to_all(
            sent.reshape(devices_all, rank_index, feature_index),
            ("tensor", "store"),
            split_axis=0,
            concat_axis=0,
            tiled=True,
        )
        for sent in (send_down, send_up)
    )
    owner_row = lax.dynamic_index_in_dim(owner, my_store, 0, keepdims=False)
    source_pick = (owner_row[:, None] == jnp.arange(devices_all, dtype=jnp.int32)[None, :]).astype(
        jnp.bfloat16
    )
    block_down = jnp.einsum(
        "bj,jrf->brf", source_pick, recv_down, preferred_element_type=jnp.float32
    ).astype(jnp.bfloat16)
    block_up = jnp.einsum(
        "bj,jrf->brf", source_pick, recv_up, preferred_element_type=jnp.float32
    ).astype(jnp.bfloat16)
    piece = lax.all_gather(own_rows, "tensor", axis=0, tiled=True)
    product = jnp.dot(piece, query_weight, preferred_element_type=jnp.float32)
    features = lax.dynamic_slice_in_dim(piece, my_tensor * feature_index, feature_index, 1)
    partial_value = jnp.einsum(
        "bnf,brf->bnr",
        features.reshape(blocks, BLOCK, feature_index),
        block_down,
        preferred_element_type=jnp.float32,
    )
    shrunk = lax.psum(partial_value, "tensor").astype(jnp.bfloat16)
    grown = jnp.einsum(
        "bnr,brf->bnf", shrunk, block_up, preferred_element_type=jnp.float32
    ).reshape(group_rows, feature_index)
    query = (product + 0.5 * grown).astype(jnp.bfloat16)
    return query[None]


def both_ways(pairs):
    return pairs + [(b, a) for a, b in pairs]


RING = [0, 2, 4, 6, 7, 5, 3, 1]
AHEAD = [(RING[i], RING[(i + 1) % 8]) for i in range(8)]
BACK = [(b, a) for a, b in AHEAD]
ACROSS = [(i, i ^ 1) for i in range(8)]
ALONG = [[(i, i ^ (2 * d)) for i in range(8)] for d in (1, 2, 3)]
HALF = BLOCK // 2
DEPTH = 1024
VMEM_LIMIT = 16 * 1024 * 1024


def send(value, pairs):
    return lax.ppermute(value, "tensor", pairs)


def swap(value, axis):
    return lax.ppermute(value, axis, [(0, 1), (1, 0)])


def settings(flops=1):
    return dict(
        compiler_params=pltpu.CompilerParams(vmem_limit_bytes=VMEM_LIMIT),
        cost_estimate=pl.CostEstimate(flops=flops, bytes_accessed=1, transcendentals=0),
    )


def in_vmem(count):
    return [pl.BlockSpec(memory_space=pltpu.VMEM)] * count


def pin_kernel(weight, own, swapped, out, sem):
    columns = weight.shape[1]
    copy = pltpu.make_async_copy(weight, out.at[:, pl.ds(0, columns)], sem)
    copy.start()
    for at in range(0, weight.shape[0], DEPTH):
        cut = pl.ds(at, DEPTH)
        out[cut, columns:] = jnp.concatenate([own[:, cut], swapped[:, cut]], axis=0).T
    copy.wait()


def pin_call(weight, own, swapped):
    width, columns = weight.shape
    return pl.pallas_call(
        pin_kernel,
        in_specs=[pl.BlockSpec(memory_space=pl.ANY)] + in_vmem(2),
        out_specs=in_vmem(1)[0],
        out_shape=pltpu.VMEM((width, columns + 2 * own.shape[0]), weight.dtype),
        scratch_shapes=[pltpu.SemaphoreType.DMA],
        name="pin",
        **settings(),
    )(weight, own, swapped)


def rows_kernel(group, table, weights, *refs):
    *pieces, shrunk, base, shrunk_out = refs
    columns = base.shape[1]
    total = None
    for at in range(0, weights.shape[0], DEPTH):
        cut = pl.ds(at, DEPTH)
        x = [p[:, cut] for p in pieces]
        x = x[0] if len(x) == 1 else jnp.concatenate(x, axis=0)
        part = jnp.dot(x, weights[cut, :], preferred_element_type=jnp.float32)
        total = part if total is None else total + part
    base[...] = total[:, :columns]
    lane = lax.broadcasted_iota(jnp.int32, shrunk.shape, 1)
    row = lax.broadcasted_iota(jnp.int32, shrunk.shape, 0)
    use = jnp.where(
        row < HALF,
        jnp.where(lane < 64, table[0, 2 * group], table[1, 2 * group]),
        jnp.where(lane < 64, table[0, 2 * group + 1], table[1, 2 * group + 1]),
    )
    small = total[:, columns:].astype(jnp.bfloat16).astype(jnp.float32)
    old = shrunk[...].astype(jnp.float32)
    shrunk_out[...] = jnp.where(use > 0, small, old).astype(jnp.bfloat16)


def rows_call(group, table, weights, pieces, shrunk):
    columns = weights.shape[1] - 128
    operands = [pltpu.with_memory_space_constraint(weights, pltpu.VMEM)] + pieces + [shrunk]
    return pl.pallas_call(
        functools.partial(rows_kernel, group),
        in_specs=[pl.BlockSpec(memory_space=pltpu.SMEM)] + in_vmem(len(operands)),
        out_specs=in_vmem(2),
        out_shape=[
            jax.ShapeDtypeStruct((BLOCK, columns), jnp.float32),
            jax.ShapeDtypeStruct((BLOCK, 128), jnp.bfloat16),
        ],
        name="rows",
        **settings(flops=10**11 if group == 7 else 1),
    )(table, *operands)


def pack_kernel(table, up, out):
    part = out.shape[3]
    for t in range(8):
        at = pl.multiple_of((2 * t + table[2]) * part, part)
        out[0, t] = up[0, :, pl.ds(at, part)]


def pack_call(table, up_maps):
    _, rank, width = up_maps.shape
    part = width // 16
    return pl.pallas_call(
        pack_kernel,
        grid_spec=pltpu.PrefetchScalarGridSpec(
            num_scalar_prefetch=1,
            grid=(2,),
            in_specs=[pl.BlockSpec((1, rank, width), lambda s, t: (t[s], 0, 0))],
            out_specs=pl.BlockSpec((1, 8, rank, part), lambda s, t: (s, 0, 0, 0)),
        ),
        out_shape=jax.ShapeDtypeStruct((2, 8, rank, part), jnp.bfloat16),
        name="pack",
        **settings(),
    )(table, pltpu.with_memory_space_constraint(up_maps, pltpu.HBM))


def take_kernel(table, got, out):
    out[...] = got[...]


def take_call(table, got):
    _, rank, part = got.shape
    return pl.pallas_call(
        take_kernel,
        grid_spec=pltpu.PrefetchScalarGridSpec(
            num_scalar_prefetch=1,
            grid=(8,),
            in_specs=[pl.BlockSpec((1, rank, part), lambda b, t: (t[b], 0, 0))],
            out_specs=pl.BlockSpec((1, rank, part), lambda b, t: (b, 0, 0)),
        ),
        out_shape=jax.ShapeDtypeStruct((8, rank, part), jnp.bfloat16),
        name="take",
        **settings(),
    )(table, got)


def finish_kernel(own_side, table, *refs):
    bases, gathered, up, refs = refs[:8], refs[8:12], refs[12], refs[-6:]
    out, base, shrunk, rows, base_sems, sems = refs
    part = up.shape[2]
    side = table[3, 0] if own_side else 1 - table[3, 0]
    cut = pl.ds(pl.multiple_of(side * part, part), part)
    fetches = [
        pltpu.make_async_copy(bases[g].at[:, cut], base.at[g], base_sems.at[g]) for g in range(8)
    ]
    for fetch in fetches:
        fetch.start()
    for i, pair in enumerate(gathered):
        shrunk[pl.ds(2 * i, 2)] = pair[...]
    copies = []
    for i in range(16):
        block, half = table[0, i], i % 2
        if half == 0:
            fetches[i // 2].wait()
        own = pl.ds(half * HALF, HALF)
        both = shrunk[table[1, i], own, :].astype(jnp.float32)
        value = jnp.where(table[2, i] > 0, both[:, 64:], both[:, :64]).astype(jnp.bfloat16)
        grown = jnp.dot(value, up[block], preferred_element_type=jnp.float32)
        rows[i] = (base[i // 2, own, :] + 0.5 * grown).astype(rows.dtype)
        to = pl.ds(pl.multiple_of((2 * block + half) * HALF, HALF), HALF)
        copies.append(pltpu.make_async_copy(rows.at[i], out.at[to, cut], sems.at[i]))
        copies[-1].start()
    for copy in copies:
        copy.wait()


def finish_call(own_side, table, bases, gathered, up, into):
    columns = bases[0].shape[1]
    part = up.shape[2]
    operands = [pltpu.with_memory_space_constraint(base, pltpu.HBM) for base in bases]
    operands += [*gathered, up]
    specs = [pl.BlockSpec(memory_space=pl.ANY)] * 8 + in_vmem(5)
    aliases = {}
    if into is not None:
        aliases = {1 + len(operands): 0}
        operands.append(pltpu.with_memory_space_constraint(into, pltpu.HBM))
        specs.append(pl.BlockSpec(memory_space=pltpu.HBM))
    return pl.pallas_call(
        functools.partial(finish_kernel, own_side),
        in_specs=[pl.BlockSpec(memory_space=pltpu.SMEM)] + specs,
        out_specs=pl.BlockSpec(memory_space=pltpu.HBM),
        out_shape=jax.ShapeDtypeStruct((8 * BLOCK, columns), jnp.bfloat16),
        scratch_shapes=[
            pltpu.VMEM((8, BLOCK, part), jnp.float32),
            pltpu.VMEM((8,) + gathered[0].shape[1:], jnp.bfloat16),
            pltpu.VMEM((16, HALF, part), jnp.bfloat16),
            pltpu.SemaphoreType.DMA((8,)),
            pltpu.SemaphoreType.DMA((16,)),
        ],
        input_output_aliases=aliases,
        name="finish",
        **settings(),
    )(table, *operands)


def chain_body(
    tokens, query_weight, adapter_down_maps, adapter_up_maps, adapter_home_slot, adapter_per_block
):
    me = lax.axis_index("tensor")
    z, y = me // 2, me % 2
    store = lax.axis_index("store")
    group = lax.axis_index("groups")
    myself = me * 2 + store
    held, rank, width = adapter_down_maps.shape
    rows = tokens[0]
    halves = [rows[:HALF], rows[HALF:]]

    ahead, back = list(halves), list(halves[::-1])
    flight = [(send(ahead[k], AHEAD), send(back[k], BACK)) for k in range(2)]
    got, ahead, back, adapter_home_slot, adapter_per_block = lax.optimization_barrier(
        (flight[0], ahead, back, adapter_home_slot, adapter_per_block)
    )
    ahead.append(got[0])
    back.append(got[1])
    flight.append((send(ahead[2], AHEAD), send(back[2], BACK)))

    store_slots = find_slots(adapter_home_slot, adapter_per_block)
    owner = store_slots // held
    inside = store_slots % held
    picked = jnp.max(jnp.where(owner == myself, inside, 0), axis=1)
    owner_row = lax.dynamic_index_in_dim(owner, store, 0, keepdims=False).astype(jnp.int32)
    pick_own = lax.dynamic_index_in_dim(picked, store, 0, keepdims=False)
    pick_lent = lax.dynamic_index_in_dim(picked, 1 - store, 0, keepdims=False)

    down_own = lax.dynamic_index_in_dim(adapter_down_maps, pick_own, 0, keepdims=False)
    down_lent = lax.dynamic_index_in_dim(adapter_down_maps, pick_lent, 0, keepdims=False)
    down_swapped = swap(down_lent, "store")
    weights = pin_call(query_weight, down_own, down_swapped)
    choice = jnp.stack([pick_own, pick_lent, group.astype(pick_own.dtype)]).astype(jnp.int32)
    up_sent = pack_call(choice, adapter_up_maps)
    up_sent = jnp.stack([up_sent[0], swap(up_sent[1], "store")], axis=1)

    position = jnp.where(y == 0, z, 7 - z)
    places = []
    for k in range(8):
        step = (k + 1) // 2
        places += [position - step, position + step] if k % 2 else [position + step, position - step]
    places = jnp.stack(places) % 8
    blocks = jnp.where(places < 4, 2 * places, 15 - 2 * places).astype(jnp.int32)
    hit = blocks[:, None] == jnp.arange(8, dtype=jnp.int32)[None, :]
    owners = jnp.sum(jnp.where(hit, owner_row[None, :], 0), axis=1)
    table = jnp.stack([owners == myself, owners == me * 2 + 1 - store]).astype(jnp.int32)

    bases = []
    shrunk = jnp.zeros((BLOCK, 2 * rank), jnp.bfloat16)
    groups = [[rows], [ahead[2], back[2]]]
    for k in range(1, 7):
        (got_ahead, got_back), ahead, back, bases, shrunk, up_sent = lax.optimization_barrier(
            (flight[k], ahead, back, bases, shrunk, up_sent)
        )
        ahead.append(got_ahead)
        back.append(got_back)
        if k < 5:
            flight.append((send(ahead[k + 2], AHEAD), send(back[k + 2], BACK)))
        if k == 5:
            up_got = lax.all_to_all(up_sent, "tensor", split_axis=0, concat_axis=0, tiled=True)
        groups.append([got_ahead, got_back] if k % 2 == 0 else [got_back, got_ahead])
        for g in range(len(bases), min(len(bases) + 2, k + 2, 7)):
            base, shrunk = rows_call(g, table, weights, groups[g], shrunk)
            bases.append(base)
    base, shrunk = rows_call(7, table, weights, groups[7], shrunk)
    bases.append(base)

    across = send(shrunk, ACROSS)
    pair = jnp.stack([shrunk, across])
    everyone = [pair] + [send(pair, pairs) for pairs in ALONG]
    up_got, _ = lax.optimization_barrier((up_got, across))
    home, core = owner_row // 2, owner_row % 2
    chosen = 2 * home + jnp.where(core == store, 0, 1)
    up_mine = take_call(chosen.astype(jnp.int32), up_got.reshape(16, rank, -1))
    up_other = swap(up_mine, "groups")
    home, core = owners // 2, owners % 2
    where = 2 * ((home // 2) ^ z) + ((home % 2) ^ y)
    table = jnp.stack([blocks, where, core != store, jnp.broadcast_to(group, (16,))])
    table = table.astype(jnp.int32)
    query = finish_call(True, table, bases, everyone, up_mine, None)
    return finish_call(False, table, bases, everyone, up_other, query)[None]


def body(tokens, *rest):
    sizes = tuple(lax.axis_size(name) for name in ("groups", "tensor", "store"))
    fits = sizes == (2, 8, 2) and tokens.shape[1] == BLOCK
    return (chain_body if fits else general_body)(tokens, *rest)


def solution(mesh):
    placed = (
        P(("groups", "store"), "tensor", None),
        P(None, "tensor"),
        P(("tensor", "store"), None, None),
        P(("tensor", "store"), None, None),
        P(),
        P(),
    )
    return jax.shard_map(
        body,
        mesh=mesh,
        in_specs=placed,
        out_specs=P(("groups", "store"), None, "tensor"),
        check_vma=False,
    )
```

```python
import functools

import jax
import jax.numpy as jnp
from jax import lax
from jax.experimental import pallas as pl
from jax.experimental.pallas import tpu as pltpu
from jax.sharding import PartitionSpec as P

BLOCK = 128


def find_slots(adapter_home_slot, adapter_per_block):
    catalog = jnp.arange(adapter_home_slot.shape[0], dtype=jnp.int32)
    return jnp.sum(
        jnp.where(
            adapter_per_block[:, :, None] == catalog[None, None, :],
            adapter_home_slot[None, None, :],
            0,
        ),
        axis=2,
    )


def general_body(
    tokens, query_weight, adapter_down_maps, adapter_up_maps, adapter_home_slot, adapter_per_block
):
    shard_count = lax.axis_size("tensor")
    store_count = lax.axis_size("store")
    devices_all = shard_count * store_count
    my_tensor = lax.axis_index("tensor")
    my_store = lax.axis_index("store")
    myself = lax.axis_index(("tensor", "store"))
    held_adapters, rank_index, feature_width = adapter_down_maps.shape
    feature_index = query_weight.shape[1]
    own_rows = tokens[0]
    group_rows = own_rows.shape[0] * shard_count
    blocks = group_rows // BLOCK
    store_slots = find_slots(adapter_home_slot, adapter_per_block)
    owner = store_slots // held_adapters
    inside = store_slots % held_adapters
    picked = jnp.max(jnp.where(owner == myself, inside, -1), axis=1)
    select = (picked[:, None] == jnp.arange(held_adapters, dtype=jnp.int32)[None, :]).astype(
        jnp.bfloat16
    )
    down_map_parts = adapter_down_maps.reshape(
        held_adapters, rank_index, shard_count, feature_index
    )
    up_map_parts = adapter_up_maps.reshape(held_adapters, rank_index, shard_count, feature_index)
    send_down = jnp.einsum(
        "sl,lrtf->tsrf", select, down_map_parts, preferred_element_type=jnp.float32
    ).astype(jnp.bfloat16)
    send_up = jnp.einsum(
        "sl,lrtf->tsrf", select, up_map_parts, preferred_element_type=jnp.float32
    ).astype(jnp.bfloat16)
    recv_down, recv_up = (
        lax.all_to_all(
            sent.reshape(devices_all, rank_index, feature_index),
            ("tensor", "store"),
            split_axis=0,
            concat_axis=0,
            tiled=True,
        )
        for sent in (send_down, send_up)
    )
    owner_row = lax.dynamic_index_in_dim(owner, my_store, 0, keepdims=False)
    source_pick = (owner_row[:, None] == jnp.arange(devices_all, dtype=jnp.int32)[None, :]).astype(
        jnp.bfloat16
    )
    block_down = jnp.einsum(
        "bj,jrf->brf", source_pick, recv_down, preferred_element_type=jnp.float32
    ).astype(jnp.bfloat16)
    block_up = jnp.einsum(
        "bj,jrf->brf", source_pick, recv_up, preferred_element_type=jnp.float32
    ).astype(jnp.bfloat16)
    piece = lax.all_gather(own_rows, "tensor", axis=0, tiled=True)
    product = jnp.dot(piece, query_weight, preferred_element_type=jnp.float32)
    features = lax.dynamic_slice_in_dim(piece, my_tensor * feature_index, feature_index, 1)
    partial_value = jnp.einsum(
        "bnf,brf->bnr",
        features.reshape(blocks, BLOCK, feature_index),
        block_down,
        preferred_element_type=jnp.float32,
    )
    shrunk = lax.psum(partial_value, "tensor").astype(jnp.bfloat16)
    grown = jnp.einsum(
        "bnr,brf->bnf", shrunk, block_up, preferred_element_type=jnp.float32
    ).reshape(group_rows, feature_index)
    query = (product + 0.5 * grown).astype(jnp.bfloat16)
    return query[None]


def both_ways(pairs):
    return pairs + [(b, a) for a, b in pairs]


RING = [0, 2, 4, 6, 7, 5, 3, 1]
AHEAD = [(RING[i], RING[(i + 1) % 8]) for i in range(8)]
BACK = [(b, a) for a, b in AHEAD]
ACROSS = [(i, i ^ 1) for i in range(8)]
ALONG = [[(i, i ^ (2 * d)) for i in range(8)] for d in (1, 2, 3)]
HALF = BLOCK // 2
DEPTH = 1024
VMEM_LIMIT = 16 * 1024 * 1024


def send(value, pairs):
    return lax.ppermute(value, "tensor", pairs)


def swap(value, axis):
    return lax.ppermute(value, axis, [(0, 1), (1, 0)])


def settings(flops=1):
    return dict(
        compiler_params=pltpu.CompilerParams(vmem_limit_bytes=VMEM_LIMIT),
        cost_estimate=pl.CostEstimate(flops=flops, bytes_accessed=1, transcendentals=0),
    )


def in_vmem(count):
    return [pl.BlockSpec(memory_space=pltpu.VMEM)] * count


def pin_kernel(weight, own, swapped, out, sem):
    columns = weight.shape[1]
    copy = pltpu.make_async_copy(weight, out.at[:, pl.ds(0, columns)], sem)
    copy.start()
    for at in range(0, weight.shape[0], DEPTH):
        cut = pl.ds(at, DEPTH)
        out[cut, columns:] = jnp.concatenate([own[:, cut], swapped[:, cut]], axis=0).T
    copy.wait()


def pin_call(weight, own, swapped):
    width, columns = weight.shape
    return pl.pallas_call(
        pin_kernel,
        in_specs=[pl.BlockSpec(memory_space=pl.ANY)] + in_vmem(2),
        out_specs=in_vmem(1)[0],
        out_shape=pltpu.VMEM((width, columns + 2 * own.shape[0]), weight.dtype),
        scratch_shapes=[pltpu.SemaphoreType.DMA],
        name="pin",
        **settings(),
    )(weight, own, swapped)


def rows_kernel(group, table, weights, *refs):
    *pieces, shrunk, base, shrunk_out = refs
    columns = base.shape[1]
    total = None
    for at in range(0, weights.shape[0], DEPTH):
        cut = pl.ds(at, DEPTH)
        x = [p[:, cut] for p in pieces]
        x = x[0] if len(x) == 1 else jnp.concatenate(x, axis=0)
        part = jnp.dot(x, weights[cut, :], preferred_element_type=jnp.float32)
        total = part if total is None else total + part
    base[...] = total[:, :columns]
    lane = lax.broadcasted_iota(jnp.int32, shrunk.shape, 1)
    row = lax.broadcasted_iota(jnp.int32, shrunk.shape, 0)
    use = jnp.where(
        row < HALF,
        jnp.where(lane < 64, table[0, 2 * group], table[1, 2 * group]),
        jnp.where(lane < 64, table[0, 2 * group + 1], table[1, 2 * group + 1]),
    )
    small = total[:, columns:].astype(jnp.bfloat16).astype(jnp.float32)
    old = shrunk[...].astype(jnp.float32)
    shrunk_out[...] = jnp.where(use > 0, small, old).astype(jnp.bfloat16)


def rows_call(group, table, weights, pieces, shrunk):
    columns = weights.shape[1] - 128
    operands = [pltpu.with_memory_space_constraint(weights, pltpu.VMEM)] + pieces + [shrunk]
    return pl.pallas_call(
        functools.partial(rows_kernel, group),
        in_specs=[pl.BlockSpec(memory_space=pltpu.SMEM)] + in_vmem(len(operands)),
        out_specs=in_vmem(2),
        out_shape=[
            jax.ShapeDtypeStruct((BLOCK, columns), jnp.float32),
            jax.ShapeDtypeStruct((BLOCK, 128), jnp.bfloat16),
        ],
        name="rows",
        **settings(flops=10**11 if group == 7 else 1),
    )(table, *operands)


def pack_kernel(table, up, out):
    part = out.shape[3]
    for t in range(8):
        at = pl.multiple_of((2 * t + table[2]) * part, part)
        out[0, t] = up[0, :, pl.ds(at, part)]


def pack_call(table, up_maps):
    _, rank, width = up_maps.shape
    part = width // 16
    return pl.pallas_call(
        pack_kernel,
        grid_spec=pltpu.PrefetchScalarGridSpec(
            num_scalar_prefetch=1,
            grid=(2,),
            in_specs=[pl.BlockSpec((1, rank, width), lambda s, t: (t[s], 0, 0))],
            out_specs=pl.BlockSpec((1, 8, rank, part), lambda s, t: (s, 0, 0, 0)),
        ),
        out_shape=jax.ShapeDtypeStruct((2, 8, rank, part), jnp.bfloat16),
        name="pack",
        **settings(),
    )(table, pltpu.with_memory_space_constraint(up_maps, pltpu.HBM))


def take_kernel(table, got, out):
    out[...] = got[...]


def take_call(table, got):
    _, rank, part = got.shape
    return pl.pallas_call(
        take_kernel,
        grid_spec=pltpu.PrefetchScalarGridSpec(
            num_scalar_prefetch=1,
            grid=(8,),
            in_specs=[pl.BlockSpec((1, rank, part), lambda b, t: (t[b], 0, 0))],
            out_specs=pl.BlockSpec((1, rank, part), lambda b, t: (b, 0, 0)),
        ),
        out_shape=jax.ShapeDtypeStruct((8, rank, part), jnp.bfloat16),
        name="take",
        **settings(),
    )(table, got)


def collect_kernel(*refs):
    *bases, out, sems = refs
    copies = [pltpu.make_async_copy(bases[g], out.at[g], sems.at[g]) for g in range(8)]
    for copy in copies:
        copy.start()
    for copy in copies:
        copy.wait()


def collect_call(bases):
    return pl.pallas_call(
        collect_kernel,
        in_specs=[pl.BlockSpec(memory_space=pl.ANY)] * 8,
        out_specs=in_vmem(1)[0],
        out_shape=pltpu.VMEM((8,) + bases[0].shape, jnp.float32),
        scratch_shapes=[pltpu.SemaphoreType.DMA((8,))],
        name="collect",
        **settings(),
    )(*[pltpu.with_memory_space_constraint(base, pltpu.HBM) for base in bases])


def finish_kernel(table, base, *refs):
    gathered, (mine, other, out, shrunk, rows, sems) = refs[:4], refs[4:]
    part = mine.shape[2]
    group = table[3, 0]
    for i, pair in enumerate(gathered):
        shrunk[pl.ds(2 * i, 2)] = pair[...]
    copies = []
    for i in range(16):
        block, half = table[0, i], i % 2
        own = pl.ds(half * HALF, HALF)
        both = shrunk[table[1, i], own, :].astype(jnp.float32)
        value = jnp.where(table[2, i] > 0, both[:, 64:], both[:, :64]).astype(jnp.bfloat16)
        for up, side in ((mine, group), (other, 1 - group)):
            cut = pl.ds(pl.multiple_of(side * part, part), part)
            grown = jnp.dot(value, up[block], preferred_element_type=jnp.float32)
            rows[i, :, cut] = (base[i // 2, own, cut] + 0.5 * grown).astype(rows.dtype)
        to = pl.ds(pl.multiple_of((2 * block + half) * HALF, HALF), HALF)
        copies.append(pltpu.make_async_copy(rows.at[i], out.at[to], sems.at[i]))
        copies[-1].start()
    for copy in copies:
        copy.wait()


def finish_call(table, base, gathered, ups):
    columns = base.shape[2]
    return pl.pallas_call(
        finish_kernel,
        in_specs=[pl.BlockSpec(memory_space=pltpu.SMEM)] + in_vmem(7),
        out_specs=pl.BlockSpec(memory_space=pltpu.HBM),
        out_shape=jax.ShapeDtypeStruct((8 * BLOCK, columns), jnp.bfloat16),
        scratch_shapes=[
            pltpu.VMEM((8,) + gathered[0].shape[1:], jnp.bfloat16),
            pltpu.VMEM((16, HALF, columns), jnp.bfloat16),
            pltpu.SemaphoreType.DMA((16,)),
        ],
        name="finish",
        **settings(),
    )(table, pltpu.with_memory_space_constraint(base, pltpu.VMEM), *gathered, *ups)


def chain_body(
    tokens, query_weight, adapter_down_maps, adapter_up_maps, adapter_home_slot, adapter_per_block
):
    me = lax.axis_index("tensor")
    z, y = me // 2, me % 2
    store = lax.axis_index("store")
    group = lax.axis_index("groups")
    myself = me * 2 + store
    held, rank, width = adapter_down_maps.shape
    rows = tokens[0]
    halves = [rows[:HALF], rows[HALF:]]

    ahead, back = list(halves), list(halves[::-1])
    flight = [(send(ahead[k], AHEAD), send(back[k], BACK)) for k in range(2)]
    got, ahead, back, adapter_home_slot, adapter_per_block = lax.optimization_barrier(
        (flight[0], ahead, back, adapter_home_slot, adapter_per_block)
    )
    ahead.append(got[0])
    back.append(got[1])
    flight.append((send(ahead[2], AHEAD), send(back[2], BACK)))

    store_slots = find_slots(adapter_home_slot, adapter_per_block)
    owner = store_slots // held
    inside = store_slots % held
    picked = jnp.max(jnp.where(owner == myself, inside, 0), axis=1)
    owner_row = lax.dynamic_index_in_dim(owner, store, 0, keepdims=False).astype(jnp.int32)
    pick_own = lax.dynamic_index_in_dim(picked, store, 0, keepdims=False)
    pick_lent = lax.dynamic_index_in_dim(picked, 1 - store, 0, keepdims=False)

    down_own = lax.dynamic_index_in_dim(adapter_down_maps, pick_own, 0, keepdims=False)
    down_lent = lax.dynamic_index_in_dim(adapter_down_maps, pick_lent, 0, keepdims=False)
    down_swapped = swap(down_lent, "store")
    weights = pin_call(query_weight, down_own, down_swapped)
    choice = jnp.stack([pick_own, pick_lent, group.astype(pick_own.dtype)]).astype(jnp.int32)
    up_sent = pack_call(choice, adapter_up_maps)
    up_sent = jnp.stack([up_sent[0], swap(up_sent[1], "store")], axis=1)

    position = jnp.where(y == 0, z, 7 - z)
    places = []
    for k in range(8):
        step = (k + 1) // 2
        places += [position - step, position + step] if k % 2 else [position + step, position - step]
    places = jnp.stack(places) % 8
    blocks = jnp.where(places < 4, 2 * places, 15 - 2 * places).astype(jnp.int32)
    hit = blocks[:, None] == jnp.arange(8, dtype=jnp.int32)[None, :]
    owners = jnp.sum(jnp.where(hit, owner_row[None, :], 0), axis=1)
    table = jnp.stack([owners == myself, owners == me * 2 + 1 - store]).astype(jnp.int32)

    bases = []
    shrunk = jnp.zeros((BLOCK, 2 * rank), jnp.bfloat16)
    groups = [[rows], [ahead[2], back[2]]]
    for k in range(1, 7):
        (got_ahead, got_back), ahead, back, bases, shrunk, up_sent = lax.optimization_barrier(
            (flight[k], ahead, back, bases, shrunk, up_sent)
        )
        ahead.append(got_ahead)
        back.append(got_back)
        if k < 5:
            flight.append((send(ahead[k + 2], AHEAD), send(back[k + 2], BACK)))
        if k == 5:
            up_got = lax.all_to_all(up_sent, "tensor", split_axis=0, concat_axis=0, tiled=True)
        groups.append([got_ahead, got_back] if k % 2 == 0 else [got_back, got_ahead])
        for g in range(len(bases), min(len(bases) + 2, k + 2, 7)):
            base, shrunk = rows_call(g, table, weights, groups[g], shrunk)
            bases.append(base)
    base, shrunk = rows_call(7, table, weights, groups[7], shrunk)
    bases.append(base)

    across = send(shrunk, ACROSS)
    pair = jnp.stack([shrunk, across])
    everyone = [pair] + [send(pair, pairs) for pairs in ALONG]
    up_got, _ = lax.optimization_barrier((up_got, across))
    home, core = owner_row // 2, owner_row % 2
    chosen = 2 * home + jnp.where(core == store, 0, 1)
    up_mine = take_call(chosen.astype(jnp.int32), up_got.reshape(16, rank, -1))
    up_other = swap(up_mine, "groups")
    home, core = owners // 2, owners % 2
    where = 2 * ((home // 2) ^ z) + ((home % 2) ^ y)
    table = jnp.stack([blocks, where, core != store, jnp.broadcast_to(group, (16,))])
    ups = [up_mine, up_other]
    return finish_call(table.astype(jnp.int32), collect_call(bases), everyone, ups)[None]


def body(tokens, *rest):
    sizes = tuple(lax.axis_size(name) for name in ("groups", "tensor", "store"))
    fits = sizes == (2, 8, 2) and tokens.shape[1] == BLOCK
    return (chain_body if fits else general_body)(tokens, *rest)


def solution(mesh):
    placed = (
        P(("groups", "store"), "tensor", None),
        P(None, "tensor"),
        P(("tensor", "store"), None, None),
        P(("tensor", "store"), None, None),
        P(),
        P(),
    )
    return jax.shard_map(
        body,
        mesh=mesh,
        in_specs=placed,
        out_specs=P(("groups", "store"), None, "tensor"),
        check_vma=False,
    )
```

```python
import functools

import jax
import jax.numpy as jnp
from jax import lax
from jax.experimental import pallas as pl
from jax.experimental.pallas import tpu as pltpu
from jax.sharding import PartitionSpec as P

BLOCK = 128


def find_slots(adapter_home_slot, adapter_per_block):
    catalog = jnp.arange(adapter_home_slot.shape[0], dtype=jnp.int32)
    return jnp.sum(
        jnp.where(
            adapter_per_block[:, :, None] == catalog[None, None, :],
            adapter_home_slot[None, None, :],
            0,
        ),
        axis=2,
    )


def general_body(
    tokens, query_weight, adapter_down_maps, adapter_up_maps, adapter_home_slot, adapter_per_block
):
    shard_count = lax.axis_size("tensor")
    store_count = lax.axis_size("store")
    devices_all = shard_count * store_count
    my_tensor = lax.axis_index("tensor")
    my_store = lax.axis_index("store")
    myself = lax.axis_index(("tensor", "store"))
    held_adapters, rank_index, feature_width = adapter_down_maps.shape
    feature_index = query_weight.shape[1]
    own_rows = tokens[0]
    group_rows = own_rows.shape[0] * shard_count
    blocks = group_rows // BLOCK
    store_slots = find_slots(adapter_home_slot, adapter_per_block)
    owner = store_slots // held_adapters
    inside = store_slots % held_adapters
    picked = jnp.max(jnp.where(owner == myself, inside, -1), axis=1)
    select = (picked[:, None] == jnp.arange(held_adapters, dtype=jnp.int32)[None, :]).astype(
        jnp.bfloat16
    )
    down_map_parts = adapter_down_maps.reshape(
        held_adapters, rank_index, shard_count, feature_index
    )
    up_map_parts = adapter_up_maps.reshape(held_adapters, rank_index, shard_count, feature_index)
    send_down = jnp.einsum(
        "sl,lrtf->tsrf", select, down_map_parts, preferred_element_type=jnp.float32
    ).astype(jnp.bfloat16)
    send_up = jnp.einsum(
        "sl,lrtf->tsrf", select, up_map_parts, preferred_element_type=jnp.float32
    ).astype(jnp.bfloat16)
    recv_down, recv_up = (
        lax.all_to_all(
            sent.reshape(devices_all, rank_index, feature_index),
            ("tensor", "store"),
            split_axis=0,
            concat_axis=0,
            tiled=True,
        )
        for sent in (send_down, send_up)
    )
    owner_row = lax.dynamic_index_in_dim(owner, my_store, 0, keepdims=False)
    source_pick = (owner_row[:, None] == jnp.arange(devices_all, dtype=jnp.int32)[None, :]).astype(
        jnp.bfloat16
    )
    block_down = jnp.einsum(
        "bj,jrf->brf", source_pick, recv_down, preferred_element_type=jnp.float32
    ).astype(jnp.bfloat16)
    block_up = jnp.einsum(
        "bj,jrf->brf", source_pick, recv_up, preferred_element_type=jnp.float32
    ).astype(jnp.bfloat16)
    piece = lax.all_gather(own_rows, "tensor", axis=0, tiled=True)
    product = jnp.dot(piece, query_weight, preferred_element_type=jnp.float32)
    features = lax.dynamic_slice_in_dim(piece, my_tensor * feature_index, feature_index, 1)
    partial_value = jnp.einsum(
        "bnf,brf->bnr",
        features.reshape(blocks, BLOCK, feature_index),
        block_down,
        preferred_element_type=jnp.float32,
    )
    shrunk = lax.psum(partial_value, "tensor").astype(jnp.bfloat16)
    grown = jnp.einsum(
        "bnr,brf->bnf", shrunk, block_up, preferred_element_type=jnp.float32
    ).reshape(group_rows, feature_index)
    query = (product + 0.5 * grown).astype(jnp.bfloat16)
    return query[None]


def both_ways(pairs):
    return pairs + [(b, a) for a, b in pairs]


RING = [0, 2, 4, 6, 7, 5, 3, 1]
AHEAD = [(RING[i], RING[(i + 1) % 8]) for i in range(8)]
BACK = [(b, a) for a, b in AHEAD]
ACROSS = [(i, i ^ 1) for i in range(8)]
ALONG = [[(i, i ^ (2 * d)) for i in range(8)] for d in (1, 2, 3)]
HALF = BLOCK // 2
DEPTH = 1024
VMEM_LIMIT = 16 * 1024 * 1024


def send(value, pairs):
    return lax.ppermute(value, "tensor", pairs)


def swap(value, axis):
    return lax.ppermute(value, axis, [(0, 1), (1, 0)])


def settings(flops=1):
    return dict(
        compiler_params=pltpu.CompilerParams(vmem_limit_bytes=VMEM_LIMIT),
        cost_estimate=pl.CostEstimate(flops=flops, bytes_accessed=1, transcendentals=0),
    )


def in_vmem(count):
    return [pl.BlockSpec(memory_space=pltpu.VMEM)] * count


def pin_kernel(weight, own, swapped, out, sem):
    columns = weight.shape[1]
    copy = pltpu.make_async_copy(weight, out.at[:, pl.ds(0, columns)], sem)
    copy.start()
    for at in range(0, weight.shape[0], DEPTH):
        cut = pl.ds(at, DEPTH)
        out[cut, columns:] = jnp.concatenate([own[:, cut], swapped[:, cut]], axis=0).T
    copy.wait()


def pin_call(weight, own, swapped):
    width, columns = weight.shape
    return pl.pallas_call(
        pin_kernel,
        in_specs=[pl.BlockSpec(memory_space=pl.ANY)] + in_vmem(2),
        out_specs=in_vmem(1)[0],
        out_shape=pltpu.VMEM((width, columns + 2 * own.shape[0]), weight.dtype),
        scratch_shapes=[pltpu.SemaphoreType.DMA],
        name="pin",
        **settings(),
    )(weight, own, swapped)


def rows_kernel(group, table, weights, *refs):
    *pieces, shrunk, base, shrunk_out = refs
    columns = base.shape[1]
    total = None
    for at in range(0, weights.shape[0], DEPTH):
        cut = pl.ds(at, DEPTH)
        x = [p[:, cut] for p in pieces]
        x = x[0] if len(x) == 1 else jnp.concatenate(x, axis=0)
        part = jnp.dot(x, weights[cut, :], preferred_element_type=jnp.float32)
        total = part if total is None else total + part
    base[...] = total[:, :columns]
    lane = lax.broadcasted_iota(jnp.int32, shrunk.shape, 1)
    row = lax.broadcasted_iota(jnp.int32, shrunk.shape, 0)
    use = jnp.where(
        row < HALF,
        jnp.where(lane < 64, table[0, 2 * group], table[1, 2 * group]),
        jnp.where(lane < 64, table[0, 2 * group + 1], table[1, 2 * group + 1]),
    )
    small = total[:, columns:].astype(jnp.bfloat16).astype(jnp.float32)
    old = shrunk[...].astype(jnp.float32)
    shrunk_out[...] = jnp.where(use > 0, small, old).astype(jnp.bfloat16)


def rows_call(group, table, weights, pieces, shrunk):
    columns = weights.shape[1] - 128
    operands = [pltpu.with_memory_space_constraint(weights, pltpu.VMEM)] + pieces + [shrunk]
    return pl.pallas_call(
        functools.partial(rows_kernel, group),
        in_specs=[pl.BlockSpec(memory_space=pltpu.SMEM)] + in_vmem(len(operands)),
        out_specs=in_vmem(2),
        out_shape=[
            jax.ShapeDtypeStruct((BLOCK, columns), jnp.float32),
            jax.ShapeDtypeStruct((BLOCK, 128), jnp.bfloat16),
        ],
        name="rows",
        **settings(flops=10**11 if group == 7 else 1),
    )(table, *operands)


def pack_kernel(table, up, out):
    part = out.shape[3]
    for t in range(8):
        at = pl.multiple_of((2 * t + table[2]) * part, part)
        out[0, t] = up[0, :, pl.ds(at, part)]


def pack_call(table, up_maps):
    _, rank, width = up_maps.shape
    part = width // 16
    return pl.pallas_call(
        pack_kernel,
        grid_spec=pltpu.PrefetchScalarGridSpec(
            num_scalar_prefetch=1,
            grid=(2,),
            in_specs=[pl.BlockSpec((1, rank, width), lambda s, t: (t[s], 0, 0))],
            out_specs=pl.BlockSpec((1, 8, rank, part), lambda s, t: (s, 0, 0, 0)),
        ),
        out_shape=jax.ShapeDtypeStruct((2, 8, rank, part), jnp.bfloat16),
        name="pack",
        **settings(),
    )(table, pltpu.with_memory_space_constraint(up_maps, pltpu.HBM))


def take_kernel(table, got, out):
    out[...] = got[...]


def take_call(table, got):
    _, rank, part = got.shape
    return pl.pallas_call(
        take_kernel,
        grid_spec=pltpu.PrefetchScalarGridSpec(
            num_scalar_prefetch=1,
            grid=(8,),
            in_specs=[pl.BlockSpec((1, rank, part), lambda b, t: (t[b], 0, 0))],
            out_specs=pl.BlockSpec((1, rank, part), lambda b, t: (b, 0, 0)),
        ),
        out_shape=jax.ShapeDtypeStruct((8, rank, part), jnp.bfloat16),
        name="take",
        **settings(),
    )(table, got)


def collect_kernel(*refs):
    *bases, out, sems = refs
    copies = [pltpu.make_async_copy(bases[g], out.at[g], sems.at[g]) for g in range(8)]
    for copy in copies:
        copy.start()
    for copy in copies:
        copy.wait()


def collect_call(bases):
    return pl.pallas_call(
        collect_kernel,
        in_specs=[pl.BlockSpec(memory_space=pl.ANY)] * 8,
        out_specs=in_vmem(1)[0],
        out_shape=pltpu.VMEM((8,) + bases[0].shape, jnp.float32),
        scratch_shapes=[pltpu.SemaphoreType.DMA((8,))],
        name="collect",
        **settings(),
    )(*[pltpu.with_memory_space_constraint(base, pltpu.HBM) for base in bases])


def finish_kernel(table, base, *refs):
    gathered, (mine_a, mine_b, other_a, other_b) = refs[:4], refs[4:8]
    out, shrunk, rows, sems = refs[8:]
    part = mine_a.shape[2]
    group = table[3, 0]
    for i, pair in enumerate(gathered):
        shrunk[pl.ds(2 * i, 2)] = pair[...]
    copies = []
    for i in range(16):
        block, half = table[0, i], i % 2
        own = pl.ds(half * HALF, HALF)
        both = shrunk[table[1, i], own, :].astype(jnp.float32)
        value = jnp.where(table[2, i] > 0, both[:, 64:], both[:, :64]).astype(jnp.bfloat16)
        for up, side in (((mine_a, mine_b), group), ((other_a, other_b), 1 - group)):
            cut = pl.ds(pl.multiple_of(side * part, part), part)
            up = jnp.concatenate([up[0][block], up[1][block]], axis=0)
            grown = jnp.dot(value, up, preferred_element_type=jnp.float32)
            rows[i, :, cut] = (base[i // 2, own, cut] + 0.5 * grown).astype(rows.dtype)
        to = pl.ds(pl.multiple_of((2 * block + half) * HALF, HALF), HALF)
        copies.append(pltpu.make_async_copy(rows.at[i], out.at[to], sems.at[i]))
        copies[-1].start()
    for copy in copies:
        copy.wait()


def finish_call(table, base, gathered, ups):
    columns = base.shape[2]
    return pl.pallas_call(
        finish_kernel,
        in_specs=[pl.BlockSpec(memory_space=pltpu.SMEM)] + in_vmem(9),
        out_specs=pl.BlockSpec(memory_space=pltpu.HBM),
        out_shape=jax.ShapeDtypeStruct((8 * BLOCK, columns), jnp.bfloat16),
        scratch_shapes=[
            pltpu.VMEM((8,) + gathered[0].shape[1:], jnp.bfloat16),
            pltpu.VMEM((16, HALF, columns), jnp.bfloat16),
            pltpu.SemaphoreType.DMA((16,)),
        ],
        name="finish",
        **settings(),
    )(table, pltpu.with_memory_space_constraint(base, pltpu.VMEM), *gathered, *ups)


def chain_body(
    tokens, query_weight, adapter_down_maps, adapter_up_maps, adapter_home_slot, adapter_per_block
):
    me = lax.axis_index("tensor")
    z, y = me // 2, me % 2
    store = lax.axis_index("store")
    group = lax.axis_index("groups")
    myself = me * 2 + store
    held, rank, width = adapter_down_maps.shape
    rows = tokens[0]
    halves = [rows[:HALF], rows[HALF:]]

    ahead, back = list(halves), list(halves[::-1])
    flight = [(send(ahead[k], AHEAD), send(back[k], BACK)) for k in range(2)]
    got, ahead, back, adapter_home_slot, adapter_per_block = lax.optimization_barrier(
        (flight[0], ahead, back, adapter_home_slot, adapter_per_block)
    )
    ahead.append(got[0])
    back.append(got[1])
    flight.append((send(ahead[2], AHEAD), send(back[2], BACK)))

    store_slots = find_slots(adapter_home_slot, adapter_per_block)
    owner = store_slots // held
    inside = store_slots % held
    picked = jnp.max(jnp.where(owner == myself, inside, 0), axis=1)
    owner_row = lax.dynamic_index_in_dim(owner, store, 0, keepdims=False).astype(jnp.int32)
    pick_own = lax.dynamic_index_in_dim(picked, store, 0, keepdims=False)
    pick_lent = lax.dynamic_index_in_dim(picked, 1 - store, 0, keepdims=False)

    down_own = lax.dynamic_index_in_dim(adapter_down_maps, pick_own, 0, keepdims=False)
    down_lent = lax.dynamic_index_in_dim(adapter_down_maps, pick_lent, 0, keepdims=False)
    down_swapped = swap(down_lent, "store")
    weights = pin_call(query_weight, down_own, down_swapped)
    choice = jnp.stack([pick_own, pick_lent, group.astype(pick_own.dtype)]).astype(jnp.int32)
    up_sent = pack_call(choice, adapter_up_maps)
    up_sent = jnp.stack([up_sent[0], swap(up_sent[1], "store")], axis=1)
    up_sent = [up_sent[:, :, : rank // 2], up_sent[:, :, rank // 2 :]]

    position = jnp.where(y == 0, z, 7 - z)
    places = []
    for k in range(8):
        step = (k + 1) // 2
        places += [position - step, position + step] if k % 2 else [position + step, position - step]
    places = jnp.stack(places) % 8
    blocks = jnp.where(places < 4, 2 * places, 15 - 2 * places).astype(jnp.int32)
    hit = blocks[:, None] == jnp.arange(8, dtype=jnp.int32)[None, :]
    owners = jnp.sum(jnp.where(hit, owner_row[None, :], 0), axis=1)
    table = jnp.stack([owners == myself, owners == me * 2 + 1 - store]).astype(jnp.int32)

    bases = []
    shrunk = jnp.zeros((BLOCK, 2 * rank), jnp.bfloat16)
    groups = [[rows], [ahead[2], back[2]]]
    for k in range(1, 7):
        (got_ahead, got_back), ahead, back, bases, shrunk, up_sent = lax.optimization_barrier(
            (flight[k], ahead, back, bases, shrunk, up_sent)
        )
        ahead.append(got_ahead)
        back.append(got_back)
        if k < 5:
            flight.append((send(ahead[k + 2], AHEAD), send(back[k + 2], BACK)))
        if k in (4, 5):
            sent = up_sent[k - 4]
            got = lax.all_to_all(sent, "tensor", split_axis=0, concat_axis=0, tiled=True)
            up_sent = [got, up_sent[1]] if k == 4 else [up_sent[0], got]
        groups.append([got_ahead, got_back] if k % 2 == 0 else [got_back, got_ahead])
        for g in range(len(bases), min(len(bases) + 2, k + 2, 7)):
            base, shrunk = rows_call(g, table, weights, groups[g], shrunk)
            bases.append(base)
    base, shrunk = rows_call(7, table, weights, groups[7], shrunk)
    bases.append(base)

    across = send(shrunk, ACROSS)
    pair = jnp.stack([shrunk, across])
    everyone = [pair] + [send(pair, pairs) for pairs in ALONG]
    home, core = owner_row // 2, owner_row % 2
    chosen = (2 * home + jnp.where(core == store, 0, 1)).astype(jnp.int32)

    def take(got):
        return take_call(chosen, got.reshape(16, rank // 2, -1))

    mine = [take(up_sent[0])]
    other = [swap(mine[0], "groups")]
    got, _ = lax.optimization_barrier((up_sent[1], across))
    mine.append(take(got))
    other.append(swap(mine[1], "groups"))
    home, core = owners // 2, owners % 2
    where = 2 * ((home // 2) ^ z) + ((home % 2) ^ y)
    table = jnp.stack([blocks, where, core != store, jnp.broadcast_to(group, (16,))])
    ups = mine + other
    return finish_call(table.astype(jnp.int32), collect_call(bases), everyone, ups)[None]


def body(tokens, *rest):
    sizes = tuple(lax.axis_size(name) for name in ("groups", "tensor", "store"))
    fits = sizes == (2, 8, 2) and tokens.shape[1] == BLOCK
    return (chain_body if fits else general_body)(tokens, *rest)


def solution(mesh):
    placed = (
        P(("groups", "store"), "tensor", None),
        P(None, "tensor"),
        P(("tensor", "store"), None, None),
        P(("tensor", "store"), None, None),
        P(),
        P(),
    )
    return jax.shard_map(
        body,
        mesh=mesh,
        in_specs=placed,
        out_specs=P(("groups", "store"), None, "tensor"),
        check_vma=False,
    )
```

```python
import functools

import jax
import jax.numpy as jnp
from jax import lax
from jax.experimental import pallas as pl
from jax.experimental.pallas import tpu as pltpu
from jax.sharding import PartitionSpec as P

BLOCK = 128


def find_slots(adapter_home_slot, adapter_per_block):
    catalog = jnp.arange(adapter_home_slot.shape[0], dtype=jnp.int32)
    return jnp.sum(
        jnp.where(
            adapter_per_block[:, :, None] == catalog[None, None, :],
            adapter_home_slot[None, None, :],
            0,
        ),
        axis=2,
    )


def general_body(
    tokens, query_weight, adapter_down_maps, adapter_up_maps, adapter_home_slot, adapter_per_block
):
    shard_count = lax.axis_size("tensor")
    store_count = lax.axis_size("store")
    devices_all = shard_count * store_count
    my_tensor = lax.axis_index("tensor")
    my_store = lax.axis_index("store")
    myself = lax.axis_index(("tensor", "store"))
    held_adapters, rank_index, feature_width = adapter_down_maps.shape
    feature_index = query_weight.shape[1]
    own_rows = tokens[0]
    group_rows = own_rows.shape[0] * shard_count
    blocks = group_rows // BLOCK
    store_slots = find_slots(adapter_home_slot, adapter_per_block)
    owner = store_slots // held_adapters
    inside = store_slots % held_adapters
    picked = jnp.max(jnp.where(owner == myself, inside, -1), axis=1)
    select = (picked[:, None] == jnp.arange(held_adapters, dtype=jnp.int32)[None, :]).astype(
        jnp.bfloat16
    )
    down_map_parts = adapter_down_maps.reshape(
        held_adapters, rank_index, shard_count, feature_index
    )
    up_map_parts = adapter_up_maps.reshape(held_adapters, rank_index, shard_count, feature_index)
    send_down = jnp.einsum(
        "sl,lrtf->tsrf", select, down_map_parts, preferred_element_type=jnp.float32
    ).astype(jnp.bfloat16)
    send_up = jnp.einsum(
        "sl,lrtf->tsrf", select, up_map_parts, preferred_element_type=jnp.float32
    ).astype(jnp.bfloat16)
    recv_down, recv_up = (
        lax.all_to_all(
            sent.reshape(devices_all, rank_index, feature_index),
            ("tensor", "store"),
            split_axis=0,
            concat_axis=0,
            tiled=True,
        )
        for sent in (send_down, send_up)
    )
    owner_row = lax.dynamic_index_in_dim(owner, my_store, 0, keepdims=False)
    source_pick = (owner_row[:, None] == jnp.arange(devices_all, dtype=jnp.int32)[None, :]).astype(
        jnp.bfloat16
    )
    block_down = jnp.einsum(
        "bj,jrf->brf", source_pick, recv_down, preferred_element_type=jnp.float32
    ).astype(jnp.bfloat16)
    block_up = jnp.einsum(
        "bj,jrf->brf", source_pick, recv_up, preferred_element_type=jnp.float32
    ).astype(jnp.bfloat16)
    piece = lax.all_gather(own_rows, "tensor", axis=0, tiled=True)
    product = jnp.dot(piece, query_weight, preferred_element_type=jnp.float32)
    features = lax.dynamic_slice_in_dim(piece, my_tensor * feature_index, feature_index, 1)
    partial_value = jnp.einsum(
        "bnf,brf->bnr",
        features.reshape(blocks, BLOCK, feature_index),
        block_down,
        preferred_element_type=jnp.float32,
    )
    shrunk = lax.psum(partial_value, "tensor").astype(jnp.bfloat16)
    grown = jnp.einsum(
        "bnr,brf->bnf", shrunk, block_up, preferred_element_type=jnp.float32
    ).reshape(group_rows, feature_index)
    query = (product + 0.5 * grown).astype(jnp.bfloat16)
    return query[None]


def both_ways(pairs):
    return pairs + [(b, a) for a, b in pairs]


RING = [0, 2, 4, 6, 7, 5, 3, 1]
AHEAD = [(RING[i], RING[(i + 1) % 8]) for i in range(8)]
BACK = [(b, a) for a, b in AHEAD]
ACROSS = [(i, i ^ 1) for i in range(8)]
ALONG = [[(i, i ^ (2 * d)) for i in range(8)] for d in (1, 2, 3)]
HALF = BLOCK // 2
DEPTH = 1024
VMEM_LIMIT = 16 * 1024 * 1024


def send(value, pairs):
    return lax.ppermute(value, "tensor", pairs)


def swap(value, axis):
    return lax.ppermute(value, axis, [(0, 1), (1, 0)])


def settings(flops=1):
    return dict(
        compiler_params=pltpu.CompilerParams(vmem_limit_bytes=VMEM_LIMIT),
        cost_estimate=pl.CostEstimate(flops=flops, bytes_accessed=1, transcendentals=0),
    )


def in_vmem(count):
    return [pl.BlockSpec(memory_space=pltpu.VMEM)] * count


def split_kernel(rows, first, second, sems):
    copies = [
        pltpu.make_async_copy(rows.at[pl.ds(i * HALF, HALF)], half, sems.at[i])
        for i, half in enumerate((first, second))
    ]
    for copy in copies:
        copy.start()
    for copy in copies:
        copy.wait()


def split_call(rows):
    half = pltpu.VMEM((HALF, rows.shape[1]), rows.dtype)
    return pl.pallas_call(
        split_kernel,
        in_specs=[pl.BlockSpec(memory_space=pl.ANY)],
        out_specs=in_vmem(2),
        out_shape=[half, half],
        scratch_shapes=[pltpu.SemaphoreType.DMA((2,))],
        name="split",
        **settings(),
    )(pltpu.with_memory_space_constraint(rows, pltpu.HBM))


def pin_kernel(weight, own, swapped, out, sem):
    columns = weight.shape[1]
    copy = pltpu.make_async_copy(weight, out.at[:, pl.ds(0, columns)], sem)
    copy.start()
    for at in range(0, weight.shape[0], DEPTH):
        cut = pl.ds(at, DEPTH)
        out[cut, columns:] = jnp.concatenate([own[:, cut], swapped[:, cut]], axis=0).T
    copy.wait()


def pin_call(weight, own, swapped):
    width, columns = weight.shape
    return pl.pallas_call(
        pin_kernel,
        in_specs=[pl.BlockSpec(memory_space=pl.ANY)] + in_vmem(2),
        out_specs=in_vmem(1)[0],
        out_shape=pltpu.VMEM((width, columns + 2 * own.shape[0]), weight.dtype),
        scratch_shapes=[pltpu.SemaphoreType.DMA],
        name="pin",
        **settings(),
    )(weight, own, swapped)


def rows_kernel(group, table, weights, *refs):
    *pieces, shrunk, base, shrunk_out = refs
    columns = base.shape[1]
    total = None
    for at in range(0, weights.shape[0], DEPTH):
        cut = pl.ds(at, DEPTH)
        x = [p[:, cut] for p in pieces]
        x = x[0] if len(x) == 1 else jnp.concatenate(x, axis=0)
        part = jnp.dot(x, weights[cut, :], preferred_element_type=jnp.float32)
        total = part if total is None else total + part
    base[...] = total[:, :columns]
    lane = lax.broadcasted_iota(jnp.int32, shrunk.shape, 1)
    row = lax.broadcasted_iota(jnp.int32, shrunk.shape, 0)
    use = jnp.where(
        row < HALF,
        jnp.where(lane < 64, table[0, 2 * group], table[1, 2 * group]),
        jnp.where(lane < 64, table[0, 2 * group + 1], table[1, 2 * group + 1]),
    )
    small = total[:, columns:].astype(jnp.bfloat16).astype(jnp.float32)
    old = shrunk[...].astype(jnp.float32)
    shrunk_out[...] = jnp.where(use > 0, small, old).astype(jnp.bfloat16)


def rows_call(group, table, weights, pieces, shrunk):
    columns = weights.shape[1] - 128
    operands = [pltpu.with_memory_space_constraint(weights, pltpu.VMEM)] + pieces + [shrunk]
    return pl.pallas_call(
        functools.partial(rows_kernel, group),
        in_specs=[pl.BlockSpec(memory_space=pltpu.SMEM)] + in_vmem(len(operands)),
        out_specs=in_vmem(2),
        out_shape=[
            jax.ShapeDtypeStruct((BLOCK, columns), jnp.float32),
            jax.ShapeDtypeStruct((BLOCK, 128), jnp.bfloat16),
        ],
        name="rows",
        **settings(flops=10**11 if group == 7 else 1),
    )(table, *operands)


def pack_kernel(table, up, out):
    part = out.shape[3]
    for t in range(8):
        at = pl.multiple_of((2 * t + table[2]) * part, part)
        out[0, t] = up[0, :, pl.ds(at, part)]


def pack_call(table, up_maps):
    _, rank, width = up_maps.shape
    part = width // 16
    return pl.pallas_call(
        pack_kernel,
        grid_spec=pltpu.PrefetchScalarGridSpec(
            num_scalar_prefetch=1,
            grid=(2,),
            in_specs=[pl.BlockSpec((1, rank, width), lambda s, t: (t[s], 0, 0))],
            out_specs=pl.BlockSpec((1, 8, rank, part), lambda s, t: (s, 0, 0, 0)),
        ),
        out_shape=jax.ShapeDtypeStruct((2, 8, rank, part), jnp.bfloat16),
        name="pack",
        **settings(),
    )(table, pltpu.with_memory_space_constraint(up_maps, pltpu.HBM))


def take_kernel(table, got, out):
    out[...] = got[...]


def take_call(table, got):
    _, rank, part = got.shape
    return pl.pallas_call(
        take_kernel,
        grid_spec=pltpu.PrefetchScalarGridSpec(
            num_scalar_prefetch=1,
            grid=(8,),
            in_specs=[pl.BlockSpec((1, rank, part), lambda b, t: (t[b], 0, 0))],
            out_specs=pl.BlockSpec((1, rank, part), lambda b, t: (b, 0, 0)),
        ),
        out_shape=jax.ShapeDtypeStruct((8, rank, part), jnp.bfloat16),
        name="take",
        **settings(),
    )(table, got)


def collect_kernel(*refs):
    *bases, out, sems = refs
    copies = [pltpu.make_async_copy(bases[g], out.at[g], sems.at[g]) for g in range(8)]
    for copy in copies:
        copy.start()
    for copy in copies:
        copy.wait()


def collect_call(bases):
    return pl.pallas_call(
        collect_kernel,
        in_specs=[pl.BlockSpec(memory_space=pl.ANY)] * 8,
        out_specs=in_vmem(1)[0],
        out_shape=pltpu.VMEM((8,) + bases[0].shape, jnp.float32),
        scratch_shapes=[pltpu.SemaphoreType.DMA((8,))],
        name="collect",
        **settings(),
    )(*[pltpu.with_memory_space_constraint(base, pltpu.HBM) for base in bases])


def finish_kernel(table, base, *refs):
    gathered, (mine, other, out, shrunk, rows, sems) = refs[:4], refs[4:]
    part = mine.shape[2]
    group = table[3, 0]
    for i, pair in enumerate(gathered):
        shrunk[pl.ds(2 * i, 2)] = pair[...]
    copies = []
    for i in range(16):
        block, half = table[0, i], i % 2
        own = pl.ds(half * HALF, HALF)
        both = shrunk[table[1, i], own, :].astype(jnp.float32)
        value = jnp.where(table[2, i] > 0, both[:, 64:], both[:, :64]).astype(jnp.bfloat16)
        for up, side in ((mine, group), (other, 1 - group)):
            cut = pl.ds(pl.multiple_of(side * part, part), part)
            grown = jnp.dot(value, up[block], preferred_element_type=jnp.float32)
            rows[i, :, cut] = (base[i // 2, own, cut] + 0.5 * grown).astype(rows.dtype)
        to = pl.ds(pl.multiple_of((2 * block + half) * HALF, HALF), HALF)
        copies.append(pltpu.make_async_copy(rows.at[i], out.at[to], sems.at[i]))
        copies[-1].start()
    for copy in copies:
        copy.wait()


def finish_call(table, base, gathered, ups):
    columns = base.shape[2]
    return pl.pallas_call(
        finish_kernel,
        in_specs=[pl.BlockSpec(memory_space=pltpu.SMEM)] + in_vmem(7),
        out_specs=pl.BlockSpec(memory_space=pltpu.HBM),
        out_shape=jax.ShapeDtypeStruct((8 * BLOCK, columns), jnp.bfloat16),
        scratch_shapes=[
            pltpu.VMEM((8,) + gathered[0].shape[1:], jnp.bfloat16),
            pltpu.VMEM((16, HALF, columns), jnp.bfloat16),
            pltpu.SemaphoreType.DMA((16,)),
        ],
        name="finish",
        **settings(),
    )(table, pltpu.with_memory_space_constraint(base, pltpu.VMEM), *gathered, *ups)


def chain_body(
    tokens, query_weight, adapter_down_maps, adapter_up_maps, adapter_home_slot, adapter_per_block
):
    me = lax.axis_index("tensor")
    z, y = me // 2, me % 2
    store = lax.axis_index("store")
    group = lax.axis_index("groups")
    myself = me * 2 + store
    held, rank, width = adapter_down_maps.shape
    rows = tokens[0]
    halves = list(split_call(rows))

    ahead, back = list(halves), list(halves[::-1])
    flight = [(send(ahead[k], AHEAD), send(back[k], BACK)) for k in range(2)]
    got, ahead, back, adapter_home_slot, adapter_per_block = lax.optimization_barrier(
        (flight[0], ahead, back, adapter_home_slot, adapter_per_block)
    )
    ahead.append(got[0])
    back.append(got[1])
    flight.append((send(ahead[2], AHEAD), send(back[2], BACK)))

    store_slots = find_slots(adapter_home_slot, adapter_per_block)
    owner = store_slots // held
    inside = store_slots % held
    picked = jnp.max(jnp.where(owner == myself, inside, 0), axis=1)
    owner_row = lax.dynamic_index_in_dim(owner, store, 0, keepdims=False).astype(jnp.int32)
    pick_own = lax.dynamic_index_in_dim(picked, store, 0, keepdims=False)
    pick_lent = lax.dynamic_index_in_dim(picked, 1 - store, 0, keepdims=False)

    down_own = lax.dynamic_index_in_dim(adapter_down_maps, pick_own, 0, keepdims=False)
    down_lent = lax.dynamic_index_in_dim(adapter_down_maps, pick_lent, 0, keepdims=False)
    down_swapped = swap(down_lent, "store")
    weights = pin_call(query_weight, down_own, down_swapped)
    choice = jnp.stack([pick_own, pick_lent, group.astype(pick_own.dtype)]).astype(jnp.int32)
    up_sent = pack_call(choice, adapter_up_maps)
    up_sent = jnp.stack([up_sent[0], swap(up_sent[1], "store")], axis=1)

    position = jnp.where(y == 0, z, 7 - z)
    places = []
    for k in range(8):
        step = (k + 1) // 2
        places += [position - step, position + step] if k % 2 else [position + step, position - step]
    places = jnp.stack(places) % 8
    blocks = jnp.where(places < 4, 2 * places, 15 - 2 * places).astype(jnp.int32)
    hit = blocks[:, None] == jnp.arange(8, dtype=jnp.int32)[None, :]
    owners = jnp.sum(jnp.where(hit, owner_row[None, :], 0), axis=1)
    table = jnp.stack([owners == myself, owners == me * 2 + 1 - store]).astype(jnp.int32)

    bases = []
    shrunk = jnp.zeros((BLOCK, 2 * rank), jnp.bfloat16)
    groups = [[rows], [ahead[2], back[2]]]
    for k in range(1, 7):
        (got_ahead, got_back), ahead, back, bases, shrunk, up_sent = lax.optimization_barrier(
            (flight[k], ahead, back, bases, shrunk, up_sent)
        )
        ahead.append(got_ahead)
        back.append(got_back)
        if k < 5:
            flight.append((send(ahead[k + 2], AHEAD), send(back[k + 2], BACK)))
        if k == 5:
            up_got = lax.all_to_all(up_sent, "tensor", split_axis=0, concat_axis=0, tiled=True)
        groups.append([got_ahead, got_back] if k % 2 == 0 else [got_back, got_ahead])
        for g in range(len(bases), min(len(bases) + 2, k + 2, 7)):
            base, shrunk = rows_call(g, table, weights, groups[g], shrunk)
            bases.append(base)
    base, shrunk = rows_call(7, table, weights, groups[7], shrunk)
    bases.append(base)

    across = send(shrunk, ACROSS)
    pair = jnp.stack([shrunk, across])
    everyone = [pair] + [send(pair, pairs) for pairs in ALONG]
    up_got, _ = lax.optimization_barrier((up_got, across))
    home, core = owner_row // 2, owner_row % 2
    chosen = 2 * home + jnp.where(core == store, 0, 1)
    up_mine = take_call(chosen.astype(jnp.int32), up_got.reshape(16, rank, -1))
    up_other = swap(up_mine, "groups")
    home, core = owners // 2, owners % 2
    where = 2 * ((home // 2) ^ z) + ((home % 2) ^ y)
    table = jnp.stack([blocks, where, core != store, jnp.broadcast_to(group, (16,))])
    ups = [up_mine, up_other]
    return finish_call(table.astype(jnp.int32), collect_call(bases), everyone, ups)[None]


def body(tokens, *rest):
    sizes = tuple(lax.axis_size(name) for name in ("groups", "tensor", "store"))
    fits = sizes == (2, 8, 2) and tokens.shape[1] == BLOCK
    return (chain_body if fits else general_body)(tokens, *rest)


def solution(mesh):
    placed = (
        P(("groups", "store"), "tensor", None),
        P(None, "tensor"),
        P(("tensor", "store"), None, None),
        P(("tensor", "store"), None, None),
        P(),
        P(),
    )
    return jax.shard_map(
        body,
        mesh=mesh,
        in_specs=placed,
        out_specs=P(("groups", "store"), None, "tensor"),
        check_vma=False,
    )
```
